32 devices in a mesh: groups: 2 (over y), ctx: 4 (over z), head: 4 (over x, core).
Axes of the slice: x: 2, y: 2, z: 4, core: 2. Of those that a mesh axis runs over, the one named last changes fastest.
Arguments:
- queries: bfloat16 [1024, 12288], P(('groups', 'ctx'), 'head'), parts along dimension 0, may hold values from -12 to 12
- kv_rows: bfloat16 [2048, 576], P(('groups', 'ctx')), parts along dimension 0, may hold values from -4.5 to 4.5
- w_kv_up: bfloat16 [512, 16384], P(None, 'head'), may hold values from -0.25 to 0.25
- w_out: bfloat16 [8192, 7168], P('head', 'ctx'), may hold values from -1 to 1
- stretch_order: int32 [8], P('groups'), parts along dimension 0, may hold values from 0 to 3, each once
- prefix_len: int32 [2], P('groups'), parts along dimension 0, may hold values from 128 to 512
Outputs:
- mixed: bfloat16 [1024, 7168], P(('groups', 'ctx', 'head')), parts along dimension 0
The draws below stay inside these ranges and needn't reach their ends.
There are 2 independent parts, one for each index of `groups`. The reference program is written for one: setup_inputs(seed, part) draws one part's arguments, and reference() takes and returns one part's arrays. A program takes and returns all parts, laid end to end along the dimension named above; an argument that names none is the same for every part. Nothing has to cross between parts.
All inputs are finite; a program needn't handle non-finite values.
Results may differ from the reference program's by a relative error of at most 0.012.
Values may be sent and summed in bfloat16 or wider, within the bound.
No kernel may reach another device: no remote copies, remote signals or barrier semaphores. Data moves between devices by JAX's collectives and lax.ppermute only.
A program may use at most 128 MiB of HBM per device.

```python
import math
import jax
import jax.numpy as jnp
from jax import lax

D = 7168
LAT = 512
NOPE = 128
ROPE = 64
VD = 128
HEADS = 64
Q_DEV = 128
CACHE_DEV = 128
ROWS_DEV = 256
STRETCH = 512
CACHE = 512
KEYS = 1024
N_CTX = 4


def draw_queries(key, part):
    key = jax.random.fold_in(key, 12)
    first_key = jax.random.fold_in(key, 0)
    full = jnp.clip(jax.random.normal(first_key, (STRETCH, HEADS, NOPE + ROPE), jnp.float32), -4.5, 4.5)
    return full.reshape(STRETCH, HEADS * (NOPE + ROPE)).astype(jnp.bfloat16)


def draw_kv_rows(key, part):
    key = jax.random.fold_in(key, 11)
    full = jnp.clip(jax.random.normal(key, (KEYS, LAT + ROPE), jnp.float32), -4.5, 4.5)
    return full.astype(jnp.bfloat16)


def shard_levels(own_key, dims, cuts, least, high):
    gain, own = 1.0, jax.random.fold_in(own_key, 6)
    for position, shards_of in cuts:
        draws = jnp.exp(jax.random.uniform(jax.random.fold_in(own, position), (shards_of,), jnp.float32, least / len(cuts), high / len(cuts)))
        gain = gain * jnp.repeat(draws, dims[position] // shards_of).reshape([-1 if axis == position else 1 for axis in range(len(dims))])
    return gain


def normal_values(stream_key, extent, width, limit, cuts=(), kind=jnp.bfloat16):
    factor_of = shard_levels(stream_key, extent, cuts, -0.22, 0.18) if cuts else 1.0
    entries = jax.random.normal(stream_key, extent, jnp.float32) * width * factor_of
    return jnp.minimum(jnp.maximum(entries, -limit), limit).astype(kind)


def setup_inputs(seed: int = 0, part: int = 0) -> dict:
    arg_keys = jax.random.split(jax.random.key(seed), 7)
    part_keys = jax.random.split(jax.random.fold_in(arg_keys[6], part), 7)
    return {
        "queries": draw_queries(jax.random.fold_in(jax.random.fold_in(arg_keys[6], part), 71), part),
        "kv_rows": draw_kv_rows(jax.random.fold_in(jax.random.fold_in(arg_keys[6], part), 71), part),
        "w_kv_up": normal_values(arg_keys[2], (LAT, HEADS * (NOPE + VD)), LAT ** -0.5, 0.25, ((1, 4),)),
        "w_out": normal_values(arg_keys[3], (HEADS * VD, D), (max(HEADS * VD // 256, 1)) ** -0.5, 1.0, ((0, 4), (1, 4))),
        "stretch_order": jax.random.permutation(part_keys[4], N_CTX).astype(jnp.int32),
        "prefix_len": jax.random.randint(part_keys[5], (1,), CACHE // 4, CACHE + 1).astype(jnp.int32),
    }


def reference(queries, kv_rows, w_kv_up, w_out, stretch_order, prefix_len):
    row_ids = jnp.arange(KEYS, dtype=jnp.int32)
    shard_ids = row_ids // ROWS_DEV
    within = row_ids % ROWS_DEV
    is_cache = within < CACHE_DEV
    slot_ids = shard_ids * CACHE_DEV + within
    key_pos = stretch_order[shard_ids].astype(jnp.int32) * Q_DEV + within - CACHE_DEV
    q_index = jnp.arange(STRETCH, dtype=jnp.int32)
    query_pos = stretch_order[q_index // Q_DEV].astype(jnp.int32) * Q_DEV + q_index % Q_DEV
    visible = jnp.where(is_cache[None, :], (slot_ids < prefix_len[0])[None, :], key_pos[None, :] <= query_pos[:, None])
    latent = kv_rows[:, :LAT]
    rope_keys = kv_rows[:, LAT:]
    score_scale = 1.0 / math.sqrt(NOPE + ROPE)
    query_heads = queries.reshape(STRETCH, HEADS, NOPE + ROPE).transpose(1, 0, 2)
    weight_heads = w_kv_up.reshape(LAT, HEADS, NOPE + VD).transpose(1, 0, 2)

    def head_attention(head_pair):
        head_query, head_weight = head_pair
        projected = jnp.dot(latent, head_weight, preferred_element_type=jnp.float32).astype(jnp.bfloat16)
        keys_full = jnp.concatenate([projected[:, :NOPE], rope_keys], axis=1)
        values = projected[:, NOPE:]
        scores = jnp.dot(head_query, keys_full.T, preferred_element_type=jnp.float32) * score_scale
        scores = jnp.where(visible, scores, -jnp.inf)
        row_max = lax.optimization_barrier(jnp.max(scores, axis=1, keepdims=True))
        weights = jnp.exp(scores - row_max)
        denominator = lax.optimization_barrier(jnp.sum(weights, axis=1, keepdims=True))
        result = jnp.dot(weights.astype(jnp.bfloat16), values, preferred_element_type=jnp.float32) / denominator
        return result.astype(jnp.bfloat16)
    attended = lax.map(head_attention, (query_heads, weight_heads))
    flattened = attended.transpose(1, 0, 2).reshape(STRETCH, HEADS * VD)
    return jnp.dot(flattened, w_out, preferred_element_type=jnp.float32).astype(jnp.bfloat16)
```

```python
import functools
import math

import jax
import jax.numpy as jnp
from jax import lax
from jax.experimental import pallas as pl
from jax.experimental.pallas import tpu as pltpu
from jax.sharding import PartitionSpec as P

LAT = 512
NOPE = 128
ROPE = 64
VD = 128
CHUNKS = 2
HEAD_BLOCK = 8
MASKED = -1e30
LOG2E = 1.4426950408889634


def lookup(table, indices):
    positions = jnp.arange(table.shape[0], dtype=jnp.int32)
    return jnp.sum(jnp.where(indices[..., None] == positions, table, 0), axis=-1)


def shift(array, axis, size, by):
    return lax.ppermute(array, axis, [(i, (i + by) % size) for i in range(size)])


def swap_cores(array, size):
    return lax.ppermute(array, "head", [(i, i ^ 1) for i in range(size)])


def attention_kernel(heads, rows, q_ref, keys_ref, bias_ref, weight_ref, out_ref):
    for head in range(heads):
        scores = jnp.dot(q_ref[head], keys_ref[...], preferred_element_type=jnp.float32)
        scores = scores + bias_ref[...]
        top = jnp.max(scores, axis=1, keepdims=True)
        weights = jnp.exp2(scores - top)
        total = jnp.sum(weights, axis=1, keepdims=True)
        mixed = lax.dot_general(
            weights.astype(jnp.bfloat16),
            keys_ref[:LAT, :],
            (((1,), (1,)), ((), ())),
            preferred_element_type=jnp.float32,
        )
        mixed = (mixed / total).astype(jnp.bfloat16)
        w_value = weight_ref[:, head * (NOPE + VD) + NOPE : (head + 1) * (NOPE + VD)]
        result = jnp.dot(mixed, w_value, preferred_element_type=jnp.float32)
        out_ref[:, head * VD : (head + 1) * VD] = result.astype(jnp.bfloat16)


def attention(q_ext, keys, bias, w_kv_up):
    head_count, rows, depth = q_ext.shape
    amount = keys.shape[1]
    block = math.gcd(HEAD_BLOCK, head_count)
    macs = head_count * rows * (amount * (depth + LAT) + LAT * VD)
    return pl.pallas_call(
        functools.partial(attention_kernel, block, rows),
        grid=(head_count // block,),
        out_shape=jax.ShapeDtypeStruct((rows, head_count * VD), jnp.bfloat16),
        in_specs=[
            pl.BlockSpec((block, rows, depth), lambda i: (i, 0, 0)),
            pl.BlockSpec((depth, amount), lambda i: (0, 0)),
            pl.BlockSpec((rows, amount), lambda i: (0, 0)),
            pl.BlockSpec((LAT, block * (NOPE + VD)), lambda i: (0, i)),
        ],
        out_specs=pl.BlockSpec((rows, block * VD), lambda i: (0, i)),
        compiler_params=pltpu.CompilerParams(vmem_limit_bytes=40 * 1024 * 1024),
        cost_estimate=pl.CostEstimate(
            flops=2 * macs,
            bytes_accessed=2 * (q_ext.size + keys.size) + 4 * bias.size + 2 * w_kv_up.size,
            transcendentals=head_count * rows * amount,
        ),
    )(q_ext, keys, bias, w_kv_up)


def shards(n_ctx, n_head, queries, kv_rows, w_kv_up, w_out, stretch_order, prefix_len):
    query_rows = queries.shape[0]
    row_span = kv_rows.shape[0]
    cache_rows = row_span - query_rows
    half = row_span // 2
    head_count = w_kv_up.shape[1] // (NOPE + VD)
    columns = w_out.shape[1]
    n_x = n_head // 2
    owned = query_rows // n_head
    piece = owned // CHUNKS
    ctx = lax.axis_index("ctx")
    head = lax.axis_index("head")
    core = head % 2
    x = head // 2

    with jax.named_scope("keys_over_ctx"):
        kv_t = kv_rows.T
        own_half = lax.dynamic_slice(kv_t, (0, core * half), (LAT + ROPE, half))
        halves = [own_half] + [shift(own_half, "ctx", n_ctx, d) for d in range(1, n_ctx)]
        others = [swap_cores(array, n_head) for array in halves[1:]]
        other_half = lax.dynamic_slice(kv_t, (0, (1 - core) * half), (LAT + ROPE, half))
        keys = jnp.concatenate(halves + [other_half] + others, axis=1)

    with jax.named_scope("visible"):
        scale = LOG2E / math.sqrt(NOPE + ROPE)
        query_ids = jnp.arange(query_rows, dtype=jnp.int32)
        query_pos = lookup(stretch_order, ctx) * query_rows + query_ids
        sources = (ctx - jnp.arange(n_ctx, dtype=jnp.int32)) % n_ctx
        offsets = jnp.arange(half, dtype=jnp.int32)
        within = jnp.stack([core * half + offsets, (1 - core) * half + offsets])
        within = jnp.broadcast_to(within[:, None, :], (2, n_ctx, half))
        sources = jnp.broadcast_to(sources[None, :, None], (2, n_ctx, half))
        is_cache = within < cache_rows
        slot_ids = sources * cache_rows + within
        key_pos = lookup(stretch_order, sources) * query_rows + within - cache_rows
        cache_pos = jnp.where(slot_ids < prefix_len[0], -1, n_ctx * query_rows)
        first_seen = jnp.where(is_cache, cache_pos, key_pos).reshape(-1)
        query_pos = query_pos.reshape(n_head, CHUNKS, piece).transpose(1, 0, 2)
        query_pos = query_pos.reshape(CHUNKS, query_rows // CHUNKS)
        bias = jnp.where(first_seen[None, None, :] <= query_pos[:, :, None], 0.0, MASKED)
        bias = bias.astype(jnp.float32)

    with jax.named_scope("queries_to_latent"):
        query_heads = queries.reshape(n_head, CHUNKS, piece, head_count, NOPE + ROPE)
        query_heads = query_heads.transpose(1, 3, 0, 2, 4)
        query_heads = query_heads.reshape(CHUNKS, head_count, query_rows // CHUNKS, NOPE + ROPE)
        w_keys = w_kv_up.reshape(LAT, head_count, NOPE + VD)[:, :, :NOPE]
        absorbed = jnp.einsum(
            "chqd,lhd->chql", query_heads[..., :NOPE], w_keys, preferred_element_type=jnp.float32
        )
        rope = query_heads[..., NOPE:].astype(jnp.float32)
        q_ext = (jnp.concatenate([absorbed, rope], axis=3) * scale).astype(jnp.bfloat16)

    results = []
    for chunk in range(CHUNKS):
        with jax.named_scope("attention"):
            attended = attention(q_ext[chunk], keys, bias[chunk], w_kv_up)
        with jax.named_scope("attended_over_ctx"):
            gathered = [attended] + [shift(attended, "ctx", n_ctx, d) for d in range(1, n_ctx)]
            gathered = jnp.concatenate(gathered, axis=0)
        with jax.named_scope("out_product"):
            partial = jnp.dot(gathered, w_out, preferred_element_type=jnp.float32)
            partial = partial.reshape(n_ctx, n_x, 2, piece, columns)
        with jax.named_scope("sum_over_cores"):
            sent = lax.dynamic_index_in_dim(partial, 1 - core, 2, keepdims=False)
            kept = lax.dynamic_index_in_dim(partial, core, 2, keepdims=False)
            summed = kept + swap_cores(sent.astype(jnp.bfloat16), n_head).astype(jnp.float32)
        with jax.named_scope("sum_over_x"):
            total = lax.dynamic_index_in_dim(summed, x, 1, keepdims=False)
            for d in range(1, n_x):
                sent = lax.dynamic_index_in_dim(summed, (x + d) % n_x, 1, keepdims=False)
                sent = shift(sent.astype(jnp.bfloat16), "head", n_head, 2 * d)
                total = total + sent.astype(jnp.float32)
        with jax.named_scope("columns_over_ctx"):
            total = total.astype(jnp.bfloat16)
            blocks = [total[0]] + [shift(total[d], "ctx", n_ctx, -d) for d in range(1, n_ctx)]
        results.append(blocks)
    with jax.named_scope("output"):
        stacked = [jnp.concatenate([r[d] for r in results], axis=0) for d in range(n_ctx)]
        doubled = jnp.concatenate(stacked + stacked, axis=1)
        start = ((n_ctx - ctx) % n_ctx) * columns
        return lax.dynamic_slice(doubled, (0, start), (owned, n_ctx * columns))


def solution(mesh):
    placed = (
        P(("groups", "ctx"), "head"),
        P(("groups", "ctx"), None),
        P(None, "head"),
        P("head", "ctx"),
        P("groups"),
        P("groups"),
    )
    return jax.shard_map(
        functools.partial(shards, mesh.shape["ctx"], mesh.shape["head"]),
        mesh=mesh,
        in_specs=placed,
        out_specs=P(("groups", "ctx", "head"), None),
        check_vma=False,
    )
```

```python
import functools
import math

import jax
import jax.numpy as jnp
from jax import lax
from jax.experimental import pallas as pl
from jax.experimental.pallas import tpu as pltpu
from jax.sharding import PartitionSpec as P

LAT = 512
NOPE = 128
ROPE = 64
VD = 128
HEAD = NOPE + ROPE
PROJ = NOPE + VD
CHUNKS = 2
SUB_ROWS = 256
MASKED = -1e30
VMEM_LIMIT = 20 * 1024 * 1024
LOG2E = 1.4426950408889634
SCALE = LOG2E / math.sqrt(HEAD)
SHORT = pl.CostEstimate(flops=1024, bytes_accessed=1024, transcendentals=0)


def lookup(table, indices):
    positions = jnp.arange(table.shape[0], dtype=jnp.int32)
    return jnp.sum(jnp.where(indices[..., None] == positions, table, 0), axis=-1)


def exchange(array, axis, size, bit):
    return lax.ppermute(array, axis, [(i, i ^ bit) for i in range(size)])


def tie_kernel(*refs):
    pass


def tie(array, after):
    if not after:
        return array
    anywhere = pl.BlockSpec(memory_space=pl.ANY)
    return pl.pallas_call(
        tie_kernel,
        out_shape=jax.ShapeDtypeStruct(array.shape, array.dtype),
        in_specs=[anywhere] * (1 + len(after)),
        out_specs=anywhere,
        input_output_aliases={0: 0},
        cost_estimate=SHORT,
    )(array, *after)


def gather_pieces(own, size, after=()):
    pieces = {0: own}
    bit = size // 2
    while bit:
        for offset in sorted(pieces, reverse=True):
            pieces[offset ^ bit] = exchange(pieces[offset], "ctx", size, bit)
        if bit == size // 2:
            pieces[bit] = tie(pieces[bit], after)
        bit //= 2
    return [pieces[offset] for offset in range(size)]


def absorb_kernel(owners, piece, q_ref, weight_ref, *out_refs):
    rows = q_ref.shape[0]
    chunks = len(out_refs)
    queries = q_ref[...].astype(jnp.float32)
    for head in range(out_refs[0].shape[0]):
        nope = queries[:, head * HEAD : head * HEAD + NOPE].astype(jnp.bfloat16)
        rope = queries[:, head * HEAD + NOPE : (head + 1) * HEAD] * SCALE
        absorbed = lax.dot_general(
            nope,
            weight_ref[:, head * PROJ : head * PROJ + NOPE],
            (((1,), (1,)), ((), ())),
            preferred_element_type=jnp.float32,
        )
        absorbed = (absorbed * SCALE).reshape(owners, chunks, piece, LAT)
        rope = rope.reshape(owners, chunks, piece, ROPE)
        for chunk, out_ref in enumerate(out_refs):
            part = absorbed[:, chunk].reshape(rows // chunks, LAT)
            out_ref[head, :, :LAT] = part.astype(jnp.bfloat16)
            part = rope[:, chunk].reshape(rows // chunks, ROPE)
            out_ref[head, :, LAT:] = part.astype(jnp.bfloat16)


def absorb(queries, w_kv_up, owners, piece):
    rows = queries.shape[0]
    head_count = w_kv_up.shape[1] // PROJ
    pair = 2
    return pl.pallas_call(
        functools.partial(absorb_kernel, owners, piece),
        grid=(head_count // pair,),
        out_shape=[
            jax.ShapeDtypeStruct((head_count, rows // CHUNKS, LAT + ROPE), jnp.bfloat16)
            for chunk in range(CHUNKS)
        ],
        in_specs=[
            pl.BlockSpec((rows, pair * HEAD), lambda i: (0, i)),
            pl.BlockSpec((LAT, pair * PROJ), lambda i: (0, i)),
        ],
        out_specs=[
            pl.BlockSpec((pair, rows // CHUNKS, LAT + ROPE), lambda i: (i, 0, 0))
            for chunk in range(CHUNKS)
        ],
        cost_estimate=SHORT,
    )(queries, w_kv_up)


def attention_kernel(count, q_ref, bias_ref, weight_ref, *refs):
    piece_refs = refs[:count]
    out_ref, keys_ref = refs[count:]

    @pl.when(pl.program_id(0) == 0)
    def _():
        start = 0
        for piece_ref in piece_refs:
            width = piece_ref.shape[1]
            keys_ref[:, start : start + width] = piece_ref[...]
            start += width

    heads, rows, depth = q_ref.shape
    amount = keys_ref.shape[1]
    group = max(1, min(heads, SUB_ROWS // rows))
    for first in range(0, heads, group):
        size = group * rows
        queries = q_ref[first : first + group].reshape(size, depth)
        scores = jnp.dot(queries, keys_ref[...], preferred_element_type=jnp.float32)
        scores = scores.reshape(group, rows, amount) + bias_ref[...][None]
        top = jnp.max(scores, axis=2, keepdims=True)
        weights = jnp.exp2(scores - top)
        total = jnp.sum(weights, axis=2, keepdims=True).reshape(size, 1)
        mixed = lax.dot_general(
            weights.reshape(size, amount).astype(jnp.bfloat16),
            keys_ref[:LAT, :],
            (((1,), (1,)), ((), ())),
            preferred_element_type=jnp.float32,
        )
        mixed = (mixed / total).astype(jnp.bfloat16)
        for head in range(first, first + group):
            result = jnp.dot(
                mixed[(head - first) * rows : (head - first + 1) * rows],
                weight_ref[:, head * PROJ + NOPE : (head + 1) * PROJ],
                preferred_element_type=jnp.float32,
            )
            out_ref[:, head * VD : (head + 1) * VD] = result.astype(jnp.bfloat16)


def attention(q_ext, bias, w_kv_up, key_pieces):
    head_count, rows, depth = q_ext.shape
    amount = sum(piece.shape[1] for piece in key_pieces)
    block = head_count // 2
    macs = head_count * rows * (amount * (depth + LAT) + LAT * VD)
    return pl.pallas_call(
        functools.partial(attention_kernel, len(key_pieces)),
        grid=(head_count // block,),
        out_shape=jax.ShapeDtypeStruct((rows, head_count * VD), jnp.bfloat16),
        in_specs=[
            pl.BlockSpec((block, rows, depth), lambda i: (i, 0, 0)),
            pl.BlockSpec((rows, amount), lambda i: (0, 0)),
            pl.BlockSpec((LAT, block * PROJ), lambda i: (0, i)),
        ]
        + [pl.BlockSpec(piece.shape, lambda i: (0, 0)) for piece in key_pieces],
        out_specs=pl.BlockSpec((rows, block * VD), lambda i: (0, i)),
        scratch_shapes=[pltpu.VMEM((depth, amount), jnp.bfloat16)],
        compiler_params=pltpu.CompilerParams(vmem_limit_bytes=VMEM_LIMIT),
        cost_estimate=SHORT,
    )(q_ext, bias, w_kv_up, *key_pieces)


def product_kernel(count, n_x, core_ref, weight_ref, *refs):
    piece_refs = refs[:count]
    sent_ref, kept_ref, rows_ref = refs[-3:]
    rows = piece_refs[0].shape[0]

    @pl.when(pl.program_id(0) == 0)
    def _():
        for index, piece_ref in enumerate(piece_refs):
            rows_ref[index * rows : (index + 1) * rows, :] = piece_ref[...]

    width = weight_ref.shape[1]
    result = jnp.dot(rows_ref[...], weight_ref[...], preferred_element_type=jnp.float32)
    result = result.reshape(count, n_x, 2, rows // (2 * n_x), width)
    is_first = core_ref[0] == 0
    for x in range(n_x):
        first, second = result[:, x, 0], result[:, x, 1]
        sent_ref[x] = jnp.where(is_first, second, first).astype(jnp.bfloat16)
        kept_ref[x] = jnp.where(is_first, first, second)


def product(pieces, w_out, core, n_x, after):
    rows, depth = pieces[0].shape
    count = len(pieces)
    columns = w_out.shape[1]
    tile = 256 if columns % 256 == 0 else columns
    shape = (n_x, count, rows // (2 * n_x), columns)
    block = pl.BlockSpec(shape[:3] + (tile,), lambda i: (0, 0, 0, i))
    return pl.pallas_call(
        functools.partial(product_kernel, count, n_x),
        grid=(columns // tile,),
        out_shape=[jax.ShapeDtypeStruct(shape, jnp.bfloat16), jax.ShapeDtypeStruct(shape, jnp.float32)],
        in_specs=[
            pl.BlockSpec(memory_space=pltpu.SMEM),
            pl.BlockSpec((depth, tile), lambda i: (0, i)),
        ]
        + [pl.BlockSpec((rows, depth), lambda i: (0, 0)) for piece in pieces]
        + [pl.BlockSpec(memory_space=pl.ANY) for array in after],
        out_specs=[block, block],
        scratch_shapes=[pltpu.VMEM((count * rows, depth), jnp.bfloat16)],
        compiler_params=pltpu.CompilerParams(vmem_limit_bytes=VMEM_LIMIT),
        cost_estimate=SHORT,
    )(core, w_out, *pieces, *after)


def output_kernel(n_ctx, ctx_ref, *refs):
    blocks, out_ref, sems = refs[:-2], refs[-2], refs[-1]
    rows, width = blocks[0].shape
    copies = []
    for index, block in enumerate(blocks):
        chunk, offset = index // n_ctx, index % n_ctx
        column = pl.multiple_of((ctx_ref[0] ^ offset) * width, 64)
        target = out_ref.at[pl.ds(chunk * rows, rows), pl.ds(column, width)]
        copies.append(pltpu.make_async_copy(block, target, sems.at[index]))
    for copy in copies:
        copy.start()
    for copy in copies:
        copy.wait()


def place_columns(results, ctx, n_ctx):
    rows, width = results[0][0].shape
    blocks = [block for result in results for block in result]
    return pl.pallas_call(
        functools.partial(output_kernel, n_ctx),
        out_shape=jax.ShapeDtypeStruct((rows * len(results), n_ctx * width), jnp.bfloat16),
        in_specs=[pl.BlockSpec(memory_space=pltpu.SMEM)]
        + [pl.BlockSpec(memory_space=pl.ANY) for block in blocks],
        out_specs=pl.BlockSpec(memory_space=pl.ANY),
        scratch_shapes=[pltpu.SemaphoreType.DMA((len(blocks),))],
    )(ctx, *blocks)


def place_columns_plain(results, ctx, n_ctx):
    rows, width = results[0][0].shape
    out = jnp.zeros((rows * len(results), n_ctx * width), jnp.bfloat16)
    for chunk, result in enumerate(results):
        for offset, block in enumerate(result):
            out = lax.dynamic_update_slice(out, block, (chunk * rows, (ctx ^ offset) * width))
    return out


def shards(n_ctx, n_head, queries, kv_rows, w_kv_up, w_out, stretch_order, prefix_len):
    query_rows = queries.shape[0]
    row_span = kv_rows.shape[0]
    cache_rows = row_span - query_rows
    half = row_span // 2
    columns = w_out.shape[1]
    n_x = n_head // 2
    owned = query_rows // n_head
    piece = owned // CHUNKS
    ctx = lax.axis_index("ctx")
    head = lax.axis_index("head")
    core = head % 2
    x = head // 2

    with jax.named_scope("keys_over_ctx"):
        kv_t = kv_rows.T
        own_half = jnp.where(core == 0, kv_t[:, :half], kv_t[:, half:])
        halves = gather_pieces(own_half, n_ctx)[1:]
        others = [exchange(array, "head", n_head, 1) for array in halves]
        key_pieces = [kv_t] + halves + others

    with jax.named_scope("visible"):
        query_pos = lookup(stretch_order, ctx) * query_rows + jnp.arange(query_rows, dtype=jnp.int32)
        offsets = jnp.arange(half, dtype=jnp.int32)
        remote = ctx ^ jnp.arange(1, n_ctx, dtype=jnp.int32)
        sources = jnp.concatenate([jnp.full((2,), ctx, jnp.int32), remote, remote])
        starts = jnp.concatenate(
            [
                jnp.array([0, half], jnp.int32),
                jnp.full((n_ctx - 1,), core * half, jnp.int32),
                jnp.full((n_ctx - 1,), (1 - core) * half, jnp.int32),
            ]
        )
        within = starts[:, None] + offsets[None, :]
        slot_ids = sources[:, None] * cache_rows + within
        key_pos = lookup(stretch_order, sources)[:, None] * query_rows + within - cache_rows
        cache_pos = jnp.where(slot_ids < prefix_len[0], -1, n_ctx * query_rows)
        first_seen = jnp.where(within < cache_rows, cache_pos, key_pos).reshape(-1)
        query_pos = query_pos.reshape(n_head, CHUNKS, piece).transpose(1, 0, 2)
        query_pos = query_pos.reshape(CHUNKS, query_rows // CHUNKS)
        bias = [
            jnp.where(first_seen[None, :] <= query_pos[chunk][:, None], 0.0, MASKED).astype(jnp.float32)
            for chunk in range(CHUNKS)
        ]

    with jax.named_scope("queries_to_latent"):
        q_ext = absorb(queries, w_kv_up, n_head, piece)

    results = []
    core_array = jnp.full((1,), core, jnp.int32)
    with jax.named_scope("attention"):
        attended = [attention(q, mask, w_kv_up, key_pieces) for q, mask in zip(q_ext, bias)]
    with jax.named_scope("attended_over_ctx"):
        gathered = [gather_pieces(own, n_ctx, attended[i + 1 :]) for i, own in enumerate(attended)]
    total = None
    for chunk in range(CHUNKS):
        after = attended[chunk + 1 :] if total is None else [total]
        with jax.named_scope("out_product"):
            sent, kept = product(gathered[chunk], w_out, core_array, n_x, after)
        with jax.named_scope("sum_over_cores"):
            summed = kept + exchange(sent, "head", n_head, 1).astype(jnp.float32)
        with jax.named_scope("sum_over_x"):
            total = lax.dynamic_index_in_dim(summed, x, 0, keepdims=False)
            for offset in range(1, n_x):
                sent = lax.dynamic_index_in_dim(summed, x ^ offset, 0, keepdims=False)
                sent = exchange(sent.astype(jnp.bfloat16), "head", n_head, 2 * offset)
                total = total + sent.astype(jnp.float32)
        with jax.named_scope("columns_over_ctx"):
            total = total.astype(jnp.bfloat16)
            blocks = [total[0]] + [exchange(total[d], "ctx", n_ctx, d) for d in range(1, n_ctx)]
        results.append(blocks)
    with jax.named_scope("output"):
        place = place_columns if columns % 128 == 0 and piece % 16 == 0 else place_columns_plain
        return place(results, jnp.full((1,), ctx, jnp.int32) if place is place_columns else ctx, n_ctx)


def solution(mesh):
    placed = (
        P(("groups", "ctx"), "head"),
        P(("groups", "ctx"), None),
        P(None, "head"),
        P("head", "ctx"),
        P("groups"),
        P("groups"),
    )
    return jax.shard_map(
        functools.partial(shards, mesh.shape["ctx"], mesh.shape["head"]),
        mesh=mesh,
        in_specs=placed,
        out_specs=P(("groups", "ctx", "head"), None),
        check_vma=False,
    )
```

```python
import functools
import math

import jax
import jax.numpy as jnp
from jax import lax
from jax.experimental import pallas as pl
from jax.experimental.pallas import tpu as pltpu
from jax.sharding import PartitionSpec as P

LAT = 512
NOPE = 128
ROPE = 64
VD = 128
HEAD = NOPE + ROPE
PROJ = NOPE + VD
CHUNKS = 2
SUB_ROWS = 256
MASKED = -1e30
LOG2E = 1.4426950408889634
SCALE = LOG2E / math.sqrt(HEAD)
SHORT = pl.CostEstimate(flops=1024, bytes_accessed=1024, transcendentals=0)
IN_VMEM = pl.BlockSpec(memory_space=pltpu.VMEM)
IN_SMEM = pl.BlockSpec(memory_space=pltpu.SMEM)
IN_HBM = pl.BlockSpec(memory_space=pltpu.HBM)
ANYWHERE = pl.BlockSpec(memory_space=pl.ANY)


def params(mebibytes):
    return pltpu.CompilerParams(vmem_limit_bytes=mebibytes * 1024 * 1024)


def exchange(array, axis, size, bit):
    return lax.ppermute(array, axis, [(i, i ^ bit) for i in range(size)])


def tie_kernel(*refs):
    pass


def tie(array, after):
    if not after:
        return array
    return pl.pallas_call(
        tie_kernel,
        out_shape=jax.ShapeDtypeStruct(array.shape, array.dtype),
        in_specs=[ANYWHERE] * (1 + len(after)),
        out_specs=ANYWHERE,
        input_output_aliases={0: 0},
        cost_estimate=SHORT,
    )(array, *after)


def gather_pieces(own, size, after=()):
    pieces = {0: own}
    bit = size // 2
    while bit:
        for offset in sorted(pieces, reverse=True):
            pieces[offset ^ bit] = exchange(pieces[offset], "ctx", size, bit)
        if bit == size // 2:
            pieces[bit] = tie(pieces[bit], after)
        bit //= 2
    return [pieces[offset] for offset in range(size)]


def absorb_kernel(owners, piece, q_hbm, weight_hbm, *refs):
    out_refs = refs[:CHUNKS]
    q_ref, weight_ref, q_sem, weight_sems = refs[CHUNKS:]
    rows = q_ref.shape[0]
    head_count = weight_ref.shape[0]
    q_copy = pltpu.make_async_copy(q_hbm, q_ref, q_sem)
    q_copy.start()
    copies = []
    for head in range(head_count):
        source = weight_hbm.at[:, pl.ds(head * PROJ, NOPE)]
        copies.append(pltpu.make_async_copy(source, weight_ref.at[head], weight_sems.at[head]))
        copies[-1].start()
    q_copy.wait()
    for head in range(head_count):
        nope = q_ref[:, head * HEAD : head * HEAD + NOPE]
        rope = q_ref[:, head * HEAD + NOPE : (head + 1) * HEAD].astype(jnp.float32) * SCALE
        copies[head].wait()
        absorbed = lax.dot_general(
            nope, weight_ref[head], (((1,), (1,)), ((), ())), preferred_element_type=jnp.float32
        )
        absorbed = (absorbed * SCALE).reshape(owners, CHUNKS, piece, LAT)
        rope = rope.reshape(owners, CHUNKS, piece, ROPE)
        for chunk, out_ref in enumerate(out_refs):
            part = absorbed[:, chunk].reshape(rows // CHUNKS, LAT)
            out_ref[head, :, :LAT] = part.astype(jnp.bfloat16)
            part = rope[:, chunk].reshape(rows // CHUNKS, ROPE)
            out_ref[head, :, LAT:] = part.astype(jnp.bfloat16)


def absorb(queries, w_kv_up, owners, piece):
    rows = queries.shape[0]
    head_count = w_kv_up.shape[1] // PROJ
    shape = jax.ShapeDtypeStruct((head_count, rows // CHUNKS, LAT + ROPE), jnp.bfloat16)
    return pl.pallas_call(
        functools.partial(absorb_kernel, owners, piece),
        out_shape=[shape] * CHUNKS,
        in_specs=[IN_HBM, IN_HBM],
        out_specs=[IN_VMEM] * CHUNKS,
        scratch_shapes=[
            pltpu.VMEM(queries.shape, jnp.bfloat16),
            pltpu.VMEM((head_count, LAT, NOPE), jnp.bfloat16),
            pltpu.SemaphoreType.DMA,
            pltpu.SemaphoreType.DMA((head_count,)),
        ],
        compiler_params=params(50),
        cost_estimate=SHORT,
    )(queries, w_kv_up)


def visible_bias(order_ref, prefix_ref, own, piece, chunk, blocks, half, cache_rows, rows):
    n_ctx = order_ref.shape[0]
    query_rows = rows * CHUNKS
    row = lax.broadcasted_iota(jnp.int32, (rows, half), 0)
    column = lax.broadcasted_iota(jnp.int32, (rows, half), 1)
    owner = row // piece
    query_pos = order_ref[own] * query_rows + owner * (piece * CHUNKS) + chunk * piece + row % piece
    parts = []
    for offset, second in blocks:
        source = own ^ offset
        within = second * half + column
        cache_pos = jnp.where(
            source * cache_rows + within < prefix_ref[0], -1, n_ctx * query_rows
        )
        key_pos = order_ref[source] * query_rows + within - cache_rows
        first_seen = jnp.where(within < cache_rows, cache_pos, key_pos)
        parts.append(jnp.where(first_seen <= query_pos, 0.0, MASKED).astype(jnp.float32))
    return jnp.concatenate(parts, axis=1)


def attention_kernel(chunk, piece, cache_rows, order_ref, prefix_ref, q_ref, weight_hbm, *refs):
    heads, rows, depth = q_ref.shape
    n_ctx = order_ref.shape[0]
    if chunk == 0:
        own_hbm = refs[0]
        remote_refs = refs[1 : 2 * n_ctx - 1]
        out_ref, keys_ref, latent_ref, weight_ref, weight_sems, own_sem = refs[2 * n_ctx - 1 :]
        own_width = own_hbm.shape[1]
        own_copy = pltpu.make_async_copy(own_hbm, keys_ref.at[:, pl.ds(0, own_width)], own_sem)
        own_copy.start()
    else:
        keys_ref, latent_ref, out_ref, weight_ref, weight_sems = refs
    copies = []
    for head in range(heads):
        source = weight_hbm.at[:, pl.ds(head * PROJ + NOPE, VD)]
        copies.append(pltpu.make_async_copy(source, weight_ref.at[head], weight_sems.at[head]))
        copies[-1].start()
    amount = keys_ref.shape[1]
    half = amount // (2 * n_ctx)
    if chunk == 0:
        start = own_width
        for remote_ref in remote_refs:
            keys_ref[:, start : start + half] = remote_ref[...]
            start += half
        own_copy.wait()
        latent_ref[...] = keys_ref[:LAT, :].T
    own = lax.axis_index("ctx")
    core = lax.axis_index("head") % 2
    blocks = [(0, 0), (0, 1)]
    blocks += [(offset, core) for offset in range(1, n_ctx)]
    blocks += [(offset, 1 - core) for offset in range(1, n_ctx)]
    bias = visible_bias(
        order_ref, prefix_ref, own, piece, chunk, blocks, half, cache_rows, rows
    )
    for copy in copies:
        copy.wait()
    group = max(1, min(heads, SUB_ROWS // rows))
    for first in range(0, heads, group):
        size = group * rows
        queries = q_ref[first : first + group].reshape(size, depth)
        scores = jnp.dot(queries, keys_ref[...], preferred_element_type=jnp.float32)
        scores = scores.reshape(group, rows, amount) + bias[None]
        top = jnp.max(scores, axis=2, keepdims=True)
        weights = jnp.exp2(scores - top)
        total = jnp.sum(weights, axis=2, keepdims=True).reshape(size, 1)
        mixed = jnp.dot(
            weights.reshape(size, amount).astype(jnp.bfloat16),
            latent_ref[...],
            preferred_element_type=jnp.float32,
        )
        mixed = (mixed / total).astype(jnp.bfloat16)
        for head in range(first, first + group):
            result = jnp.dot(
                mixed[(head - first) * rows : (head - first + 1) * rows],
                weight_ref[head],
                preferred_element_type=jnp.float32,
            )
            out_ref[:, head * VD : (head + 1) * VD] = result.astype(jnp.bfloat16)


def attention(chunk, piece, cache_rows, q_ext, w_kv_up, stretch_order, prefix_len, keys):
    head_count, rows, depth = q_ext.shape
    n_ctx = stretch_order.shape[0]
    first = chunk == 0
    amount = n_ctx * keys[0].shape[1] if first else keys[0].shape[1]
    out_shape = [jax.ShapeDtypeStruct((rows, head_count * VD), jnp.bfloat16)]
    key_specs = [IN_VMEM] * len(keys)
    scratch = [
        pltpu.VMEM((head_count, LAT, VD), jnp.bfloat16),
        pltpu.SemaphoreType.DMA((head_count,)),
    ]
    if first:
        key_specs[0] = IN_HBM
        scratch.append(pltpu.SemaphoreType.DMA)
        out_shape.append(jax.ShapeDtypeStruct((depth, amount), jnp.bfloat16))
        out_shape.append(jax.ShapeDtypeStruct((amount, LAT), jnp.bfloat16))
    return pl.pallas_call(
        functools.partial(attention_kernel, chunk, piece, cache_rows),
        out_shape=out_shape,
        in_specs=[IN_SMEM, IN_SMEM, IN_VMEM, IN_HBM] + key_specs,
        out_specs=[IN_VMEM] * len(out_shape),
        scratch_shapes=scratch,
        compiler_params=params(50),
        cost_estimate=SHORT,
    )(stretch_order, prefix_len, q_ext, w_kv_up, *keys)


def product_kernel(count, n_x, after, weight_hbm, *refs):
    piece_refs = refs[:count]
    sent_ref, kept_ref, rows_ref, weight_ref, sems = refs[count + after :]
    rows = piece_refs[0].shape[0]
    tiles = weight_ref.shape[0]
    width = weight_ref.shape[2]
    copies = []
    for tile in range(tiles):
        source = weight_hbm.at[:, pl.ds(tile * width, width)]
        copies.append(pltpu.make_async_copy(source, weight_ref.at[tile], sems.at[tile]))
        copies[-1].start()
    for index, piece_ref in enumerate(piece_refs):
        rows_ref[index * rows : (index + 1) * rows, :] = piece_ref[...]
    is_first = lax.axis_index("head") % 2 == 0
    for tile in range(tiles):
        copies[tile].wait()
        result = jnp.dot(rows_ref[...], weight_ref[tile], preferred_element_type=jnp.float32)
        result = result.reshape(count, n_x, 2, rows // (2 * n_x), width)
        span = slice(tile * width, (tile + 1) * width)
        for x in range(n_x):
            first, second = result[:, x, 0], result[:, x, 1]
            sent_ref[x, :, :, span] = jnp.where(is_first, second, first).astype(jnp.bfloat16)
            kept_ref[x, :, :, span] = jnp.where(is_first, first, second)


def product(pieces, w_out, n_x, after):
    rows, depth = pieces[0].shape
    count = len(pieces)
    columns = w_out.shape[1]
    width = 256 if columns % 256 == 0 else columns
    tiles = columns // width
    shape = (n_x, count, rows // (2 * n_x), columns)
    return pl.pallas_call(
        functools.partial(product_kernel, count, n_x, len(after)),
        out_shape=[jax.ShapeDtypeStruct(shape, jnp.bfloat16), jax.ShapeDtypeStruct(shape, jnp.float32)],
        in_specs=[IN_HBM] + [IN_VMEM] * count + [ANYWHERE] * len(after),
        out_specs=[IN_VMEM, IN_VMEM],
        scratch_shapes=[
            pltpu.VMEM((count * rows, depth), jnp.bfloat16),
            pltpu.VMEM((tiles, depth, width), jnp.bfloat16),
            pltpu.SemaphoreType.DMA((tiles,)),
        ],
        compiler_params=params(50),
        cost_estimate=SHORT,
    )(w_out, *pieces, *after)


def place_kernel(n_ctx, ctx_ref, *refs):
    blocks, out_ref = refs[:-1], refs[-1]
    rows = blocks[0].shape[0]
    for offset in range(n_ctx):

        @pl.when(pl.program_id(0) == offset)
        def _():
            for chunk in range(CHUNKS):
                block = blocks[chunk * n_ctx + offset][...]
                out_ref[chunk * rows : (chunk + 1) * rows, :] = block


def place_columns(results, ctx, n_ctx):
    rows, width = results[0][0].shape
    total = rows * len(results)
    if width % 128 or rows % 16:
        out = jnp.zeros((total, n_ctx * width), jnp.bfloat16)
        for offset in range(n_ctx):
            block = jnp.concatenate([result[offset] for result in results], axis=0)
            out = lax.dynamic_update_slice(out, block, (0, (ctx ^ offset) * width))
        return out
    blocks = [block for result in results for block in result]
    return pl.pallas_call(
        functools.partial(place_kernel, n_ctx),
        out_shape=jax.ShapeDtypeStruct((total, n_ctx * width), jnp.bfloat16),
        grid_spec=pltpu.PrefetchScalarGridSpec(
            num_scalar_prefetch=1,
            grid=(n_ctx,),
            in_specs=[IN_VMEM] * len(blocks),
            out_specs=pl.BlockSpec((total, width), lambda i, ctx_ref: (0, ctx_ref[0] ^ i)),
        ),
        cost_estimate=SHORT,
    )(jnp.full((1,), ctx, jnp.int32), *blocks)


def shards(n_ctx, n_head, queries, kv_rows, w_kv_up, w_out, stretch_order, prefix_len):
    query_rows = queries.shape[0]
    row_span = kv_rows.shape[0]
    cache_rows = row_span - query_rows
    half = row_span // 2
    n_x = n_head // 2
    piece = query_rows // n_head // CHUNKS
    ctx = lax.axis_index("ctx")
    head = lax.axis_index("head")
    x = head // 2

    with jax.named_scope("keys_over_ctx"):
        kv_t = kv_rows.T
        own_half = jnp.where(head % 2 == 0, kv_t[:, :half], kv_t[:, half:])
        halves = [exchange(own_half, "ctx", n_ctx, offset) for offset in range(1, n_ctx)]
    with jax.named_scope("queries_to_latent"):
        q_ext = absorb(queries, w_kv_up, n_head, piece)
    with jax.named_scope("keys_over_cores"):
        halves = [tie(array, q_ext[:1]) for array in halves]
        others = [exchange(array, "head", n_head, 1) for array in halves]
    keys = [kv_t] + halves + others
    attended = []
    for chunk in range(CHUNKS):
        with jax.named_scope("attention"):
            result = attention(
                chunk, piece, cache_rows, q_ext[chunk], w_kv_up, stretch_order, prefix_len, keys
            )
        attended.append(result[0])
        if chunk == 0:
            keys = list(result[1:])
    with jax.named_scope("attended_over_ctx"):
        gathered = [
            gather_pieces(own, n_ctx, attended[chunk + 1 :]) for chunk, own in enumerate(attended)
        ]
    results = []
    after = attended[1:]
    for chunk in range(CHUNKS):
        with jax.named_scope("out_product"):
            sent, kept = product(gathered[chunk], w_out, n_x, after)
        with jax.named_scope("sum_over_cores"):
            if chunk + 1 < CHUNKS:
                later = gathered[chunk + 1]
                sent = tie(sent, [later[n_ctx // 2], later[1]])
            summed = kept + exchange(sent, "head", n_head, 1).astype(jnp.float32)
        with jax.named_scope("sum_over_x"):
            total = lax.dynamic_index_in_dim(summed, x, 0, keepdims=False)
            for offset in range(1, n_x):
                sent = lax.dynamic_index_in_dim(summed, x ^ offset, 0, keepdims=False)
                sent = exchange(sent.astype(jnp.bfloat16), "head", n_head, 2 * offset)
                total = total + sent.astype(jnp.float32)
        with jax.named_scope("columns_over_ctx"):
            total = total.astype(jnp.bfloat16)
            after = [total]
            blocks = [total[0]] + [exchange(total[d], "ctx", n_ctx, d) for d in range(1, n_ctx)]
        results.append(blocks)
    with jax.named_scope("output"):
        return place_columns(results, ctx, n_ctx)


def solution(mesh):
    placed = (
        P(("groups", "ctx"), "head"),
        P(("groups", "ctx"), None),
        P(None, "head"),
        P("head", "ctx"),
        P("groups"),
        P("groups"),
    )
    return jax.shard_map(
        functools.partial(shards, mesh.shape["ctx"], mesh.shape["head"]),
        mesh=mesh,
        in_specs=placed,
        out_specs=P(("groups", "ctx", "head"), None),
        check_vma=False,
    )
```

```python
import functools
import math

import jax
import jax.numpy as jnp
from jax import lax
from jax.experimental import pallas as pl
from jax.experimental.pallas import tpu as pltpu
from jax.sharding import PartitionSpec as P

LAT = 512
NOPE = 128
ROPE = 64
VD = 128
HEAD = NOPE + ROPE
PROJ = NOPE + VD
CHUNKS = 2
SUB_ROWS = 256
LOAD_LIMIT = 44
MASKED = -1e30
LOG2E = 1.4426950408889634
SCALE = LOG2E / math.sqrt(HEAD)
SHORT = pl.CostEstimate(flops=1024, bytes_accessed=1024, transcendentals=0)
IN_VMEM = pl.BlockSpec(memory_space=pltpu.VMEM)
IN_SMEM = pl.BlockSpec(memory_space=pltpu.SMEM)
IN_HBM = pl.BlockSpec(memory_space=pltpu.HBM)
ANYWHERE = pl.BlockSpec(memory_space=pl.ANY)


def params(mebibytes):
    return pltpu.CompilerParams(vmem_limit_bytes=mebibytes * 1024 * 1024)


def exchange(array, axis, size, bit):
    return lax.ppermute(array, axis, [(i, i ^ bit) for i in range(size)])


def tie_kernel(*refs):
    pass


def tie(array, after):
    if not after:
        return array
    return pl.pallas_call(
        tie_kernel,
        out_shape=jax.ShapeDtypeStruct(array.shape, array.dtype),
        in_specs=[ANYWHERE] * (1 + len(after)),
        out_specs=ANYWHERE,
        input_output_aliases={0: 0},
        compiler_params=params(1),
        cost_estimate=SHORT,
    )(array, *after)


def gather_pieces(own, size, after=()):
    pieces = {0: own}
    bit = size // 2
    while bit:
        for offset in sorted(pieces, reverse=True):
            pieces[offset ^ bit] = exchange(pieces[offset], "ctx", size, bit)
        if bit == size // 2:
            pieces[bit] = tie(pieces[bit], after)
        bit //= 2
    return [pieces[offset] for offset in range(size)]


def load_kernel(owners, piece, cache_rows, order_ref, prefix_ref, q_hbm, up_hbm, own_hbm, *refs):
    q_exts, refs = refs[:CHUNKS], refs[CHUNKS:]
    biases, refs = refs[:CHUNKS], refs[CHUNKS:]
    value_ref, own_ref, q_ref, key_ref, sems, key_sems, value_sems = refs
    rows = q_ref.shape[0]
    head_count = key_ref.shape[0]
    q_copy = pltpu.make_async_copy(q_hbm, q_ref, sems.at[0])
    own_copy = pltpu.make_async_copy(own_hbm, own_ref, sems.at[1])
    q_copy.start()
    key_copies, value_copies = [], []
    for head in range(head_count):
        source = up_hbm.at[:, pl.ds(head * PROJ, NOPE)]
        key_copies.append(pltpu.make_async_copy(source, key_ref.at[head], key_sems.at[head]))
        source = up_hbm.at[:, pl.ds(head * PROJ + NOPE, VD)]
        value_copies.append(pltpu.make_async_copy(source, value_ref.at[head], value_sems.at[head]))
    for copy in key_copies + [own_copy] + value_copies:
        copy.start()
    for chunk, bias_ref in enumerate(biases):
        visible_bias(order_ref, prefix_ref, bias_ref, piece, chunk, own_hbm.shape[1], cache_rows)
    q_copy.wait()
    for head in range(head_count):
        nope = q_ref[:, head * HEAD : head * HEAD + NOPE]
        rope = q_ref[:, head * HEAD + NOPE : (head + 1) * HEAD].astype(jnp.float32) * SCALE
        key_copies[head].wait()
        absorbed = lax.dot_general(
            nope, key_ref[head], (((1,), (1,)), ((), ())), preferred_element_type=jnp.float32
        )
        absorbed = (absorbed * SCALE).reshape(owners, CHUNKS, piece, LAT)
        rope = rope.reshape(owners, CHUNKS, piece, ROPE)
        for chunk, q_ext in enumerate(q_exts):
            part = absorbed[:, chunk].reshape(rows // CHUNKS, LAT)
            q_ext[head, :, :LAT] = part.astype(jnp.bfloat16)
            part = rope[:, chunk].reshape(rows // CHUNKS, ROPE)
            q_ext[head, :, LAT:] = part.astype(jnp.bfloat16)
    for copy in [own_copy] + value_copies:
        copy.wait()


def load(queries, w_kv_up, own_keys, stretch_order, prefix_len, owners, cache_rows):
    rows = queries.shape[0]
    part = rows // CHUNKS
    head_count = w_kv_up.shape[1] // PROJ
    n_ctx = stretch_order.shape[0]
    out_shape = [jax.ShapeDtypeStruct((head_count, part, LAT + ROPE), jnp.bfloat16)] * CHUNKS
    out_shape += [jax.ShapeDtypeStruct((part, n_ctx * own_keys.shape[1]), jnp.float32)] * CHUNKS
    out_shape += [
        jax.ShapeDtypeStruct((head_count, LAT, VD), jnp.bfloat16),
        jax.ShapeDtypeStruct(own_keys.shape, jnp.bfloat16),
    ]
    out = pl.pallas_call(
        functools.partial(load_kernel, owners, part // owners, cache_rows),
        out_shape=out_shape,
        in_specs=[IN_SMEM, IN_SMEM] + [IN_HBM] * 3,
        out_specs=[IN_VMEM] * len(out_shape),
        scratch_shapes=[
            pltpu.VMEM(queries.shape, jnp.bfloat16),
            pltpu.VMEM((head_count, LAT, NOPE), jnp.bfloat16),
            pltpu.SemaphoreType.DMA((2,)),
            pltpu.SemaphoreType.DMA((head_count,)),
            pltpu.SemaphoreType.DMA((head_count,)),
        ],
        compiler_params=params(LOAD_LIMIT),
        cost_estimate=SHORT,
    )(stretch_order, prefix_len, queries, w_kv_up, own_keys)
    return out[:CHUNKS], out[CHUNKS : 2 * CHUNKS], *out[2 * CHUNKS :]


def visible_bias(order_ref, prefix_ref, bias_ref, piece, chunk, row_span, cache_rows):
    n_ctx = order_ref.shape[0]
    half = row_span // 2
    rows = bias_ref.shape[0]
    query_rows = rows * CHUNKS
    own = lax.axis_index("ctx")
    core = lax.axis_index("head") % 2
    blocks = [(0, 0), (0, 1)]
    blocks += [(offset, core) for offset in range(1, n_ctx)]
    blocks += [(offset, 1 - core) for offset in range(1, n_ctx)]
    row = lax.broadcasted_iota(jnp.int32, (rows, half), 0)
    column = lax.broadcasted_iota(jnp.int32, (rows, half), 1)
    owner = row // piece
    query_pos = order_ref[own] * query_rows + owner * (piece * CHUNKS) + chunk * piece + row % piece
    for index, (offset, second) in enumerate(blocks):
        source = own ^ offset
        within = second * half + column
        cache_pos = jnp.where(
            source * cache_rows + within < prefix_ref[0], -1, n_ctx * query_rows
        )
        key_pos = order_ref[source] * query_rows + within - cache_rows
        first_seen = jnp.where(within < cache_rows, cache_pos, key_pos)
        bias = jnp.where(first_seen <= query_pos, 0.0, MASKED).astype(jnp.float32)
        bias_ref[:, index * half : (index + 1) * half] = bias


def attention_kernel(count, q_ref, bias_ref, value_ref, *refs):
    heads, rows, depth = q_ref.shape
    if count:
        piece_refs, (out_ref, keys_ref, latent_ref) = refs[:count], refs[count:]
        start = 0
        for piece_ref in piece_refs:
            width = piece_ref.shape[1]
            keys_ref[:, start : start + width] = piece_ref[...]
            latent_ref[start : start + width, :] = piece_ref[:LAT, :].T
            start += width
    else:
        keys_ref, latent_ref, out_ref = refs
    amount = keys_ref.shape[1]
    group = max(1, min(heads, SUB_ROWS // rows))
    size = group * rows

    def score(first):
        queries = q_ref[first : first + group].reshape(size, depth)
        return jnp.dot(queries, keys_ref[...], preferred_element_type=jnp.float32)

    scores = score(0)
    for first in range(0, heads, group):
        later = score(first + group) if first + group < heads else None
        scores = scores.reshape(group, rows, amount) + bias_ref[...][None]
        top = jnp.max(scores, axis=2, keepdims=True)
        weights = jnp.exp2(scores - top)
        total = jnp.sum(weights, axis=2, keepdims=True).reshape(size, 1)
        mixed = jnp.dot(
            weights.reshape(size, amount).astype(jnp.bfloat16),
            latent_ref[...],
            preferred_element_type=jnp.float32,
        )
        mixed = (mixed / total).astype(jnp.bfloat16)
        for head in range(first, first + group):
            result = jnp.dot(
                mixed[(head - first) * rows : (head - first + 1) * rows],
                value_ref[head],
                preferred_element_type=jnp.float32,
            )
            out_ref[:, head * VD : (head + 1) * VD] = result.astype(jnp.bfloat16)
        scores = later


def attention(q_ext, bias, w_values, keys, gathered):
    head_count, rows, depth = q_ext.shape
    amount = bias.shape[1]
    out_shape = [jax.ShapeDtypeStruct((rows, head_count * VD), jnp.bfloat16)]
    if not gathered:
        out_shape.append(jax.ShapeDtypeStruct((depth, amount), jnp.bfloat16))
        out_shape.append(jax.ShapeDtypeStruct((amount, LAT), jnp.bfloat16))
    return pl.pallas_call(
        functools.partial(attention_kernel, 0 if gathered else len(keys)),
        out_shape=out_shape,
        in_specs=[IN_VMEM] * (3 + len(keys)),
        out_specs=[IN_VMEM] * len(out_shape),
        compiler_params=params(16 if amount <= 1024 else 40),
        cost_estimate=SHORT,
    )(q_ext, bias, w_values, *keys)


def product_kernel(count, n_x, after, weight_ref, *refs):
    piece_refs = refs[:count]
    sent_ref, kept_ref, rows_ref = refs[count + after :]
    rows = piece_refs[0].shape[0]
    columns = weight_ref.shape[1]
    for index, piece_ref in enumerate(piece_refs):
        rows_ref[index * rows : (index + 1) * rows, :] = piece_ref[...]
    is_first = lax.axis_index("head") % 2 == 0
    width = 256 if columns % 256 == 0 else columns
    for start in range(0, columns, width):
        span = slice(start, start + width)
        result = jnp.dot(rows_ref[...], weight_ref[:, span], preferred_element_type=jnp.float32)
        result = result.reshape(count, n_x, 2, rows // (2 * n_x), width)
        for x in range(n_x):
            first, second = result[:, x, 0], result[:, x, 1]
            sent_ref[x, :, :, span] = jnp.where(is_first, second, first).astype(jnp.bfloat16)
            kept_ref[x, :, :, span] = jnp.where(is_first, first, second)


def product(pieces, w_out, n_x, after):
    rows, depth = pieces[0].shape
    count = len(pieces)
    shape = (n_x, count, rows // (2 * n_x), w_out.shape[1])
    return pl.pallas_call(
        functools.partial(product_kernel, count, n_x, len(after)),
        out_shape=[jax.ShapeDtypeStruct(shape, jnp.bfloat16), jax.ShapeDtypeStruct(shape, jnp.float32)],
        in_specs=[IN_VMEM] * (1 + count) + [ANYWHERE] * len(after),
        out_specs=[IN_VMEM, IN_VMEM],
        scratch_shapes=[pltpu.VMEM((count * rows, depth), jnp.bfloat16)],
        compiler_params=params(16),
        cost_estimate=SHORT,
    )(w_out, *pieces, *after)


def place_kernel(n_ctx, ctx_ref, *refs):
    blocks, out_ref = refs[:-1], refs[-1]
    rows = blocks[0].shape[0]
    for offset in range(n_ctx):

        @pl.when(pl.program_id(0) == offset)
        def _():
            for chunk in range(CHUNKS):
                block = blocks[chunk * n_ctx + offset][...]
                out_ref[chunk * rows : (chunk + 1) * rows, :] = block


def place_columns(results, ctx, n_ctx):
    rows, width = results[0][0].shape
    total = rows * len(results)
    if width % 128 or rows % 16:
        out = jnp.zeros((total, n_ctx * width), jnp.bfloat16)
        for offset in range(n_ctx):
            block = jnp.concatenate([result[offset] for result in results], axis=0)
            out = lax.dynamic_update_slice(out, block, (0, (ctx ^ offset) * width))
        return out
    blocks = [block for result in results for block in result]
    return pl.pallas_call(
        functools.partial(place_kernel, n_ctx),
        out_shape=jax.ShapeDtypeStruct((total, n_ctx * width), jnp.bfloat16),
        grid_spec=pltpu.PrefetchScalarGridSpec(
            num_scalar_prefetch=1,
            grid=(n_ctx,),
            in_specs=[IN_VMEM] * len(blocks),
            out_specs=pl.BlockSpec((total, width), lambda i, ctx_ref: (0, ctx_ref[0] ^ i)),
        ),
        compiler_params=params(4),
        cost_estimate=SHORT,
    )(jnp.full((1,), ctx, jnp.int32), *blocks)


def shards(n_ctx, n_head, queries, kv_rows, w_kv_up, w_out, stretch_order, prefix_len):
    query_rows = queries.shape[0]
    row_span = kv_rows.shape[0]
    cache_rows = row_span - query_rows
    half = row_span // 2
    n_x = n_head // 2
    ctx = lax.axis_index("ctx")
    head = lax.axis_index("head")
    x = head // 2

    with jax.named_scope("keys_over_ctx"):
        kv_t = kv_rows.T
        own_half = jnp.where(head % 2 == 0, kv_t[:, :half], kv_t[:, half:])
        halves = [exchange(own_half, "ctx", n_ctx, offset) for offset in range(1, n_ctx)]
    with jax.named_scope("load"):
        q_ext, bias, w_values, own_keys = load(
            queries, w_kv_up, kv_t, stretch_order, prefix_len, n_head, cache_rows
        )
    with jax.named_scope("keys_over_cores"):
        halves = [tie(array, [own_keys]) for array in halves]
        others = [exchange(array, "head", n_head, 1) for array in halves]
    keys = [own_keys] + halves + others
    attended = []
    for chunk in range(CHUNKS):
        with jax.named_scope("attention"):
            result = attention(q_ext[chunk], bias[chunk], w_values, keys, chunk > 0)
        attended.append(result[0])
        if chunk == 0:
            keys = list(result[1:])
    with jax.named_scope("attended_over_ctx"):
        gathered = [gather_pieces(attended[0], n_ctx, attended[1:])]
        for own in attended[1:]:
            gathered.append([own] + [exchange(own, "ctx", n_ctx, d) for d in range(1, n_ctx)])
    results = []
    after = attended[1:]
    for chunk in range(CHUNKS):
        with jax.named_scope("out_product"):
            sent, kept = product(gathered[chunk], w_out, n_x, after)
            after = [sent]
        with jax.named_scope("sum_over_cores"):
            if chunk + 1 < CHUNKS:
                later = gathered[chunk + 1]
                sent = tie(sent, later[1:])
            summed = kept + exchange(sent, "head", n_head, 1).astype(jnp.float32)
        with jax.named_scope("sum_over_x"):
            total = lax.dynamic_index_in_dim(summed, x, 0, keepdims=False)
            for offset in range(1, n_x):
                sent = lax.dynamic_index_in_dim(summed, x ^ offset, 0, keepdims=False)
                sent = exchange(sent.astype(jnp.bfloat16), "head", n_head, 2 * offset)
                total = total + sent.astype(jnp.float32)
        with jax.named_scope("columns_over_ctx"):
            total = total.astype(jnp.bfloat16)
            blocks = [total[0]] + [exchange(total[d], "ctx", n_ctx, d) for d in range(1, n_ctx)]
        results.append(blocks)
    with jax.named_scope("output"):
        return place_columns(results, ctx, n_ctx)


def solution(mesh):
    placed = (
        P(("groups", "ctx"), "head"),
        P(("groups", "ctx"), None),
        P(None, "head"),
        P("head", "ctx"),
        P("groups"),
        P("groups"),
    )
    return jax.shard_map(
        functools.partial(shards, mesh.shape["ctx"], mesh.shape["head"]),
        mesh=mesh,
        in_specs=placed,
        out_specs=P(("groups", "ctx", "head"), None),
        check_vma=False,
    )
```

```python
import functools
import math

import jax
import jax.numpy as jnp
from jax import lax
from jax.experimental import pallas as pl
from jax.experimental.pallas import tpu as pltpu
from jax.sharding import PartitionSpec as P

LAT = 512
NOPE = 128
ROPE = 64
VD = 128
HEAD = NOPE + ROPE
PROJ = NOPE + VD
CHUNKS = 2
SUB_ROWS = 256
LOAD_LIMIT = 44
MASKED = -1e30
LOG2E = 1.4426950408889634
SCALE = LOG2E / math.sqrt(HEAD)
SHORT = pl.CostEstimate(flops=1024, bytes_accessed=1024, transcendentals=0)
IN_VMEM = pl.BlockSpec(memory_space=pltpu.VMEM)
IN_SMEM = pl.BlockSpec(memory_space=pltpu.SMEM)
IN_HBM = pl.BlockSpec(memory_space=pltpu.HBM)
ANYWHERE = pl.BlockSpec(memory_space=pl.ANY)


def params(mebibytes):
    return pltpu.CompilerParams(vmem_limit_bytes=mebibytes * 1024 * 1024)


def exchange(array, axis, size, bit):
    return lax.ppermute(array, axis, [(i, i ^ bit) for i in range(size)])


def tie_kernel(*refs):
    pass


def tie(array, after):
    if not after:
        return array
    return pl.pallas_call(
        tie_kernel,
        out_shape=jax.ShapeDtypeStruct(array.shape, array.dtype),
        in_specs=[ANYWHERE] * (1 + len(after)),
        out_specs=ANYWHERE,
        input_output_aliases={0: 0},
        compiler_params=params(1),
        cost_estimate=SHORT,
    )(array, *after)


def gather_pieces(own, size, after=()):
    pieces = {0: own}
    bit = size // 2
    while bit:
        pieces[bit] = exchange(own, "ctx", size, bit)
        bit //= 2
    bit = 1
    while bit < size:
        for offset in range(bit + 1, 2 * bit):
            if offset == bit + 1:
                pieces[bit] = tie(pieces[bit], after)
            pieces[offset] = exchange(pieces[bit], "ctx", size, offset ^ bit)
        bit *= 2
    return [pieces[offset] for offset in range(size)]


def load_kernel(owners, piece, cache_rows, order_ref, prefix_ref, q_hbm, up_hbm, own_hbm, *refs):
    q_exts, refs = refs[:CHUNKS], refs[CHUNKS:]
    biases, refs = refs[:CHUNKS], refs[CHUNKS:]
    value_ref, own_ref, q_ref, key_ref, sems, key_sems, value_sems = refs
    rows = q_ref.shape[0]
    head_count = key_ref.shape[0]
    q_copy = pltpu.make_async_copy(q_hbm, q_ref, sems.at[0])
    own_copy = pltpu.make_async_copy(own_hbm, own_ref, sems.at[1])
    q_copy.start()
    key_copies, value_copies = [], []
    for head in range(head_count):
        source = up_hbm.at[:, pl.ds(head * PROJ, NOPE)]
        key_copies.append(pltpu.make_async_copy(source, key_ref.at[head], key_sems.at[head]))
        source = up_hbm.at[:, pl.ds(head * PROJ + NOPE, VD)]
        value_copies.append(pltpu.make_async_copy(source, value_ref.at[head], value_sems.at[head]))
    for copy in key_copies + [own_copy] + value_copies:
        copy.start()
    for chunk, bias_ref in enumerate(biases):
        visible_bias(order_ref, prefix_ref, bias_ref, piece, chunk, own_hbm.shape[1], cache_rows)
    q_copy.wait()
    for head in range(head_count):
        nope = q_ref[:, head * HEAD : head * HEAD + NOPE]
        rope = q_ref[:, head * HEAD + NOPE : (head + 1) * HEAD].astype(jnp.float32) * SCALE
        key_copies[head].wait()
        absorbed = lax.dot_general(
            nope, key_ref[head], (((1,), (1,)), ((), ())), preferred_element_type=jnp.float32
        )
        absorbed = (absorbed * SCALE).reshape(owners, CHUNKS, piece, LAT)
        rope = rope.reshape(owners, CHUNKS, piece, ROPE)
        for chunk, q_ext in enumerate(q_exts):
            part = absorbed[:, chunk].reshape(rows // CHUNKS, LAT)
            q_ext[head, :, :LAT] = part.astype(jnp.bfloat16)
            part = rope[:, chunk].reshape(rows // CHUNKS, ROPE)
            q_ext[head, :, LAT:] = part.astype(jnp.bfloat16)
    for copy in [own_copy] + value_copies:
        copy.wait()


def load(queries, w_kv_up, own_keys, stretch_order, prefix_len, owners, cache_rows):
    rows = queries.shape[0]
    part = rows // CHUNKS
    head_count = w_kv_up.shape[1] // PROJ
    n_ctx = stretch_order.shape[0]
    out_shape = [jax.ShapeDtypeStruct((head_count, part, LAT + ROPE), jnp.bfloat16)] * CHUNKS
    out_shape += [jax.ShapeDtypeStruct((part, n_ctx * own_keys.shape[1]), jnp.float32)] * CHUNKS
    out_shape += [
        jax.ShapeDtypeStruct((head_count, LAT, VD), jnp.bfloat16),
        jax.ShapeDtypeStruct(own_keys.shape, jnp.bfloat16),
    ]
    out = pl.pallas_call(
        functools.partial(load_kernel, owners, part // owners, cache_rows),
        out_shape=out_shape,
        in_specs=[IN_SMEM, IN_SMEM] + [IN_HBM] * 3,
        out_specs=[IN_VMEM] * len(out_shape),
        scratch_shapes=[
            pltpu.VMEM(queries.shape, jnp.bfloat16),
            pltpu.VMEM((head_count, LAT, NOPE), jnp.bfloat16),
            pltpu.SemaphoreType.DMA((2,)),
            pltpu.SemaphoreType.DMA((head_count,)),
            pltpu.SemaphoreType.DMA((head_count,)),
        ],
        compiler_params=params(LOAD_LIMIT),
        cost_estimate=SHORT,
    )(stretch_order, prefix_len, queries, w_kv_up, own_keys)
    return out[:CHUNKS], out[CHUNKS : 2 * CHUNKS], *out[2 * CHUNKS :]


def visible_bias(order_ref, prefix_ref, bias_ref, piece, chunk, row_span, cache_rows):
    n_ctx = order_ref.shape[0]
    half = row_span // 2
    rows = bias_ref.shape[0]
    query_rows = rows * CHUNKS
    own = lax.axis_index("ctx")
    core = lax.axis_index("head") % 2
    blocks = [(0, 0), (0, 1)]
    blocks += [(offset, core) for offset in range(1, n_ctx)]
    blocks += [(offset, 1 - core) for offset in range(1, n_ctx)]
    row = lax.broadcasted_iota(jnp.int32, (rows, half), 0)
    column = lax.broadcasted_iota(jnp.int32, (rows, half), 1)
    owner = row // piece
    query_pos = order_ref[own] * query_rows + owner * (piece * CHUNKS) + chunk * piece + row % piece
    for index, (offset, second) in enumerate(blocks):
        source = own ^ offset
        within = second * half + column
        cache_pos = jnp.where(
            source * cache_rows + within < prefix_ref[0], -1, n_ctx * query_rows
        )
        key_pos = order_ref[source] * query_rows + within - cache_rows
        first_seen = jnp.where(within < cache_rows, cache_pos, key_pos)
        bias = jnp.where(first_seen <= query_pos, 0.0, MASKED).astype(jnp.float32)
        bias_ref[:, index * half : (index + 1) * half] = bias


def attention_kernel(count, q_ref, bias_ref, value_ref, *refs):
    heads, rows, depth = q_ref.shape
    if count:
        piece_refs, (out_ref, keys_ref, latent_ref) = refs[:count], refs[count:]
        start = 0
        for piece_ref in piece_refs:
            width = piece_ref.shape[1]
            keys_ref[:, start : start + width] = piece_ref[...]
            latent_ref[start : start + width, :] = piece_ref[:LAT, :].T
            start += width
    else:
        keys_ref, latent_ref, out_ref = refs
    amount = keys_ref.shape[1]
    group = max(1, min(heads, SUB_ROWS // rows))
    size = group * rows

    def score(first):
        queries = q_ref[first : first + group].reshape(size, depth)
        return jnp.dot(queries, keys_ref[...], preferred_element_type=jnp.float32)

    scores = score(0)
    for first in range(0, heads, group):
        later = score(first + group) if first + group < heads else None
        scores = scores.reshape(group, rows, amount) + bias_ref[...][None]
        top = jnp.max(scores, axis=2, keepdims=True)
        weights = jnp.exp2(scores - top)
        total = jnp.sum(weights, axis=2, keepdims=True).reshape(size, 1)
        mixed = jnp.dot(
            weights.reshape(size, amount).astype(jnp.bfloat16),
            latent_ref[...],
            preferred_element_type=jnp.float32,
        )
        mixed = (mixed / total).astype(jnp.bfloat16)
        for head in range(first, first + group):
            result = jnp.dot(
                mixed[(head - first) * rows : (head - first + 1) * rows],
                value_ref[head],
                preferred_element_type=jnp.float32,
            )
            out_ref[:, head * VD : (head + 1) * VD] = result.astype(jnp.bfloat16)
        scores = later


def attention(q_ext, bias, w_values, keys, gathered):
    head_count, rows, depth = q_ext.shape
    amount = bias.shape[1]
    out_shape = [jax.ShapeDtypeStruct((rows, head_count * VD), jnp.bfloat16)]
    if not gathered:
        out_shape.append(jax.ShapeDtypeStruct((depth, amount), jnp.bfloat16))
        out_shape.append(jax.ShapeDtypeStruct((amount, LAT), jnp.bfloat16))
    return pl.pallas_call(
        functools.partial(attention_kernel, 0 if gathered else len(keys)),
        out_shape=out_shape,
        in_specs=[IN_VMEM] * (3 + len(keys)),
        out_specs=[IN_VMEM] * len(out_shape),
        compiler_params=params(16 if amount <= 1024 else 40),
        cost_estimate=SHORT,
    )(q_ext, bias, w_values, *keys)


def product_kernel(count, n_x, after, weight_ref, *refs):
    piece_refs = refs[:count]
    sent_ref, kept_ref, rows_ref = refs[count + after :]
    rows = piece_refs[0].shape[0]
    columns = weight_ref.shape[1]
    for index, piece_ref in enumerate(piece_refs):
        rows_ref[index * rows : (index + 1) * rows, :] = piece_ref[...]
    is_first = lax.axis_index("head") % 2 == 0
    width = 256 if columns % 256 == 0 else columns
    for start in range(0, columns, width):
        span = slice(start, start + width)
        result = jnp.dot(rows_ref[...], weight_ref[:, span], preferred_element_type=jnp.float32)
        result = result.reshape(count, n_x, 2, rows // (2 * n_x), width)
        for x in range(n_x):
            first, second = result[:, x, 0], result[:, x, 1]
            sent_ref[x, :, :, span] = jnp.where(is_first, second, first).astype(jnp.bfloat16)
            kept_ref[x, :, :, span] = jnp.where(is_first, first, second)


def product(pieces, w_out, n_x, after):
    rows, depth = pieces[0].shape
    count = len(pieces)
    shape = (n_x, count, rows // (2 * n_x), w_out.shape[1])
    return pl.pallas_call(
        functools.partial(product_kernel, count, n_x, len(after)),
        out_shape=[jax.ShapeDtypeStruct(shape, jnp.bfloat16), jax.ShapeDtypeStruct(shape, jnp.float32)],
        in_specs=[IN_VMEM] * (1 + count) + [ANYWHERE] * len(after),
        out_specs=[IN_VMEM, IN_VMEM],
        scratch_shapes=[pltpu.VMEM((count * rows, depth), jnp.bfloat16)],
        compiler_params=params(16),
        cost_estimate=SHORT,
    )(w_out, *pieces, *after)


def place_kernel(n_ctx, ctx_ref, *refs):
    blocks, out_ref = refs[:-1], refs[-1]
    rows = blocks[0].shape[0]
    for offset in range(n_ctx):

        @pl.when(pl.program_id(0) == offset)
        def _():
            for chunk in range(CHUNKS):
                block = blocks[chunk * n_ctx + offset][...]
                out_ref[chunk * rows : (chunk + 1) * rows, :] = block


def place_columns(results, ctx, n_ctx):
    rows, width = results[0][0].shape
    total = rows * len(results)
    if width % 128 or rows % 16:
        out = jnp.zeros((total, n_ctx * width), jnp.bfloat16)
        for offset in range(n_ctx):
            block = jnp.concatenate([result[offset] for result in results], axis=0)
            out = lax.dynamic_update_slice(out, block, (0, (ctx ^ offset) * width))
        return out
    blocks = [block for result in results for block in result]
    return pl.pallas_call(
        functools.partial(place_kernel, n_ctx),
        out_shape=jax.ShapeDtypeStruct((total, n_ctx * width), jnp.bfloat16),
        grid_spec=pltpu.PrefetchScalarGridSpec(
            num_scalar_prefetch=1,
            grid=(n_ctx,),
            in_specs=[IN_VMEM] * len(blocks),
            out_specs=pl.BlockSpec((total, width), lambda i, ctx_ref: (0, ctx_ref[0] ^ i)),
        ),
        compiler_params=params(4),
        cost_estimate=SHORT,
    )(jnp.full((1,), ctx, jnp.int32), *blocks)


def shards(n_ctx, n_head, queries, kv_rows, w_kv_up, w_out, stretch_order, prefix_len):
    query_rows = queries.shape[0]
    row_span = kv_rows.shape[0]
    cache_rows = row_span - query_rows
    half = row_span // 2
    n_x = n_head // 2
    ctx = lax.axis_index("ctx")
    head = lax.axis_index("head")
    x = head // 2

    with jax.named_scope("keys_over_ctx"):
        kv_t = kv_rows.T
        own_half = jnp.where(head % 2 == 0, kv_t[:, :half], kv_t[:, half:])
        halves = [exchange(own_half, "ctx", n_ctx, offset) for offset in range(1, n_ctx)]
    with jax.named_scope("load"):
        q_ext, bias, w_values, own_keys = load(
            queries, w_kv_up, kv_t, stretch_order, prefix_len, n_head, cache_rows
        )
    with jax.named_scope("keys_over_cores"):
        halves = [tie(array, [own_keys]) for array in halves]
        others = [exchange(array, "head", n_head, 1) for array in halves]
    keys = [own_keys] + halves + others
    attended = []
    for chunk in range(CHUNKS):
        with jax.named_scope("attention"):
            result = attention(q_ext[chunk], bias[chunk], w_values, keys, chunk > 0)
        attended.append(result[0])
        if chunk == 0:
            keys = list(result[1:])
    with jax.named_scope("attended_over_ctx"):
        gathered = [
            gather_pieces(own, n_ctx, attended[chunk + 1 :]) for chunk, own in enumerate(attended)
        ]
    results = []
    after = attended[1:]
    for chunk in range(CHUNKS):
        with jax.named_scope("out_product"):
            sent, kept = product(gathered[chunk], w_out, n_x, after)
        with jax.named_scope("sum_over_cores"):
            if chunk + 1 < CHUNKS:
                received = [gathered[chunk + 1][1], gathered[chunk + 1][n_ctx // 2]]
            sent = tie(sent, received)
            summed = kept + exchange(sent, "head", n_head, 1).astype(jnp.float32)
            after = [summed]
        with jax.named_scope("sum_over_x"):
            total = lax.dynamic_index_in_dim(summed, x, 0, keepdims=False)
            received = []
            for offset in range(1, n_x):
                sent = lax.dynamic_index_in_dim(summed, x ^ offset, 0, keepdims=False)
                sent = exchange(sent.astype(jnp.bfloat16), "head", n_head, 2 * offset)
                received.append(sent)
                total = total + sent.astype(jnp.float32)
        with jax.named_scope("columns_over_ctx"):
            total = total.astype(jnp.bfloat16)
            blocks = [total[0]] + [exchange(total[d], "ctx", n_ctx, d) for d in range(1, n_ctx)]
        results.append(blocks)
    with jax.named_scope("output"):
        return place_columns(results, ctx, n_ctx)


def solution(mesh):
    placed = (
        P(("groups", "ctx"), "head"),
        P(("groups", "ctx"), None),
        P(None, "head"),
        P("head", "ctx"),
        P("groups"),
        P("groups"),
    )
    return jax.shard_map(
        functools.partial(shards, mesh.shape["ctx"], mesh.shape["head"]),
        mesh=mesh,
        in_specs=placed,
        out_specs=P(("groups", "ctx", "head"), None),
        check_vma=False,
    )
```

```python
import functools
import math

import jax
import jax.numpy as jnp
from jax import lax
from jax.experimental import pallas as pl
from jax.experimental.pallas import tpu as pltpu
from jax.sharding import PartitionSpec as P

LAT = 512
NOPE = 128
ROPE = 64
VD = 128
HEAD = NOPE + ROPE
PROJ = NOPE + VD
SUB_ROWS = 256
LOAD_LIMIT = 44
MASKED = -1e30
LOG2E = 1.4426950408889634
SCALE = LOG2E / math.sqrt(HEAD)
SHORT = pl.CostEstimate(flops=1024, bytes_accessed=1024, transcendentals=0)
IN_VMEM = pl.BlockSpec(memory_space=pltpu.VMEM)
IN_SMEM = pl.BlockSpec(memory_space=pltpu.SMEM)
IN_HBM = pl.BlockSpec(memory_space=pltpu.HBM)
ANYWHERE = pl.BlockSpec(memory_space=pl.ANY)


def chunk_rows(owned):
    if owned % 32 == 0:
        return (owned // 2, owned // 4, owned // 4)
    return (owned // 2, owned // 2)


def params(mebibytes):
    return pltpu.CompilerParams(vmem_limit_bytes=mebibytes * 1024 * 1024)


def exchange(array, axis, size, bit):
    return lax.ppermute(array, axis, [(i, i ^ bit) for i in range(size)])


def tie_kernel(*refs):
    pass


def tie(array, after):
    if not after:
        return array
    return pl.pallas_call(
        tie_kernel,
        out_shape=jax.ShapeDtypeStruct(array.shape, array.dtype),
        in_specs=[ANYWHERE] * (1 + len(after)),
        out_specs=ANYWHERE,
        input_output_aliases={0: 0},
        compiler_params=params(1),
        cost_estimate=SHORT,
    )(array, *after)


def gather_pieces(own, size, after=()):
    pieces = {0: own}
    bit = size // 2
    while bit:
        pieces[bit] = exchange(own, "ctx", size, bit)
        bit //= 2
    bit = 1
    while bit < size:
        for offset in range(bit + 1, 2 * bit):
            if offset == bit + 1:
                pieces[bit] = tie(pieces[bit], after)
            pieces[offset] = exchange(pieces[bit], "ctx", size, offset ^ bit)
        bit *= 2
    return [pieces[offset] for offset in range(size)]


def load_kernel(owners, pieces, cache_rows, order_ref, prefix_ref, q_hbm, up_hbm, own_hbm, *refs):
    count = len(pieces)
    q_exts, biases, refs = refs[:count], refs[count : 2 * count], refs[2 * count :]
    value_ref, own_ref, q_ref, key_ref, sems, key_sems, value_sems = refs
    rows = q_ref.shape[0]
    head_count = key_ref.shape[0]
    q_copy = pltpu.make_async_copy(q_hbm, q_ref, sems.at[0])
    own_copy = pltpu.make_async_copy(own_hbm, own_ref, sems.at[1])
    q_copy.start()
    key_copies, value_copies = [], []
    for head in range(head_count):
        source = up_hbm.at[:, pl.ds(head * PROJ, NOPE)]
        key_copies.append(pltpu.make_async_copy(source, key_ref.at[head], key_sems.at[head]))
        source = up_hbm.at[:, pl.ds(head * PROJ + NOPE, VD)]
        value_copies.append(pltpu.make_async_copy(source, value_ref.at[head], value_sems.at[head]))
    for copy in key_copies + [own_copy] + value_copies:
        copy.start()
    start = 0
    for piece, bias_ref in zip(pieces, biases):
        visible_bias(
            order_ref, prefix_ref, bias_ref, rows, owners, start, own_hbm.shape[1], cache_rows
        )
        start += piece
    q_copy.wait()
    for head in range(head_count):
        nope = q_ref[:, head * HEAD : head * HEAD + NOPE]
        rope = q_ref[:, head * HEAD + NOPE : (head + 1) * HEAD].astype(jnp.float32) * SCALE
        key_copies[head].wait()
        absorbed = lax.dot_general(
            nope, key_ref[head], (((1,), (1,)), ((), ())), preferred_element_type=jnp.float32
        )
        absorbed = (absorbed * SCALE).reshape(owners, rows // owners, LAT)
        rope = rope.reshape(owners, rows // owners, ROPE)
        start = 0
        for piece, q_ext in zip(pieces, q_exts):
            part = absorbed[:, start : start + piece].reshape(owners * piece, LAT)
            q_ext[head, :, :LAT] = part.astype(jnp.bfloat16)
            part = rope[:, start : start + piece].reshape(owners * piece, ROPE)
            q_ext[head, :, LAT:] = part.astype(jnp.bfloat16)
            start += piece
    for copy in [own_copy] + value_copies:
        copy.wait()


def load(queries, w_kv_up, own_keys, stretch_order, prefix_len, owners, pieces, cache_rows):
    head_count = w_kv_up.shape[1] // PROJ
    amount = stretch_order.shape[0] * own_keys.shape[1]
    out_shape = [
        jax.ShapeDtypeStruct((head_count, owners * piece, LAT + ROPE), jnp.bfloat16)
        for piece in pieces
    ]
    out_shape += [jax.ShapeDtypeStruct((owners * piece, amount), jnp.float32) for piece in pieces]
    out_shape += [
        jax.ShapeDtypeStruct((head_count, LAT, VD), jnp.bfloat16),
        jax.ShapeDtypeStruct(own_keys.shape, jnp.bfloat16),
    ]
    out = pl.pallas_call(
        functools.partial(load_kernel, owners, pieces, cache_rows),
        out_shape=out_shape,
        in_specs=[IN_SMEM, IN_SMEM] + [IN_HBM] * 3,
        out_specs=[IN_VMEM] * len(out_shape),
        scratch_shapes=[
            pltpu.VMEM(queries.shape, jnp.bfloat16),
            pltpu.VMEM((head_count, LAT, NOPE), jnp.bfloat16),
            pltpu.SemaphoreType.DMA((2,)),
            pltpu.SemaphoreType.DMA((head_count,)),
            pltpu.SemaphoreType.DMA((head_count,)),
        ],
        compiler_params=params(LOAD_LIMIT),
        cost_estimate=SHORT,
    )(stretch_order, prefix_len, queries, w_kv_up, own_keys)
    count = len(pieces)
    return out[:count], out[count : 2 * count], *out[2 * count :]


def visible_bias(order_ref, prefix_ref, bias_ref, query_rows, owners, start, row_span, cache_rows):
    n_ctx = order_ref.shape[0]
    half = row_span // 2
    rows = bias_ref.shape[0]
    piece = rows // owners
    own = lax.axis_index("ctx")
    core = lax.axis_index("head") % 2
    blocks = [(0, 0), (0, 1)]
    blocks += [(offset, core) for offset in range(1, n_ctx)]
    blocks += [(offset, 1 - core) for offset in range(1, n_ctx)]
    row = lax.broadcasted_iota(jnp.int32, (rows, half), 0)
    column = lax.broadcasted_iota(jnp.int32, (rows, half), 1)
    within_own = row // piece * (query_rows // owners) + start + row % piece
    query_pos = order_ref[own] * query_rows + within_own
    for index, (offset, second) in enumerate(blocks):
        source = own ^ offset
        within = second * half + column
        cache_pos = jnp.where(
            source * cache_rows + within < prefix_ref[0], -1, n_ctx * query_rows
        )
        key_pos = order_ref[source] * query_rows + within - cache_rows
        first_seen = jnp.where(within < cache_rows, cache_pos, key_pos)
        bias = jnp.where(first_seen <= query_pos, 0.0, MASKED).astype(jnp.float32)
        bias_ref[:, index * half : (index + 1) * half] = bias


def attention_kernel(count, hold, q_ref, bias_ref, value_ref, *refs):
    heads, rows, depth = q_ref.shape
    if count:
        piece_refs, (out_ref, keys_ref, latent_ref) = refs[:count], refs[count:]
        start = 0
        for piece_ref in piece_refs:
            width = piece_ref.shape[1]
            keys_ref[:, start : start + width] = piece_ref[...]
            latent_ref[start : start + width, :] = piece_ref[:LAT, :].T
            start += width
    else:
        keys_ref, latent_ref, *refs = refs
        if hold:
            mix_hbm, out_ref, mix_ref, mix_sem = refs
            mix_copy = pltpu.make_async_copy(mix_hbm, mix_ref, mix_sem)
            mix_copy.start()
        else:
            (out_ref,) = refs
    amount = keys_ref.shape[1]
    group = max(1, min(heads, SUB_ROWS // rows))
    size = group * rows

    def score(first):
        queries = q_ref[first : first + group].reshape(size, depth)
        return jnp.dot(queries, keys_ref[...], preferred_element_type=jnp.float32)

    scores = score(0)
    for first in range(0, heads, group):
        later = score(first + group) if first + group < heads else None
        scores = scores.reshape(group, rows, amount) + bias_ref[...][None]
        top = jnp.max(scores, axis=2, keepdims=True)
        weights = jnp.exp2(scores - top)
        total = jnp.sum(weights, axis=2, keepdims=True).reshape(size, 1)
        mixed = jnp.dot(
            weights.reshape(size, amount).astype(jnp.bfloat16),
            latent_ref[...],
            preferred_element_type=jnp.float32,
        )
        mixed = (mixed / total).astype(jnp.bfloat16)
        for head in range(first, first + group):
            result = jnp.dot(
                mixed[(head - first) * rows : (head - first + 1) * rows],
                value_ref[head],
                preferred_element_type=jnp.float32,
            )
            out_ref[:, head * VD : (head + 1) * VD] = result.astype(jnp.bfloat16)
        scores = later
    if hold:
        mix_copy.wait()


def attention(q_ext, bias, w_values, keys, gathered, held=()):
    head_count, rows, depth = q_ext.shape
    amount = bias.shape[1]
    out_shape = [jax.ShapeDtypeStruct((rows, head_count * VD), jnp.bfloat16)]
    if not gathered:
        out_shape.append(jax.ShapeDtypeStruct((depth, amount), jnp.bfloat16))
        out_shape.append(jax.ShapeDtypeStruct((amount, LAT), jnp.bfloat16))
    out_shape += [jax.ShapeDtypeStruct(array.shape, array.dtype) for array in held]
    return pl.pallas_call(
        functools.partial(attention_kernel, 0 if gathered else len(keys), len(held) > 0),
        out_shape=out_shape,
        in_specs=[IN_VMEM] * (3 + len(keys)) + [IN_HBM] * len(held),
        out_specs=[IN_VMEM] * len(out_shape),
        scratch_shapes=[pltpu.SemaphoreType.DMA] * len(held),
        compiler_params=params(16 if amount <= 1024 else 40),
        cost_estimate=SHORT,
    )(q_ext, bias, w_values, *keys, *held)


def product_kernel(count, n_x, after, weight_ref, *refs):
    piece_refs = refs[:count]
    sent_ref, kept_ref, rows_ref = refs[count + after :]
    rows = piece_refs[0].shape[0]
    columns = weight_ref.shape[1]
    for index, piece_ref in enumerate(piece_refs):
        rows_ref[index * rows : (index + 1) * rows, :] = piece_ref[...]
    is_first = lax.axis_index("head") % 2 == 0
    width = 256 if columns % 256 == 0 else columns
    for start in range(0, columns, width):
        span = slice(start, start + width)
        result = jnp.dot(rows_ref[...], weight_ref[:, span], preferred_element_type=jnp.float32)
        result = result.reshape(count, n_x, 2, rows // (2 * n_x), width)
        for x in range(n_x):
            first = result[:, x, 0].reshape(rows * count // (2 * n_x), width)
            second = result[:, x, 1].reshape(rows * count // (2 * n_x), width)
            sent_ref[x, :, span] = jnp.where(is_first, second, first).astype(jnp.bfloat16)
            kept_ref[x, :, span] = jnp.where(is_first, first, second)


def product(pieces, w_out, n_x, after):
    rows, depth = pieces[0].shape
    count = len(pieces)
    shape = (n_x, count * rows // (2 * n_x), w_out.shape[1])
    return pl.pallas_call(
        functools.partial(product_kernel, count, n_x, len(after)),
        out_shape=[jax.ShapeDtypeStruct(shape, jnp.bfloat16), jax.ShapeDtypeStruct(shape, jnp.float32)],
        in_specs=[IN_VMEM] * (1 + count) + [ANYWHERE] * len(after),
        out_specs=[IN_VMEM, IN_VMEM],
        scratch_shapes=[pltpu.VMEM((count * rows, depth), jnp.bfloat16)],
        compiler_params=params(16),
        cost_estimate=SHORT,
    )(w_out, *pieces, *after)


def place_kernel(n_ctx, ctx_ref, *refs):
    blocks, out_ref = refs[:-1], refs[-1]
    for offset in range(n_ctx):

        @pl.when(pl.program_id(0) == offset)
        def _():
            parts = [block[...].astype(jnp.float32) for block in blocks[offset::n_ctx]]
            out_ref[...] = jnp.concatenate(parts, axis=0).astype(jnp.bfloat16)


def place_columns(results, ctx, n_ctx):
    width = results[0][0].shape[1]
    total = sum(result[0].shape[0] for result in results)
    if width % 128:
        out = jnp.zeros((total, n_ctx * width), jnp.bfloat16)
        for offset in range(n_ctx):
            block = jnp.concatenate([result[offset] for result in results], axis=0)
            out = lax.dynamic_update_slice(out, block, (0, (ctx ^ offset) * width))
        return out
    blocks = [block for result in results for block in result]
    return pl.pallas_call(
        functools.partial(place_kernel, n_ctx),
        out_shape=jax.ShapeDtypeStruct((total, n_ctx * width), jnp.bfloat16),
        grid_spec=pltpu.PrefetchScalarGridSpec(
            num_scalar_prefetch=1,
            grid=(n_ctx,),
            in_specs=[IN_VMEM] * len(blocks),
            out_specs=pl.BlockSpec((total, width), lambda i, ctx_ref: (0, ctx_ref[0] ^ i)),
        ),
        compiler_params=params(4),
        cost_estimate=SHORT,
    )(jnp.full((1,), ctx, jnp.int32), *blocks)


def shards(n_ctx, n_head, queries, kv_rows, w_kv_up, w_out, stretch_order, prefix_len):
    query_rows = queries.shape[0]
    row_span = kv_rows.shape[0]
    cache_rows = row_span - query_rows
    half = row_span // 2
    columns = w_out.shape[1]
    n_x = n_head // 2
    pieces = chunk_rows(query_rows // n_head)
    ctx = lax.axis_index("ctx")
    head = lax.axis_index("head")
    x = head // 2

    with jax.named_scope("keys_over_ctx"):
        kv_t = kv_rows.T
        own_half = jnp.where(head % 2 == 0, kv_t[:, :half], kv_t[:, half:])
        halves = [exchange(own_half, "ctx", n_ctx, offset) for offset in range(1, n_ctx)]
    with jax.named_scope("load"):
        q_ext, bias, w_values, own_keys = load(
            queries, w_kv_up, kv_t, stretch_order, prefix_len, n_head, pieces, cache_rows
        )
    with jax.named_scope("keys_over_cores"):
        halves = [tie(array, [own_keys]) for array in halves]
        others = [exchange(array, "head", n_head, 1) for array in halves]
    with jax.named_scope("attention"):
        first, *keys = attention(q_ext[0], bias[0], w_values, [own_keys] + halves + others, False)
        second, held = attention(q_ext[1], bias[1], w_values, keys, True, [w_out])
        attended = [first, second]
        for chunk in range(2, len(pieces)):
            attended += attention(q_ext[chunk], bias[chunk], w_values, keys, True)
    with jax.named_scope("attended_over_ctx"):
        gathered = [
            gather_pieces(own, n_ctx, attended[chunk + 1 : chunk + 2])
            for chunk, own in enumerate(attended)
        ]
    results = []
    after = attended[1:]
    crossed = []
    for chunk, piece in enumerate(pieces):
        with jax.named_scope("out_product"):
            sent, kept = product(gathered[chunk], held, n_x, after)
        with jax.named_scope("sum_over_cores"):
            ahead = list(crossed)
            if chunk + 1 < len(pieces):
                ahead += [gathered[chunk + 1][1], gathered[chunk + 1][n_ctx // 2]]
            sent = tie(sent, ahead)
            summed = kept + exchange(sent, "head", n_head, 1).astype(jnp.float32)
            after = [summed]
        with jax.named_scope("sum_over_x"):
            total = lax.dynamic_index_in_dim(summed, x, 0, keepdims=False)
            crossed = []
            for offset in range(1, n_x):
                sent = lax.dynamic_index_in_dim(summed, x ^ offset, 0, keepdims=False)
                sent = exchange(sent.astype(jnp.bfloat16), "head", n_head, 2 * offset)
                crossed.append(sent)
                total = total + sent.astype(jnp.float32)
        with jax.named_scope("columns_over_ctx"):
            total = total.astype(jnp.bfloat16).reshape(n_ctx, piece, columns)
            blocks = [total[0]] + [exchange(total[d], "ctx", n_ctx, d) for d in range(1, n_ctx)]
        results.append(blocks)
    with jax.named_scope("output"):
        return place_columns(results, ctx, n_ctx)


def solution(mesh):
    placed = (
        P(("groups", "ctx"), "head"),
        P(("groups", "ctx"), None),
        P(None, "head"),
        P("head", "ctx"),
        P("groups"),
        P("groups"),
    )
    return jax.shard_map(
        functools.partial(shards, mesh.shape["ctx"], mesh.shape["head"]),
        mesh=mesh,
        in_specs=placed,
        out_specs=P(("groups", "ctx", "head"), None),
        check_vma=False,
    )
```

```python
import functools
import math

import jax
import jax.numpy as jnp
from jax import lax
from jax.experimental import pallas as pl
from jax.experimental.pallas import tpu as pltpu
from jax.sharding import PartitionSpec as P

LAT = 512
NOPE = 128
ROPE = 64
VD = 128
HEAD = NOPE + ROPE
PROJ = NOPE + VD
SUB_ROWS = 256
LOAD_LIMIT = 44
MASKED = -1e30
LOG2E = 1.4426950408889634
SCALE = LOG2E / math.sqrt(HEAD)
SHORT = pl.CostEstimate(flops=1024, bytes_accessed=1024, transcendentals=0)
IN_VMEM = pl.BlockSpec(memory_space=pltpu.VMEM)
IN_SMEM = pl.BlockSpec(memory_space=pltpu.SMEM)
IN_HBM = pl.BlockSpec(memory_space=pltpu.HBM)
ANYWHERE = pl.BlockSpec(memory_space=pl.ANY)


def chunk_rows(owned):
    return (owned // 2, owned // 2)


def params(mebibytes):
    return pltpu.CompilerParams(vmem_limit_bytes=mebibytes * 1024 * 1024)


def exchange(array, axis, size, bit):
    return lax.ppermute(array, axis, [(i, i ^ bit) for i in range(size)])


def tie_kernel(*refs):
    pass


def tie(array, after):
    if not after:
        return array
    return pl.pallas_call(
        tie_kernel,
        out_shape=jax.ShapeDtypeStruct(array.shape, array.dtype),
        in_specs=[ANYWHERE] * (1 + len(after)),
        out_specs=ANYWHERE,
        input_output_aliases={0: 0},
        compiler_params=params(1),
        cost_estimate=SHORT,
    )(array, *after)


def gather_pieces(own, size, after=()):
    pieces = {0: own}
    bit = size // 2
    while bit:
        pieces[bit] = exchange(own, "ctx", size, bit)
        bit //= 2
    bit = 1
    while bit < size:
        for offset in range(bit + 1, 2 * bit):
            if offset == bit + 1:
                pieces[bit] = tie(pieces[bit], after)
            pieces[offset] = exchange(pieces[bit], "ctx", size, offset ^ bit)
        bit *= 2
    return [pieces[offset] for offset in range(size)]


def load_kernel(owners, pieces, cache_rows, order_ref, prefix_ref, q_hbm, up_hbm, own_hbm, *refs):
    count = len(pieces)
    q_exts, biases, refs = refs[:count], refs[count : 2 * count], refs[2 * count :]
    value_ref, own_ref, q_ref, key_ref, sems, key_sems, value_sems = refs
    rows = q_ref.shape[0]
    head_count = key_ref.shape[0]
    q_copy = pltpu.make_async_copy(q_hbm, q_ref, sems.at[0])
    own_copy = pltpu.make_async_copy(own_hbm, own_ref, sems.at[1])
    q_copy.start()
    key_copies, value_copies = [], []
    for head in range(head_count):
        source = up_hbm.at[:, pl.ds(head * PROJ, NOPE)]
        key_copies.append(pltpu.make_async_copy(source, key_ref.at[head], key_sems.at[head]))
        source = up_hbm.at[:, pl.ds(head * PROJ + NOPE, VD)]
        value_copies.append(pltpu.make_async_copy(source, value_ref.at[head], value_sems.at[head]))
    for copy in key_copies + [own_copy] + value_copies:
        copy.start()
    start = 0
    for piece, bias_ref in zip(pieces, biases):
        visible_bias(
            order_ref, prefix_ref, bias_ref, rows, owners, start, own_hbm.shape[1], cache_rows
        )
        start += piece
    q_copy.wait()
    for head in range(head_count):
        nope = q_ref[:, head * HEAD : head * HEAD + NOPE]
        rope = q_ref[:, head * HEAD + NOPE : (head + 1) * HEAD].astype(jnp.float32) * SCALE
        key_copies[head].wait()
        absorbed = lax.dot_general(
            nope, key_ref[head], (((1,), (1,)), ((), ())), preferred_element_type=jnp.float32
        )
        absorbed = (absorbed * SCALE).reshape(owners, rows // owners, LAT)
        rope = rope.reshape(owners, rows // owners, ROPE)
        start = 0
        for piece, q_ext in zip(pieces, q_exts):
            part = absorbed[:, start : start + piece].reshape(owners * piece, LAT)
            q_ext[head, :, :LAT] = part.astype(jnp.bfloat16)
            part = rope[:, start : start + piece].reshape(owners * piece, ROPE)
            q_ext[head, :, LAT:] = part.astype(jnp.bfloat16)
            start += piece
    for copy in [own_copy] + value_copies:
        copy.wait()


def load(queries, w_kv_up, own_keys, stretch_order, prefix_len, owners, pieces, cache_rows):
    head_count = w_kv_up.shape[1] // PROJ
    amount = stretch_order.shape[0] * own_keys.shape[1]
    out_shape = [
        jax.ShapeDtypeStruct((head_count, owners * piece, LAT + ROPE), jnp.bfloat16)
        for piece in pieces
    ]
    out_shape += [jax.ShapeDtypeStruct((owners * piece, amount), jnp.float32) for piece in pieces]
    out_shape += [
        jax.ShapeDtypeStruct((head_count, LAT, VD), jnp.bfloat16),
        jax.ShapeDtypeStruct(own_keys.shape, jnp.bfloat16),
    ]
    out = pl.pallas_call(
        functools.partial(load_kernel, owners, pieces, cache_rows),
        out_shape=out_shape,
        in_specs=[IN_SMEM, IN_SMEM] + [IN_HBM] * 3,
        out_specs=[IN_VMEM] * len(out_shape),
        scratch_shapes=[
            pltpu.VMEM(queries.shape, jnp.bfloat16),
            pltpu.VMEM((head_count, LAT, NOPE), jnp.bfloat16),
            pltpu.SemaphoreType.DMA((2,)),
            pltpu.SemaphoreType.DMA((head_count,)),
            pltpu.SemaphoreType.DMA((head_count,)),
        ],
        compiler_params=params(LOAD_LIMIT),
        cost_estimate=SHORT,
    )(stretch_order, prefix_len, queries, w_kv_up, own_keys)
    count = len(pieces)
    return out[:count], out[count : 2 * count], *out[2 * count :]


def visible_bias(order_ref, prefix_ref, bias_ref, query_rows, owners, start, row_span, cache_rows):
    n_ctx = order_ref.shape[0]
    half = row_span // 2
    rows = bias_ref.shape[0]
    piece = rows // owners
    own = lax.axis_index("ctx")
    core = lax.axis_index("head") % 2
    blocks = [(0, 0), (0, 1)]
    blocks += [(offset, core) for offset in range(1, n_ctx)]
    blocks += [(offset, 1 - core) for offset in range(1, n_ctx)]
    row = lax.broadcasted_iota(jnp.int32, (rows, half), 0)
    column = lax.broadcasted_iota(jnp.int32, (rows, half), 1)
    within_own = row // piece * (query_rows // owners) + start + row % piece
    query_pos = order_ref[own] * query_rows + within_own
    for index, (offset, second) in enumerate(blocks):
        source = own ^ offset
        within = second * half + column
        cache_pos = jnp.where(
            source * cache_rows + within < prefix_ref[0], -1, n_ctx * query_rows
        )
        key_pos = order_ref[source] * query_rows + within - cache_rows
        first_seen = jnp.where(within < cache_rows, cache_pos, key_pos)
        bias = jnp.where(first_seen <= query_pos, 0.0, MASKED).astype(jnp.float32)
        bias_ref[:, index * half : (index + 1) * half] = bias


def attention_kernel(count, q_ref, bias_ref, value_ref, *refs):
    heads, rows, depth = q_ref.shape
    if count:
        piece_refs, (out_ref, keys_ref, latent_ref) = refs[:count], refs[count:]
        start = 0
        for piece_ref in piece_refs:
            width = piece_ref.shape[1]
            keys_ref[:, start : start + width] = piece_ref[...]
            latent_ref[start : start + width, :] = piece_ref[:LAT, :].T
            start += width
    else:
        keys_ref, latent_ref, out_ref = refs
    amount = keys_ref.shape[1]
    group = max(1, min(heads, SUB_ROWS // rows))
    size = group * rows

    def score(first):
        queries = q_ref[first : first + group].reshape(size, depth)
        return jnp.dot(queries, keys_ref[...], preferred_element_type=jnp.float32)

    scores = score(0)
    for first in range(0, heads, group):
        later = score(first + group) if first + group < heads else None
        scores = scores.reshape(group, rows, amount) + bias_ref[...][None]
        top = jnp.max(scores, axis=2, keepdims=True)
        weights = jnp.exp2(scores - top)
        total = jnp.sum(weights, axis=2, keepdims=True).reshape(size, 1)
        mixed = jnp.dot(
            weights.reshape(size, amount).astype(jnp.bfloat16),
            latent_ref[...],
            preferred_element_type=jnp.float32,
        )
        mixed = (mixed / total).astype(jnp.bfloat16)
        for head in range(first, first + group):
            result = jnp.dot(
                mixed[(head - first) * rows : (head - first + 1) * rows],
                value_ref[head],
                preferred_element_type=jnp.float32,
            )
            out_ref[:, head * VD : (head + 1) * VD] = result.astype(jnp.bfloat16)
        scores = later


def attention(q_ext, bias, w_values, keys, gathered):
    head_count, rows, depth = q_ext.shape
    amount = bias.shape[1]
    out_shape = [jax.ShapeDtypeStruct((rows, head_count * VD), jnp.bfloat16)]
    if not gathered:
        out_shape.append(jax.ShapeDtypeStruct((depth, amount), jnp.bfloat16))
        out_shape.append(jax.ShapeDtypeStruct((amount, LAT), jnp.bfloat16))
    return pl.pallas_call(
        functools.partial(attention_kernel, 0 if gathered else len(keys)),
        out_shape=out_shape,
        in_specs=[IN_VMEM] * (3 + len(keys)),
        out_specs=[IN_VMEM] * len(out_shape),
        compiler_params=params(16 if amount <= 1024 else 40),
        cost_estimate=SHORT,
    )(q_ext, bias, w_values, *keys)


def product_kernel(count, n_x, after, weight_ref, *refs):
    piece_refs = refs[:count]
    sent_ref, kept_ref, rows_ref = refs[count + after :]
    rows = piece_refs[0].shape[0]
    columns = weight_ref.shape[1]
    for index, piece_ref in enumerate(piece_refs):
        rows_ref[index * rows : (index + 1) * rows, :] = piece_ref[...]
    is_first = lax.axis_index("head") % 2 == 0
    width = 256 if columns % 256 == 0 else columns
    for start in range(0, columns, width):
        span = slice(start, start + width)
        result = jnp.dot(rows_ref[...], weight_ref[:, span], preferred_element_type=jnp.float32)
        result = result.reshape(count, n_x, 2, rows // (2 * n_x), width)
        for x in range(n_x):
            first = result[:, x, 0].reshape(rows * count // (2 * n_x), width)
            second = result[:, x, 1].reshape(rows * count // (2 * n_x), width)
            sent_ref[x, :, span] = jnp.where(is_first, second, first).astype(jnp.bfloat16)
            kept_ref[x, :, span] = jnp.where(is_first, first, second)


def product(pieces, w_out, n_x, after):
    rows, depth = pieces[0].shape
    count = len(pieces)
    shape = (n_x, count * rows // (2 * n_x), w_out.shape[1])
    return pl.pallas_call(
        functools.partial(product_kernel, count, n_x, len(after)),
        out_shape=[jax.ShapeDtypeStruct(shape, jnp.bfloat16), jax.ShapeDtypeStruct(shape, jnp.float32)],
        in_specs=[IN_VMEM] * (1 + count) + [ANYWHERE] * len(after),
        out_specs=[IN_VMEM, IN_VMEM],
        scratch_shapes=[pltpu.VMEM((count * rows, depth), jnp.bfloat16)],
        compiler_params=params(16),
        cost_estimate=SHORT,
    )(w_out, *pieces, *after)


def core_sum_kernel(n_x, kept_ref, received_ref, total_ref, *sent_refs):
    x = lax.axis_index("head") // 2
    for offset in range(n_x):
        summed = kept_ref[x ^ offset] + received_ref[x ^ offset].astype(jnp.float32)
        if offset:
            sent_refs[offset - 1][...] = summed.astype(jnp.bfloat16)
        else:
            total_ref[...] = summed


def core_sum(kept, received):
    n_x, rows, columns = kept.shape
    own = jax.ShapeDtypeStruct((rows, columns), jnp.float32)
    sent = jax.ShapeDtypeStruct((rows, columns), jnp.bfloat16)
    out = pl.pallas_call(
        functools.partial(core_sum_kernel, n_x),
        out_shape=[own] + [sent] * (n_x - 1),
        in_specs=[IN_VMEM, IN_VMEM],
        out_specs=[IN_VMEM] * n_x,
        compiler_params=params(4),
        cost_estimate=SHORT,
    )(kept, received)
    return out[0], out[1:]


def x_sum_kernel(count, total_ref, *refs):
    received, block_refs = refs[:count], refs[count:]
    total = total_ref[...]
    for ref in received:
        total = total + ref[...].astype(jnp.float32)
    rows = block_refs[0].shape[0]
    for index, block_ref in enumerate(block_refs):
        block_ref[...] = total[index * rows : (index + 1) * rows].astype(jnp.bfloat16)


def x_sum(total, received, n_ctx):
    rows, columns = total.shape
    block = jax.ShapeDtypeStruct((rows // n_ctx, columns), jnp.bfloat16)
    return pl.pallas_call(
        functools.partial(x_sum_kernel, len(received)),
        out_shape=[block] * n_ctx,
        in_specs=[IN_VMEM] * (1 + len(received)),
        out_specs=[IN_VMEM] * n_ctx,
        compiler_params=params(4),
        cost_estimate=SHORT,
    )(total, *received)


def place_kernel(n_ctx, *refs):
    blocks, out_ref = refs[:-1], refs[-1]
    ctx = lax.axis_index("ctx")
    width = blocks[0].shape[1]
    for offset in range(n_ctx):
        parts = [block[...].astype(jnp.float32) for block in blocks[offset::n_ctx]]
        column = pl.multiple_of((ctx ^ offset) * width, 128)
        out_ref[:, pl.ds(column, width)] = jnp.concatenate(parts, axis=0).astype(jnp.bfloat16)


def place_columns(results, n_ctx):
    width = results[0][0].shape[1]
    total = sum(result[0].shape[0] for result in results)
    if width % 128:
        ctx = lax.axis_index("ctx")
        out = jnp.zeros((total, n_ctx * width), jnp.bfloat16)
        for offset in range(n_ctx):
            block = jnp.concatenate([result[offset] for result in results], axis=0)
            out = lax.dynamic_update_slice(out, block, (0, (ctx ^ offset) * width))
        return out
    blocks = [block for result in results for block in result]
    return pl.pallas_call(
        functools.partial(place_kernel, n_ctx),
        grid=(1,),
        out_shape=jax.ShapeDtypeStruct((total, n_ctx * width), jnp.bfloat16),
        in_specs=[IN_VMEM] * len(blocks),
        out_specs=pl.BlockSpec((total, n_ctx * width), lambda i: (0, 0)),
        compiler_params=params(4),
        cost_estimate=SHORT,
    )(*blocks)


def shards(n_ctx, n_head, queries, kv_rows, w_kv_up, w_out, stretch_order, prefix_len):
    query_rows = queries.shape[0]
    row_span = kv_rows.shape[0]
    cache_rows = row_span - query_rows
    half = row_span // 2
    n_x = n_head // 2
    pieces = chunk_rows(query_rows // n_head)
    core = lax.axis_index("head") % 2

    with jax.named_scope("keys_over_ctx"):
        kv_t = kv_rows.T
        own_half = jnp.where(core == 0, kv_t[:, :half], kv_t[:, half:])
        halves = [exchange(own_half, "ctx", n_ctx, offset) for offset in range(1, n_ctx)]
    with jax.named_scope("load"):
        q_ext, bias, w_values, own_keys = load(
            queries, w_kv_up, kv_t, stretch_order, prefix_len, n_head, pieces, cache_rows
        )
    with jax.named_scope("keys_over_cores"):
        halves = [tie(array, [own_keys]) for array in halves]
        others = [exchange(array, "head", n_head, 1) for array in halves]
    with jax.named_scope("attention"):
        first, *keys = attention(q_ext[0], bias[0], w_values, [own_keys] + halves + others, False)
        attended = [first]
        for chunk in range(1, len(pieces)):
            attended += attention(q_ext[chunk], bias[chunk], w_values, keys, True)
    with jax.named_scope("attended_over_ctx"):
        gathered = [
            gather_pieces(own, n_ctx, attended[chunk + 1 : chunk + 2])
            for chunk, own in enumerate(attended)
        ]
    results = []
    after = attended[1:]
    crossed = []
    for chunk in range(len(pieces)):
        with jax.named_scope("out_product"):
            sent, kept = product(gathered[chunk], w_out, n_x, after)
        with jax.named_scope("sum_over_cores"):
            ahead = list(crossed)
            if chunk + 1 < len(pieces):
                ahead += [gathered[chunk + 1][1], gathered[chunk + 1][n_ctx // 2]]
            sent = tie(sent, ahead)
            total, sent = core_sum(kept, exchange(sent, "head", n_head, 1))
            after = [total]
        with jax.named_scope("sum_over_x"):
            crossed = [
                exchange(array, "head", n_head, 2 * offset) for offset, array in enumerate(sent, 1)
            ]
            total = x_sum(total, crossed, n_ctx)
        with jax.named_scope("columns_over_ctx"):
            blocks = [total[0]] + [exchange(total[d], "ctx", n_ctx, d) for d in range(1, n_ctx)]
        results.append(blocks)
    with jax.named_scope("output"):
        return place_columns(results, n_ctx)


def solution(mesh):
    placed = (
        P(("groups", "ctx"), "head"),
        P(("groups", "ctx"), None),
        P(None, "head"),
        P("head", "ctx"),
        P("groups"),
        P("groups"),
    )
    return jax.shard_map(
        functools.partial(shards, mesh.shape["ctx"], mesh.shape["head"]),
        mesh=mesh,
        in_specs=placed,
        out_specs=P(("groups", "ctx", "head"), None),
        check_vma=False,
    )
```

```python
import functools
import math

import jax
import jax.numpy as jnp
from jax import lax
from jax.experimental import pallas as pl
from jax.experimental.pallas import tpu as pltpu
from jax.sharding import PartitionSpec as P

LAT = 512
NOPE = 128
ROPE = 64
VD = 128
HEAD = NOPE + ROPE
PROJ = NOPE + VD
SUB_ROWS = 256
LOAD_LIMIT = 44
MASKED = -1e30
LOG2E = 1.4426950408889634
SCALE = LOG2E / math.sqrt(HEAD)
SHORT = pl.CostEstimate(flops=1024, bytes_accessed=1024, transcendentals=0)
IN_VMEM = pl.BlockSpec(memory_space=pltpu.VMEM)
IN_SMEM = pl.BlockSpec(memory_space=pltpu.SMEM)
IN_HBM = pl.BlockSpec(memory_space=pltpu.HBM)
ANYWHERE = pl.BlockSpec(memory_space=pl.ANY)


def chunk_rows(owned):
    return (owned // 2, owned // 2)


def params(mebibytes):
    return pltpu.CompilerParams(vmem_limit_bytes=mebibytes * 1024 * 1024)


def exchange(array, axis, size, bit):
    return lax.ppermute(array, axis, [(i, i ^ bit) for i in range(size)])


def tie_kernel(*refs):
    pass


def tie(array, after):
    if not after:
        return array
    return pl.pallas_call(
        tie_kernel,
        out_shape=jax.ShapeDtypeStruct(array.shape, array.dtype),
        in_specs=[ANYWHERE] * (1 + len(after)),
        out_specs=ANYWHERE,
        input_output_aliases={0: 0},
        compiler_params=params(1),
        cost_estimate=SHORT,
    )(array, *after)


def gather_pieces(own, size, after=()):
    pieces = {0: own}
    bit = size // 2
    while bit:
        pieces[bit] = exchange(own, "ctx", size, bit)
        bit //= 2
    bit = 1
    while bit < size:
        for offset in range(bit + 1, 2 * bit):
            if offset == bit + 1:
                pieces[bit] = tie(pieces[bit], after)
            pieces[offset] = exchange(pieces[bit], "ctx", size, offset ^ bit)
        bit *= 2
    return [pieces[offset] for offset in range(size)]


def load_kernel(owners, pieces, cache_rows, order_ref, prefix_ref, q_hbm, up_hbm, own_hbm, *refs):
    count = len(pieces)
    q_exts, biases, refs = refs[:count], refs[count : 2 * count], refs[2 * count :]
    value_ref, own_ref, q_ref, key_ref, sems, key_sems, value_sems = refs
    rows = q_ref.shape[0]
    head_count = key_ref.shape[0]
    q_copy = pltpu.make_async_copy(q_hbm, q_ref, sems.at[0])
    own_copy = pltpu.make_async_copy(own_hbm, own_ref, sems.at[1])
    q_copy.start()
    key_copies, value_copies = [], []
    for head in range(head_count):
        source = up_hbm.at[:, pl.ds(head * PROJ, NOPE)]
        key_copies.append(pltpu.make_async_copy(source, key_ref.at[head], key_sems.at[head]))
        source = up_hbm.at[:, pl.ds(head * PROJ + NOPE, VD)]
        value_copies.append(pltpu.make_async_copy(source, value_ref.at[head], value_sems.at[head]))
    for copy in key_copies + [own_copy] + value_copies:
        copy.start()
    start = 0
    for piece, bias_ref in zip(pieces, biases):
        visible_bias(
            order_ref, prefix_ref, bias_ref, rows, owners, start, own_hbm.shape[1], cache_rows
        )
        start += piece
    q_copy.wait()
    for head in range(head_count):
        nope = q_ref[:, head * HEAD : head * HEAD + NOPE]
        rope = q_ref[:, head * HEAD + NOPE : (head + 1) * HEAD].astype(jnp.float32) * SCALE
        key_copies[head].wait()
        absorbed = lax.dot_general(
            nope, key_ref[head], (((1,), (1,)), ((), ())), preferred_element_type=jnp.float32
        )
        absorbed = (absorbed * SCALE).reshape(owners, rows // owners, LAT)
        rope = rope.reshape(owners, rows // owners, ROPE)
        start = 0
        for piece, q_ext in zip(pieces, q_exts):
            part = absorbed[:, start : start + piece].reshape(owners * piece, LAT)
            q_ext[head, :, :LAT] = part.astype(jnp.bfloat16)
            part = rope[:, start : start + piece].reshape(owners * piece, ROPE)
            q_ext[head, :, LAT:] = part.astype(jnp.bfloat16)
            start += piece
    for copy in [own_copy] + value_copies:
        copy.wait()


def load(queries, w_kv_up, own_keys, stretch_order, prefix_len, owners, pieces, cache_rows):
    head_count = w_kv_up.shape[1] // PROJ
    amount = stretch_order.shape[0] * own_keys.shape[1]
    out_shape = [
        jax.ShapeDtypeStruct((head_count, owners * piece, LAT + ROPE), jnp.bfloat16)
        for piece in pieces
    ]
    out_shape += [jax.ShapeDtypeStruct((owners * piece, amount), jnp.float32) for piece in pieces]
    out_shape += [
        jax.ShapeDtypeStruct((head_count, LAT, VD), jnp.bfloat16),
        jax.ShapeDtypeStruct(own_keys.shape, jnp.bfloat16),
    ]
    out = pl.pallas_call(
        functools.partial(load_kernel, owners, pieces, cache_rows),
        out_shape=out_shape,
        in_specs=[IN_SMEM, IN_SMEM] + [IN_HBM] * 3,
        out_specs=[IN_VMEM] * len(out_shape),
        scratch_shapes=[
            pltpu.VMEM(queries.shape, jnp.bfloat16),
            pltpu.VMEM((head_count, LAT, NOPE), jnp.bfloat16),
            pltpu.SemaphoreType.DMA((2,)),
            pltpu.SemaphoreType.DMA((head_count,)),
            pltpu.SemaphoreType.DMA((head_count,)),
        ],
        compiler_params=params(LOAD_LIMIT),
        cost_estimate=SHORT,
    )(stretch_order, prefix_len, queries, w_kv_up, own_keys)
    count = len(pieces)
    return out[:count], out[count : 2 * count], *out[2 * count :]


def visible_bias(order_ref, prefix_ref, bias_ref, query_rows, owners, start, row_span, cache_rows):
    n_ctx = order_ref.shape[0]
    half = row_span // 2
    rows = bias_ref.shape[0]
    piece = rows // owners
    own = lax.axis_index("ctx")
    core = lax.axis_index("head") % 2
    blocks = [(0, 0), (0, 1)]
    blocks += [(offset, core) for offset in range(1, n_ctx)]
    blocks += [(offset, 1 - core) for offset in range(1, n_ctx)]
    row = lax.broadcasted_iota(jnp.int32, (rows, half), 0)
    column = lax.broadcasted_iota(jnp.int32, (rows, half), 1)
    within_own = row // piece * (query_rows // owners) + start + row % piece
    query_pos = order_ref[own] * query_rows + within_own
    for index, (offset, second) in enumerate(blocks):
        source = own ^ offset
        within = second * half + column
        cache_pos = jnp.where(
            source * cache_rows + within < prefix_ref[0], -1, n_ctx * query_rows
        )
        key_pos = order_ref[source] * query_rows + within - cache_rows
        first_seen = jnp.where(within < cache_rows, cache_pos, key_pos)
        bias = jnp.where(first_seen <= query_pos, 0.0, MASKED).astype(jnp.float32)
        bias_ref[:, index * half : (index + 1) * half] = bias


def attention_kernel(count, q_ref, bias_ref, value_ref, *refs):
    heads, rows, depth = q_ref.shape
    if count:
        piece_refs, (out_ref, keys_ref, latent_ref) = refs[:count], refs[count:]
        start = 0
        for piece_ref in piece_refs:
            width = piece_ref.shape[1]
            keys_ref[:, start : start + width] = piece_ref[...]
            latent_ref[start : start + width, :] = piece_ref[:LAT, :].T
            start += width
    else:
        keys_ref, latent_ref, out_ref = refs
    amount = keys_ref.shape[1]
    group = max(1, min(heads, SUB_ROWS // rows))
    size = group * rows

    def score(first):
        queries = q_ref[first : first + group].reshape(size, depth)
        return jnp.dot(queries, keys_ref[...], preferred_element_type=jnp.float32)

    scores = score(0)
    for first in range(0, heads, group):
        later = score(first + group) if first + group < heads else None
        scores = scores.reshape(group, rows, amount) + bias_ref[...][None]
        top = jnp.max(scores, axis=2, keepdims=True)
        weights = jnp.exp2(scores - top)
        total = jnp.sum(weights, axis=2, keepdims=True).reshape(size, 1)
        mixed = jnp.dot(
            weights.reshape(size, amount).astype(jnp.bfloat16),
            latent_ref[...],
            preferred_element_type=jnp.float32,
        )
        mixed = (mixed / total).astype(jnp.bfloat16)
        for head in range(first, first + group):
            result = jnp.dot(
                mixed[(head - first) * rows : (head - first + 1) * rows],
                value_ref[head],
                preferred_element_type=jnp.float32,
            )
            out_ref[:, head * VD : (head + 1) * VD] = result.astype(jnp.bfloat16)
        scores = later


def attention(q_ext, bias, w_values, keys, gathered):
    head_count, rows, depth = q_ext.shape
    amount = bias.shape[1]
    out_shape = [jax.ShapeDtypeStruct((rows, head_count * VD), jnp.bfloat16)]
    if not gathered:
        out_shape.append(jax.ShapeDtypeStruct((depth, amount), jnp.bfloat16))
        out_shape.append(jax.ShapeDtypeStruct((amount, LAT), jnp.bfloat16))
    return pl.pallas_call(
        functools.partial(attention_kernel, 0 if gathered else len(keys)),
        out_shape=out_shape,
        in_specs=[IN_VMEM] * (3 + len(keys)),
        out_specs=[IN_VMEM] * len(out_shape),
        compiler_params=params(16 if amount <= 1024 else 40),
        cost_estimate=SHORT,
    )(q_ext, bias, w_values, *keys)


def product_kernel(count, n_x, after, weight_ref, *refs):
    piece_refs = refs[:count]
    sent_ref, kept_ref, rows_ref = refs[count + after :]
    rows = piece_refs[0].shape[0]
    columns = weight_ref.shape[1]
    for index, piece_ref in enumerate(piece_refs):
        rows_ref[index * rows : (index + 1) * rows, :] = piece_ref[...]
    is_first = lax.axis_index("head") % 2 == 0
    width = 256 if columns % 256 == 0 else columns
    for start in range(0, columns, width):
        span = slice(start, start + width)
        result = jnp.dot(rows_ref[...], weight_ref[:, span], preferred_element_type=jnp.float32)
        result = result.reshape(count, n_x, 2, rows // (2 * n_x), width)
        for x in range(n_x):
            first = result[:, x, 0].reshape(rows * count // (2 * n_x), width)
            second = result[:, x, 1].reshape(rows * count // (2 * n_x), width)
            sent_ref[x, :, span] = jnp.where(is_first, second, first).astype(jnp.bfloat16)
            kept_ref[x, :, span] = jnp.where(is_first, first, second)


def product(pieces, w_out, n_x, after):
    rows, depth = pieces[0].shape
    count = len(pieces)
    shape = (n_x, count * rows // (2 * n_x), w_out.shape[1])
    return pl.pallas_call(
        functools.partial(product_kernel, count, n_x, len(after)),
        out_shape=[jax.ShapeDtypeStruct(shape, jnp.bfloat16), jax.ShapeDtypeStruct(shape, jnp.float32)],
        in_specs=[IN_VMEM] * (1 + count) + [ANYWHERE] * len(after),
        out_specs=[IN_VMEM, IN_VMEM],
        scratch_shapes=[pltpu.VMEM((count * rows, depth), jnp.bfloat16)],
        compiler_params=params(16),
        cost_estimate=SHORT,
    )(w_out, *pieces, *after)


def core_sum_kernel(n_x, kept_ref, received_ref, total_ref, *sent_refs):
    x = lax.axis_index("head") // 2
    for offset in range(n_x):
        summed = kept_ref[x ^ offset] + received_ref[x ^ offset].astype(jnp.float32)
        if offset:
            sent_refs[offset - 1][...] = summed.astype(jnp.bfloat16)
        else:
            total_ref[...] = summed


def core_sum(kept, received):
    n_x, rows, columns = kept.shape
    own = jax.ShapeDtypeStruct((rows, columns), jnp.float32)
    sent = jax.ShapeDtypeStruct((rows, columns), jnp.bfloat16)
    out = pl.pallas_call(
        functools.partial(core_sum_kernel, n_x),
        out_shape=[own] + [sent] * (n_x - 1),
        in_specs=[IN_VMEM, IN_VMEM],
        out_specs=[IN_VMEM] * n_x,
        compiler_params=params(4),
        cost_estimate=SHORT,
    )(kept, received)
    return out[0], out[1:]


def x_sum_kernel(total_ref, *refs):
    received, out_ref = refs[:-1], refs[-1]
    total = total_ref[...]
    for ref in received:
        total = total + ref[...].astype(jnp.float32)
    n_ctx, rows, columns = out_ref.shape
    ctx = lax.axis_index("ctx")
    for offset in range(n_ctx):
        part = total[offset * rows : (offset + 1) * rows]
        out_ref[ctx ^ offset] = part.astype(jnp.bfloat16)


def x_sum(total, received, n_ctx):
    rows, columns = total.shape
    return pl.pallas_call(
        x_sum_kernel,
        out_shape=jax.ShapeDtypeStruct((n_ctx, rows // n_ctx, columns), jnp.bfloat16),
        in_specs=[IN_VMEM] * (1 + len(received)),
        out_specs=IN_VMEM,
        compiler_params=params(4),
        cost_estimate=SHORT,
    )(total, *received)


def place_kernel(*refs):
    parts, out_ref = refs[:-1], refs[-1]
    width = parts[0].shape[2]
    for index in range(parts[0].shape[0]):
        rows = jnp.concatenate([part[index].astype(jnp.float32) for part in parts], axis=0)
        out_ref[:, index * width : (index + 1) * width] = rows.astype(jnp.bfloat16)


def place_columns(parts):
    n_ctx, rows, width = parts[0].shape
    shape = (rows * len(parts), n_ctx * width)
    return pl.pallas_call(
        place_kernel,
        grid=(1,),
        out_shape=jax.ShapeDtypeStruct(shape, jnp.bfloat16),
        in_specs=[IN_VMEM] * len(parts),
        out_specs=pl.BlockSpec(shape, lambda i: (0, 0)),
        compiler_params=params(4),
        cost_estimate=SHORT,
    )(*parts)


def shards(n_ctx, n_head, queries, kv_rows, w_kv_up, w_out, stretch_order, prefix_len):
    query_rows = queries.shape[0]
    row_span = kv_rows.shape[0]
    cache_rows = row_span - query_rows
    half = row_span // 2
    n_x = n_head // 2
    pieces = chunk_rows(query_rows // n_head)
    core = lax.axis_index("head") % 2

    with jax.named_scope("keys_over_ctx"):
        kv_t = kv_rows.T
        own_half = jnp.where(core == 0, kv_t[:, :half], kv_t[:, half:])
        halves = [exchange(own_half, "ctx", n_ctx, offset) for offset in range(1, n_ctx)]
    with jax.named_scope("load"):
        q_ext, bias, w_values, own_keys = load(
            queries, w_kv_up, kv_t, stretch_order, prefix_len, n_head, pieces, cache_rows
        )
    with jax.named_scope("keys_over_cores"):
        halves = [tie(array, [own_keys]) for array in halves]
        others = [exchange(array, "head", n_head, 1) for array in halves]
    with jax.named_scope("attention"):
        first, *keys = attention(q_ext[0], bias[0], w_values, [own_keys] + halves + others, False)
        attended = [first]
        for chunk in range(1, len(pieces)):
            attended += attention(q_ext[chunk], bias[chunk], w_values, keys, True)
    with jax.named_scope("attended_over_ctx"):
        gathered = [
            gather_pieces(own, n_ctx, attended[chunk + 1 : chunk + 2])
            for chunk, own in enumerate(attended)
        ]
    results = []
    after = attended[1:]
    crossed = []
    for chunk in range(len(pieces)):
        with jax.named_scope("out_product"):
            sent, kept = product(gathered[chunk], w_out, n_x, after)
        with jax.named_scope("sum_over_cores"):
            ahead = list(crossed)
            if chunk + 1 < len(pieces):
                ahead += [gathered[chunk + 1][1], gathered[chunk + 1][n_ctx // 2]]
            sent = tie(sent, ahead)
            total, sent = core_sum(kept, exchange(sent, "head", n_head, 1))
            after = [total]
        with jax.named_scope("sum_over_x"):
            crossed = [
                exchange(array, "head", n_head, 2 * offset) for offset, array in enumerate(sent, 1)
            ]
            total = x_sum(total, crossed, n_ctx)
        with jax.named_scope("columns_over_ctx"):
            results.append(lax.all_to_all(total, "ctx", 0, 0))
    with jax.named_scope("output"):
        return place_columns(results)


def solution(mesh):
    placed = (
        P(("groups", "ctx"), "head"),
        P(("groups", "ctx"), None),
        P(None, "head"),
        P("head", "ctx"),
        P("groups"),
        P("groups"),
    )
    return jax.shard_map(
        functools.partial(shards, mesh.shape["ctx"], mesh.shape["head"]),
        mesh=mesh,
        in_specs=placed,
        out_specs=P(("groups", "ctx", "head"), None),
        check_vma=False,
    )
```

```python
import functools
import math

import jax
import jax.numpy as jnp
from jax import lax
from jax.experimental import pallas as pl
from jax.experimental.pallas import tpu as pltpu
from jax.sharding import PartitionSpec as P

LAT = 512
NOPE = 128
ROPE = 64
VD = 128
HEAD = NOPE + ROPE
PROJ = NOPE + VD
SUB_ROWS = 256
LOAD_LIMIT = 44
MASKED = -1e30
LOG2E = 1.4426950408889634
SCALE = LOG2E / math.sqrt(HEAD)
SHORT = pl.CostEstimate(flops=1024, bytes_accessed=1024, transcendentals=0)
IN_VMEM = pl.BlockSpec(memory_space=pltpu.VMEM)
IN_SMEM = pl.BlockSpec(memory_space=pltpu.SMEM)
IN_HBM = pl.BlockSpec(memory_space=pltpu.HBM)
ANYWHERE = pl.BlockSpec(memory_space=pl.ANY)


def chunk_rows(owned):
    return (owned // 2, owned // 2)


def params(mebibytes):
    return pltpu.CompilerParams(vmem_limit_bytes=mebibytes * 1024 * 1024)


def exchange(array, axis, size, bit):
    return lax.ppermute(array, axis, [(i, i ^ bit) for i in range(size)])


def tie_kernel(*refs):
    pass


def tie(array, after):
    if not after:
        return array
    return pl.pallas_call(
        tie_kernel,
        out_shape=jax.ShapeDtypeStruct(array.shape, array.dtype),
        in_specs=[ANYWHERE] * (1 + len(after)),
        out_specs=ANYWHERE,
        input_output_aliases={0: 0},
        compiler_params=params(1),
        cost_estimate=SHORT,
    )(array, *after)


def gather_pieces(own, size, after=()):
    pieces = {0: own}
    bit = size // 2
    while bit:
        pieces[bit] = exchange(own, "ctx", size, bit)
        bit //= 2
    bit = 1
    while bit < size:
        for offset in range(bit + 1, 2 * bit):
            if offset == bit + 1:
                pieces[bit] = tie(pieces[bit], after)
            pieces[offset] = exchange(pieces[bit], "ctx", size, offset ^ bit)
        bit *= 2
    return [pieces[offset] for offset in range(size)]


def load_kernel(owners, pieces, cache_rows, order_ref, prefix_ref, q_hbm, up_hbm, own_hbm, *refs):
    count = len(pieces)
    q_exts, biases, refs = refs[:count], refs[count : 2 * count], refs[2 * count :]
    value_ref, own_ref, q_ref, key_ref, sems, key_sems, value_sems = refs
    rows = q_ref.shape[0]
    head_count = key_ref.shape[0]
    q_copy = pltpu.make_async_copy(q_hbm, q_ref, sems.at[0])
    own_copy = pltpu.make_async_copy(own_hbm, own_ref, sems.at[1])
    q_copy.start()
    key_copies, value_copies = [], []
    for head in range(head_count):
        source = up_hbm.at[:, pl.ds(head * PROJ, NOPE)]
        key_copies.append(pltpu.make_async_copy(source, key_ref.at[head], key_sems.at[head]))
        source = up_hbm.at[:, pl.ds(head * PROJ + NOPE, VD)]
        value_copies.append(pltpu.make_async_copy(source, value_ref.at[head], value_sems.at[head]))
    for copy in key_copies + [own_copy] + value_copies:
        copy.start()
    start = 0
    for piece, bias_ref in zip(pieces, biases):
        visible_bias(
            order_ref, prefix_ref, bias_ref, rows, owners, start, own_hbm.shape[1], cache_rows
        )
        start += piece
    q_copy.wait()
    for head in range(head_count):
        nope = q_ref[:, head * HEAD : head * HEAD + NOPE]
        rope = q_ref[:, head * HEAD + NOPE : (head + 1) * HEAD].astype(jnp.float32) * SCALE
        key_copies[head].wait()
        absorbed = lax.dot_general(
            nope, key_ref[head], (((1,), (1,)), ((), ())), preferred_element_type=jnp.float32
        )
        absorbed = (absorbed * SCALE).reshape(owners, rows // owners, LAT)
        rope = rope.reshape(owners, rows // owners, ROPE)
        start = 0
        for piece, q_ext in zip(pieces, q_exts):
            part = absorbed[:, start : start + piece].reshape(owners * piece, LAT)
            q_ext[head, :, :LAT] = part.astype(jnp.bfloat16)
            part = rope[:, start : start + piece].reshape(owners * piece, ROPE)
            q_ext[head, :, LAT:] = part.astype(jnp.bfloat16)
            start += piece
    for copy in [own_copy] + value_copies:
        copy.wait()


def load(queries, w_kv_up, own_keys, stretch_order, prefix_len, owners, pieces, cache_rows):
    head_count = w_kv_up.shape[1] // PROJ
    amount = stretch_order.shape[0] * own_keys.shape[1]
    out_shape = [
        jax.ShapeDtypeStruct((head_count, owners * piece, LAT + ROPE), jnp.bfloat16)
        for piece in pieces
    ]
    out_shape += [jax.ShapeDtypeStruct((owners * piece, amount), jnp.float32) for piece in pieces]
    out_shape += [
        jax.ShapeDtypeStruct((head_count, LAT, VD), jnp.bfloat16),
        jax.ShapeDtypeStruct(own_keys.shape, jnp.bfloat16),
    ]
    out = pl.pallas_call(
        functools.partial(load_kernel, owners, pieces, cache_rows),
        out_shape=out_shape,
        in_specs=[IN_SMEM, IN_SMEM] + [IN_HBM] * 3,
        out_specs=[IN_VMEM] * len(out_shape),
        scratch_shapes=[
            pltpu.VMEM(queries.shape, jnp.bfloat16),
            pltpu.VMEM((head_count, LAT, NOPE), jnp.bfloat16),
            pltpu.SemaphoreType.DMA((2,)),
            pltpu.SemaphoreType.DMA((head_count,)),
            pltpu.SemaphoreType.DMA((head_count,)),
        ],
        compiler_params=params(LOAD_LIMIT),
        cost_estimate=SHORT,
    )(stretch_order, prefix_len, queries, w_kv_up, own_keys)
    count = len(pieces)
    return out[:count], out[count : 2 * count], *out[2 * count :]


def visible_bias(order_ref, prefix_ref, bias_ref, query_rows, owners, start, row_span, cache_rows):
    n_ctx = order_ref.shape[0]
    half = row_span // 2
    rows = bias_ref.shape[0]
    piece = rows // owners
    own = lax.axis_index("ctx")
    core = lax.axis_index("head") % 2
    blocks = [(0, 0), (0, 1)]
    blocks += [(offset, core) for offset in range(1, n_ctx)]
    blocks += [(offset, 1 - core) for offset in range(1, n_ctx)]
    row = lax.broadcasted_iota(jnp.int32, (rows, half), 0)
    column = lax.broadcasted_iota(jnp.int32, (rows, half), 1)
    within_own = row // piece * (query_rows // owners) + start + row % piece
    query_pos = order_ref[own] * query_rows + within_own
    for index, (offset, second) in enumerate(blocks):
        source = own ^ offset
        within = second * half + column
        cache_pos = jnp.where(
            source * cache_rows + within < prefix_ref[0], -1, n_ctx * query_rows
        )
        key_pos = order_ref[source] * query_rows + within - cache_rows
        first_seen = jnp.where(within < cache_rows, cache_pos, key_pos)
        bias = jnp.where(first_seen <= query_pos, 0.0, MASKED).astype(jnp.float32)
        bias_ref[:, index * half : (index + 1) * half] = bias


def attention_kernel(count, q_ref, bias_ref, value_ref, *refs):
    heads, rows, depth = q_ref.shape
    if count:
        piece_refs, (out_ref, keys_ref, latent_ref) = refs[:count], refs[count:]
        start = 0
        for piece_ref in piece_refs:
            width = piece_ref.shape[1]
            keys_ref[:, start : start + width] = piece_ref[...]
            latent_ref[start : start + width, :] = piece_ref[:LAT, :].T
            start += width
    else:
        keys_ref, latent_ref, out_ref = refs
    amount = keys_ref.shape[1]
    group = max(1, min(heads, SUB_ROWS // rows))
    size = group * rows

    def score(first):
        queries = q_ref[first : first + group].reshape(size, depth)
        return jnp.dot(queries, keys_ref[...], preferred_element_type=jnp.float32)

    scores = score(0)
    for first in range(0, heads, group):
        later = score(first + group) if first + group < heads else None
        scores = scores.reshape(group, rows, amount) + bias_ref[...][None]
        top = jnp.max(scores, axis=2, keepdims=True)
        weights = jnp.exp2(scores - top)
        total = jnp.sum(weights, axis=2, keepdims=True).reshape(size, 1)
        mixed = jnp.dot(
            weights.reshape(size, amount).astype(jnp.bfloat16),
            latent_ref[...],
            preferred_element_type=jnp.float32,
        )
        mixed = (mixed / total).astype(jnp.bfloat16)
        for head in range(first, first + group):
            result = jnp.dot(
                mixed[(head - first) * rows : (head - first + 1) * rows],
                value_ref[head],
                preferred_element_type=jnp.float32,
            )
            out_ref[:, head * VD : (head + 1) * VD] = result.astype(jnp.bfloat16)
        scores = later


def attention(q_ext, bias, w_values, keys, gathered):
    head_count, rows, depth = q_ext.shape
    amount = bias.shape[1]
    out_shape = [jax.ShapeDtypeStruct((rows, head_count * VD), jnp.bfloat16)]
    if not gathered:
        out_shape.append(jax.ShapeDtypeStruct((depth, amount), jnp.bfloat16))
        out_shape.append(jax.ShapeDtypeStruct((amount, LAT), jnp.bfloat16))
    return pl.pallas_call(
        functools.partial(attention_kernel, 0 if gathered else len(keys)),
        out_shape=out_shape,
        in_specs=[IN_VMEM] * (3 + len(keys)),
        out_specs=[IN_VMEM] * len(out_shape),
        compiler_params=params(16 if amount <= 1024 else 40),
        cost_estimate=SHORT,
    )(q_ext, bias, w_values, *keys)


def product_kernel(count, n_x, after, weight_ref, *refs):
    piece_refs = refs[:count]
    sent_ref, kept_ref, rows_ref = refs[count + after :]
    rows = piece_refs[0].shape[0]
    columns = weight_ref.shape[1]
    for index, piece_ref in enumerate(piece_refs):
        rows_ref[index * rows : (index + 1) * rows, :] = piece_ref[...]
    is_first = lax.axis_index("head") % 2 == 0
    width = 256 if columns % 256 == 0 else columns
    for start in range(0, columns, width):
        span = slice(start, start + width)
        result = jnp.dot(rows_ref[...], weight_ref[:, span], preferred_element_type=jnp.float32)
        result = result.reshape(count, n_x, 2, rows // (2 * n_x), width)
        for x in range(n_x):
            first = result[:, x, 0].reshape(rows * count // (2 * n_x), width)
            second = result[:, x, 1].reshape(rows * count // (2 * n_x), width)
            sent_ref[x, :, span] = jnp.where(is_first, second, first).astype(jnp.bfloat16)
            kept_ref[x, :, span] = jnp.where(is_first, first, second)


def product(pieces, w_out, n_x, after):
    rows, depth = pieces[0].shape
    count = len(pieces)
    shape = (n_x, count * rows // (2 * n_x), w_out.shape[1])
    return pl.pallas_call(
        functools.partial(product_kernel, count, n_x, len(after)),
        out_shape=[jax.ShapeDtypeStruct(shape, jnp.bfloat16), jax.ShapeDtypeStruct(shape, jnp.float32)],
        in_specs=[IN_VMEM] * (1 + count) + [ANYWHERE] * len(after),
        out_specs=[IN_VMEM, IN_VMEM],
        scratch_shapes=[pltpu.VMEM((count * rows, depth), jnp.bfloat16)],
        compiler_params=params(16),
        cost_estimate=SHORT,
    )(w_out, *pieces, *after)


def core_sum_kernel(n_x, kept_ref, received_ref, total_ref, *sent_refs):
    x = lax.axis_index("head") // 2
    for offset in range(n_x):
        summed = kept_ref[x ^ offset] + received_ref[x ^ offset].astype(jnp.float32)
        if offset:
            sent_refs[offset - 1][...] = summed.astype(jnp.bfloat16)
        else:
            total_ref[...] = summed


def core_sum(kept, received):
    n_x, rows, columns = kept.shape
    own = jax.ShapeDtypeStruct((rows, columns), jnp.float32)
    sent = jax.ShapeDtypeStruct((rows, columns), jnp.bfloat16)
    out = pl.pallas_call(
        functools.partial(core_sum_kernel, n_x),
        out_shape=[own] + [sent] * (n_x - 1),
        in_specs=[IN_VMEM, IN_VMEM],
        out_specs=[IN_VMEM] * n_x,
        compiler_params=params(4),
        cost_estimate=SHORT,
    )(kept, received)
    return out[0], out[1:]


def x_sum_kernel(count, total_ref, *refs):
    received, block_refs = refs[:count], refs[count:]
    total = total_ref[...]
    for ref in received:
        total = total + ref[...].astype(jnp.float32)
    rows = block_refs[0].shape[0]
    for index, block_ref in enumerate(block_refs):
        block_ref[...] = total[index * rows : (index + 1) * rows].astype(jnp.bfloat16)


def x_sum(total, received, count):
    rows, columns = total.shape
    block = jax.ShapeDtypeStruct((rows // count, columns), jnp.bfloat16)
    return pl.pallas_call(
        functools.partial(x_sum_kernel, len(received)),
        out_shape=[block] * count,
        in_specs=[IN_VMEM] * (1 + len(received)),
        out_specs=[IN_VMEM] * count,
        compiler_params=params(4),
        cost_estimate=SHORT,
    )(total, *received)


def place_kernel(n_ctx, *refs):
    blocks, out_ref = refs[:-1], refs[-1]
    ctx = lax.axis_index("ctx")
    width = blocks[0].shape[1]
    for offset in range(n_ctx):
        parts = [block[...].astype(jnp.float32) for block in blocks[offset::n_ctx]]
        column = pl.multiple_of((ctx ^ offset) * width, 128)
        out_ref[:, pl.ds(column, width)] = jnp.concatenate(parts, axis=0).astype(jnp.bfloat16)


def place_columns(results, n_ctx):
    width = results[0][0].shape[1]
    total = sum(result[0].shape[0] for result in results)
    if width % 128:
        ctx = lax.axis_index("ctx")
        out = jnp.zeros((total, n_ctx * width), jnp.bfloat16)
        for offset in range(n_ctx):
            block = jnp.concatenate([result[offset] for result in results], axis=0)
            out = lax.dynamic_update_slice(out, block, (0, (ctx ^ offset) * width))
        return out
    blocks = [block for result in results for block in result]
    return pl.pallas_call(
        functools.partial(place_kernel, n_ctx),
        grid=(1,),
        out_shape=jax.ShapeDtypeStruct((total, n_ctx * width), jnp.bfloat16),
        in_specs=[IN_VMEM] * len(blocks),
        out_specs=pl.BlockSpec((total, n_ctx * width), lambda i: (0, 0)),
        compiler_params=params(4),
        cost_estimate=SHORT,
    )(*blocks)


def shards(n_ctx, n_head, queries, kv_rows, w_kv_up, w_out, stretch_order, prefix_len):
    query_rows = queries.shape[0]
    row_span = kv_rows.shape[0]
    cache_rows = row_span - query_rows
    half = row_span // 2
    n_x = n_head // 2
    pieces = chunk_rows(query_rows // n_head)
    core = lax.axis_index("head") % 2

    with jax.named_scope("keys_over_ctx"):
        kv_t = kv_rows.T
        own_half = jnp.where(core == 0, kv_t[:, :half], kv_t[:, half:])
        halves = [exchange(own_half, "ctx", n_ctx, offset) for offset in range(1, n_ctx)]
    with jax.named_scope("load"):
        q_ext, bias, w_values, own_keys = load(
            queries, w_kv_up, kv_t, stretch_order, prefix_len, n_head, pieces, cache_rows
        )
    with jax.named_scope("keys_over_cores"):
        halves = [tie(array, [own_keys]) for array in halves]
        others = [exchange(array, "head", n_head, 1) for array in halves]
    with jax.named_scope("attention"):
        first, *keys = attention(q_ext[0], bias[0], w_values, [own_keys] + halves + others, False)
        attended = [first]
        for chunk in range(1, len(pieces)):
            attended += attention(q_ext[chunk], bias[chunk], w_values, keys, True)
    with jax.named_scope("attended_over_ctx"):
        gathered = [
            gather_pieces(own, n_ctx, attended[chunk + 1 : chunk + 2])
            for chunk, own in enumerate(attended)
        ]
    near = [0] + [1 << bit for bit in range(n_ctx.bit_length() - 1)]
    far = [offset for offset in range(n_ctx) if offset not in near]
    last = len(pieces) - 1
    units = [(chunk, list(range(n_ctx))) for chunk in range(last)] + [(last, near), (last, far)]
    results = [{} for chunk in pieces]
    after = attended[1:]
    crossed = []
    for unit, (chunk, offsets) in enumerate(units):
        with jax.named_scope("out_product"):
            first = after if unit == 0 else []
            sent, kept = product([gathered[chunk][d] for d in offsets], w_out, n_x, first)
        with jax.named_scope("sum_over_cores"):
            if chunk < last:
                sent = tie(sent, [gathered[chunk + 1][1], gathered[chunk + 1][n_ctx // 2]])
            elif offsets is far:
                sent = tie(sent, [*crossed[0], *after])
            total, sent = core_sum(kept, exchange(sent, "head", n_head, 1))
            after = [total]
        with jax.named_scope("sum_over_x"):
            if offsets is far:
                sent = [tie(array, crossed[-1]) for array in sent]
            crossed.append(
                [exchange(array, "head", n_head, 2 * d) for d, array in enumerate(sent, 1)]
            )
            blocks = x_sum(total, crossed[-1], len(offsets))
        with jax.named_scope("columns_over_ctx"):
            for d, block in zip(offsets, blocks):
                results[chunk][d] = exchange(block, "ctx", n_ctx, d) if d else block
    results = [[result[d] for d in range(n_ctx)] for result in results]
    with jax.named_scope("output"):
        return place_columns(results, n_ctx)


def solution(mesh):
    placed = (
        P(("groups", "ctx"), "head"),
        P(("groups", "ctx"), None),
        P(None, "head"),
        P("head", "ctx"),
        P("groups"),
        P("groups"),
    )
    return jax.shard_map(
        functools.partial(shards, mesh.shape["ctx"], mesh.shape["head"]),
        mesh=mesh,
        in_specs=placed,
        out_specs=P(("groups", "ctx", "head"), None),
        check_vma=False,
    )
```

```python
import functools
import math

import jax
import jax.numpy as jnp
from jax import lax
from jax.experimental import pallas as pl
from jax.experimental.pallas import tpu as pltpu
from jax.sharding import PartitionSpec as P

LAT = 512
NOPE = 128
ROPE = 64
VD = 128
HEAD = NOPE + ROPE
PROJ = NOPE + VD
SUB_ROWS = 256
LOAD_LIMIT = 44
MASKED = -1e30
LOG2E = 1.4426950408889634
SCALE = LOG2E / math.sqrt(HEAD)
SHORT = pl.CostEstimate(flops=1024, bytes_accessed=1024, transcendentals=0)
IN_VMEM = pl.BlockSpec(memory_space=pltpu.VMEM)
IN_SMEM = pl.BlockSpec(memory_space=pltpu.SMEM)
IN_HBM = pl.BlockSpec(memory_space=pltpu.HBM)
ANYWHERE = pl.BlockSpec(memory_space=pl.ANY)


def chunk_rows(owned):
    return (owned // 2, owned // 2)


def params(mebibytes):
    return pltpu.CompilerParams(vmem_limit_bytes=mebibytes * 1024 * 1024)


def exchange(array, axis, size, bit):
    return lax.ppermute(array, axis, [(i, i ^ bit) for i in range(size)])


def tie_kernel(*refs):
    pass


def tie(array, after):
    if not after:
        return array
    return pl.pallas_call(
        tie_kernel,
        out_shape=jax.ShapeDtypeStruct(array.shape, array.dtype),
        in_specs=[ANYWHERE] * (1 + len(after)),
        out_specs=ANYWHERE,
        input_output_aliases={0: 0},
        compiler_params=params(1),
        cost_estimate=SHORT,
    )(array, *after)


def gather_pieces(own, size, after=()):
    pieces = {0: own}
    bit = size // 2
    while bit:
        pieces[bit] = exchange(own, "ctx", size, bit)
        bit //= 2
    bit = 1
    while bit < size:
        for offset in range(bit + 1, 2 * bit):
            if offset == bit + 1:
                pieces[bit] = tie(pieces[bit], after)
            pieces[offset] = exchange(pieces[bit], "ctx", size, offset ^ bit)
        bit *= 2
    return [pieces[offset] for offset in range(size)]


def load_kernel(owners, pieces, cache_rows, order_ref, prefix_ref, q_hbm, up_hbm, own_hbm, *refs):
    count = len(pieces)
    q_exts, biases, refs = refs[:count], refs[count : 2 * count], refs[2 * count :]
    value_ref, own_ref, q_ref, key_ref, sems, key_sems, value_sems = refs
    rows = q_ref.shape[0]
    head_count = key_ref.shape[0]
    q_copy = pltpu.make_async_copy(q_hbm, q_ref, sems.at[0])
    own_copy = pltpu.make_async_copy(own_hbm, own_ref, sems.at[1])
    q_copy.start()
    key_copies, value_copies = [], []
    for head in range(head_count):
        source = up_hbm.at[:, pl.ds(head * PROJ, NOPE)]
        key_copies.append(pltpu.make_async_copy(source, key_ref.at[head], key_sems.at[head]))
        source = up_hbm.at[:, pl.ds(head * PROJ + NOPE, VD)]
        value_copies.append(pltpu.make_async_copy(source, value_ref.at[head], value_sems.at[head]))
    for copy in key_copies + [own_copy] + value_copies:
        copy.start()
    start = 0
    for piece, bias_ref in zip(pieces, biases):
        visible_bias(
            order_ref, prefix_ref, bias_ref, rows, owners, start, own_hbm.shape[1], cache_rows
        )
        start += piece
    q_copy.wait()
    for head in range(head_count):
        nope = q_ref[:, head * HEAD : head * HEAD + NOPE]
        rope = q_ref[:, head * HEAD + NOPE : (head + 1) * HEAD].astype(jnp.float32) * SCALE
        key_copies[head].wait()
        absorbed = lax.dot_general(
            nope, key_ref[head], (((1,), (1,)), ((), ())), preferred_element_type=jnp.float32
        )
        absorbed = (absorbed * SCALE).reshape(owners, rows // owners, LAT)
        rope = rope.reshape(owners, rows // owners, ROPE)
        start = 0
        for piece, q_ext in zip(pieces, q_exts):
            part = absorbed[:, start : start + piece].reshape(owners * piece, LAT)
            q_ext[head, :, :LAT] = part.astype(jnp.bfloat16)
            part = rope[:, start : start + piece].reshape(owners * piece, ROPE)
            q_ext[head, :, LAT:] = part.astype(jnp.bfloat16)
            start += piece
    for copy in [own_copy] + value_copies:
        copy.wait()


def load(queries, w_kv_up, own_keys, stretch_order, prefix_len, owners, pieces, cache_rows):
    head_count = w_kv_up.shape[1] // PROJ
    amount = stretch_order.shape[0] * own_keys.shape[1]
    out_shape = [
        jax.ShapeDtypeStruct((head_count, owners * piece, LAT + ROPE), jnp.bfloat16)
        for piece in pieces
    ]
    out_shape += [jax.ShapeDtypeStruct((owners * piece, amount), jnp.float32) for piece in pieces]
    out_shape += [
        jax.ShapeDtypeStruct((head_count, LAT, VD), jnp.bfloat16),
        jax.ShapeDtypeStruct(own_keys.shape, jnp.bfloat16),
    ]
    out = pl.pallas_call(
        functools.partial(load_kernel, owners, pieces, cache_rows),
        out_shape=out_shape,
        in_specs=[IN_SMEM, IN_SMEM] + [IN_HBM] * 3,
        out_specs=[IN_VMEM] * len(out_shape),
        scratch_shapes=[
            pltpu.VMEM(queries.shape, jnp.bfloat16),
            pltpu.VMEM((head_count, LAT, NOPE), jnp.bfloat16),
            pltpu.SemaphoreType.DMA((2,)),
            pltpu.SemaphoreType.DMA((head_count,)),
            pltpu.SemaphoreType.DMA((head_count,)),
        ],
        compiler_params=params(LOAD_LIMIT),
        cost_estimate=SHORT,
    )(stretch_order, prefix_len, queries, w_kv_up, own_keys)
    count = len(pieces)
    return out[:count], out[count : 2 * count], *out[2 * count :]


def visible_bias(order_ref, prefix_ref, bias_ref, query_rows, owners, start, row_span, cache_rows):
    n_ctx = order_ref.shape[0]
    half = row_span // 2
    rows = bias_ref.shape[0]
    piece = rows // owners
    own = lax.axis_index("ctx")
    core = lax.axis_index("head") % 2
    blocks = [(0, 0), (0, 1)]
    blocks += [(offset, core) for offset in range(1, n_ctx)]
    blocks += [(offset, 1 - core) for offset in range(1, n_ctx)]
    row = lax.broadcasted_iota(jnp.int32, (rows, half), 0)
    column = lax.broadcasted_iota(jnp.int32, (rows, half), 1)
    within_own = row // piece * (query_rows // owners) + start + row % piece
    query_pos = order_ref[own] * query_rows + within_own
    for index, (offset, second) in enumerate(blocks):
        source = own ^ offset
        within = second * half + column
        cache_pos = jnp.where(
            source * cache_rows + within < prefix_ref[0], -1, n_ctx * query_rows
        )
        key_pos = order_ref[source] * query_rows + within - cache_rows
        first_seen = jnp.where(within < cache_rows, cache_pos, key_pos)
        bias = jnp.where(first_seen <= query_pos, 0.0, MASKED).astype(jnp.float32)
        bias_ref[:, index * half : (index + 1) * half] = bias


def attention_kernel(count, q_ref, bias_ref, value_ref, *refs):
    heads, rows, depth = q_ref.shape
    if count:
        piece_refs, (out_ref, keys_ref, latent_ref) = refs[:count], refs[count:]
        start = 0
        for piece_ref in piece_refs:
            width = piece_ref.shape[1]
            keys_ref[:, start : start + width] = piece_ref[...]
            latent_ref[start : start + width, :] = piece_ref[:LAT, :].T
            start += width
    else:
        keys_ref, latent_ref, out_ref = refs
    amount = keys_ref.shape[1]
    group = max(1, min(heads, SUB_ROWS // rows))
    size = group * rows

    def score(first):
        queries = q_ref[first : first + group].reshape(size, depth)
        return jnp.dot(queries, keys_ref[...], preferred_element_type=jnp.float32)

    scores = score(0)
    for first in range(0, heads, group):
        later = score(first + group) if first + group < heads else None
        scores = scores.reshape(group, rows, amount) + bias_ref[...][None]
        top = jnp.max(scores, axis=2, keepdims=True)
        weights = jnp.exp2(scores - top)
        total = jnp.sum(weights, axis=2, keepdims=True).reshape(size, 1)
        mixed = jnp.dot(
            weights.reshape(size, amount).astype(jnp.bfloat16),
            latent_ref[...],
            preferred_element_type=jnp.float32,
        )
        mixed = (mixed / total).astype(jnp.bfloat16)
        for head in range(first, first + group):
            result = jnp.dot(
                mixed[(head - first) * rows : (head - first + 1) * rows],
                value_ref[head],
                preferred_element_type=jnp.float32,
            )
            out_ref[:, head * VD : (head + 1) * VD] = result.astype(jnp.bfloat16)
        scores = later


def attention(q_ext, bias, w_values, keys, gathered):
    head_count, rows, depth = q_ext.shape
    amount = bias.shape[1]
    out_shape = [jax.ShapeDtypeStruct((rows, head_count * VD), jnp.bfloat16)]
    if not gathered:
        out_shape.append(jax.ShapeDtypeStruct((depth, amount), jnp.bfloat16))
        out_shape.append(jax.ShapeDtypeStruct((amount, LAT), jnp.bfloat16))
    return pl.pallas_call(
        functools.partial(attention_kernel, 0 if gathered else len(keys)),
        out_shape=out_shape,
        in_specs=[IN_VMEM] * (3 + len(keys)),
        out_specs=[IN_VMEM] * len(out_shape),
        compiler_params=params(16 if amount <= 1024 else 40),
        cost_estimate=SHORT,
    )(q_ext, bias, w_values, *keys)


def product_kernel(count, n_x, after, weight_ref, *refs):
    piece_refs = refs[:count]
    sent_ref, kept_ref, rows_ref = refs[count + after :]
    rows = piece_refs[0].shape[0]
    columns = weight_ref.shape[1]
    for index, piece_ref in enumerate(piece_refs):
        rows_ref[index * rows : (index + 1) * rows, :] = piece_ref[...]
    is_first = lax.axis_index("head") % 2 == 0
    width = 256 if columns % 256 == 0 else columns
    for start in range(0, columns, width):
        span = slice(start, start + width)
        result = jnp.dot(rows_ref[...], weight_ref[:, span], preferred_element_type=jnp.float32)
        result = result.reshape(count, n_x, 2, rows // (2 * n_x), width)
        for x in range(n_x):
            first = result[:, x, 0].reshape(rows * count // (2 * n_x), width)
            second = result[:, x, 1].reshape(rows * count // (2 * n_x), width)
            sent_ref[x, :, span] = jnp.where(is_first, second, first).astype(jnp.bfloat16)
            kept_ref[x, :, span] = jnp.where(is_first, first, second)


def product(pieces, w_out, n_x, after):
    rows, depth = pieces[0].shape
    count = len(pieces)
    shape = (n_x, count * rows // (2 * n_x), w_out.shape[1])
    return pl.pallas_call(
        functools.partial(product_kernel, count, n_x, len(after)),
        out_shape=[jax.ShapeDtypeStruct(shape, jnp.bfloat16), jax.ShapeDtypeStruct(shape, jnp.float32)],
        in_specs=[IN_VMEM] * (1 + count) + [ANYWHERE] * len(after),
        out_specs=[IN_VMEM, IN_VMEM],
        scratch_shapes=[pltpu.VMEM((count * rows, depth), jnp.bfloat16)],
        compiler_params=params(16),
        cost_estimate=SHORT,
    )(w_out, *pieces, *after)


def core_sum_kernel(n_x, kept_ref, received_ref, total_ref, *sent_refs):
    x = lax.axis_index("head") // 2
    for offset in range(n_x):
        summed = kept_ref[x ^ offset] + received_ref[x ^ offset].astype(jnp.float32)
        if offset:
            sent_refs[offset - 1][...] = summed.astype(jnp.bfloat16)
        else:
            total_ref[...] = summed


def core_sum(kept, received):
    n_x, rows, columns = kept.shape
    own = jax.ShapeDtypeStruct((rows, columns), jnp.float32)
    sent = jax.ShapeDtypeStruct((rows, columns), jnp.bfloat16)
    out = pl.pallas_call(
        functools.partial(core_sum_kernel, n_x),
        out_shape=[own] + [sent] * (n_x - 1),
        in_specs=[IN_VMEM, IN_VMEM],
        out_specs=[IN_VMEM] * n_x,
        compiler_params=params(4),
        cost_estimate=SHORT,
    )(kept, received)
    return out[0], out[1:]


def x_sum_kernel(places, *refs):
    sources, refs = [], list(refs)
    for count, rows, indices in places:
        total = refs.pop(0)[...]
        for _ in range(count):
            total = total + refs.pop(0)[...].astype(jnp.float32)
        sources.append([total[index * rows : (index + 1) * rows] for index in indices])
    for out_ref, parts in zip(refs, zip(*sources)):
        out_ref[...] = jnp.concatenate(parts, axis=0).astype(jnp.bfloat16)


def x_sum(sources):
    columns = sources[0][0].shape[1]
    block = jax.ShapeDtypeStruct((sum(rows for _, _, rows, _ in sources), columns), jnp.bfloat16)
    arrays = [array for total, received, _, _ in sources for array in [total, *received]]
    places = [(len(received), rows, indices) for _, received, rows, indices in sources]
    outputs = len(sources[0][3])
    return pl.pallas_call(
        functools.partial(x_sum_kernel, places),
        out_shape=[block] * outputs,
        in_specs=[IN_VMEM] * len(arrays),
        out_specs=[IN_VMEM] * outputs,
        compiler_params=params(8),
        cost_estimate=SHORT,
    )(*arrays)


def place_kernel(*refs):
    blocks, out_ref = refs[:-1], refs[-1]
    ctx = lax.axis_index("ctx")
    width = blocks[0].shape[1]
    for offset, block in enumerate(blocks):
        column = pl.multiple_of((ctx ^ offset) * width, 128)
        out_ref[:, pl.ds(column, width)] = block[...]


def place_columns(blocks):
    n_ctx = len(blocks)
    rows, width = blocks[0].shape
    if width % 128:
        ctx = lax.axis_index("ctx")
        out = jnp.zeros((rows, n_ctx * width), jnp.bfloat16)
        for offset, block in enumerate(blocks):
            out = lax.dynamic_update_slice(out, block, (0, (ctx ^ offset) * width))
        return out
    return pl.pallas_call(
        place_kernel,
        grid=(1,),
        out_shape=jax.ShapeDtypeStruct((rows, n_ctx * width), jnp.bfloat16),
        in_specs=[IN_VMEM] * n_ctx,
        out_specs=pl.BlockSpec((rows, n_ctx * width), lambda i: (0, 0)),
        compiler_params=params(4),
        cost_estimate=SHORT,
    )(*blocks)


def shards(n_ctx, n_head, queries, kv_rows, w_kv_up, w_out, stretch_order, prefix_len):
    query_rows = queries.shape[0]
    row_span = kv_rows.shape[0]
    cache_rows = row_span - query_rows
    half = row_span // 2
    n_x = n_head // 2
    pieces = chunk_rows(query_rows // n_head)
    core = lax.axis_index("head") % 2

    with jax.named_scope("keys_over_ctx"):
        kv_t = kv_rows.T
        own_half = jnp.where(core == 0, kv_t[:, :half], kv_t[:, half:])
        halves = [exchange(own_half, "ctx", n_ctx, offset) for offset in range(1, n_ctx)]
    with jax.named_scope("load"):
        q_ext, bias, w_values, own_keys = load(
            queries, w_kv_up, kv_t, stretch_order, prefix_len, n_head, pieces, cache_rows
        )
    with jax.named_scope("keys_over_cores"):
        halves = [tie(array, [own_keys]) for array in halves]
        others = [exchange(array, "head", n_head, 1) for array in halves]
    with jax.named_scope("attention"):
        first, *keys = attention(q_ext[0], bias[0], w_values, [own_keys] + halves + others, False)
        attended = [first]
        for chunk in range(1, len(pieces)):
            attended += attention(q_ext[chunk], bias[chunk], w_values, keys, True)
    with jax.named_scope("attended_over_ctx"):
        gathered = [
            gather_pieces(own, n_ctx, attended[chunk + 1 : chunk + 2])
            for chunk, own in enumerate(attended)
        ]
    near = [0] + [1 << bit for bit in range(n_ctx.bit_length() - 1)]
    far = [offset for offset in range(n_ctx) if offset not in near]
    last = len(pieces) - 1
    units = [(chunk, list(range(n_ctx))) for chunk in range(last)] + [(last, near), (last, far)]
    sums = []
    after = attended[1:]
    crossed = []
    for unit, (chunk, offsets) in enumerate(units):
        with jax.named_scope("out_product"):
            first = after if unit == 0 else []
            sent, kept = product([gathered[chunk][d] for d in offsets], w_out, n_x, first)
        with jax.named_scope("sum_over_cores"):
            if chunk < last:
                sent = tie(sent, [gathered[chunk + 1][1], gathered[chunk + 1][n_ctx // 2]])
            elif offsets is far:
                sent = tie(sent, [*crossed[0], *after])
            total, sent = core_sum(kept, exchange(sent, "head", n_head, 1))
            after = [total]
        with jax.named_scope("sum_over_x"):
            if offsets is far:
                sent = [tie(array, crossed[-1]) for array in sent]
            crossed.append(
                [exchange(array, "head", n_head, 2 * d) for d, array in enumerate(sent, 1)]
            )
        sums.append((total, crossed[-1], pieces[chunk]))
    blocks = {}
    for group, ending in ((near, sums[-2]), (far, sums[-1])):
        with jax.named_scope("sum_over_x"):
            sources = [(*part, group) for part in sums[:-2]] + [(*ending, range(len(group)))]
            blocks.update(zip(group, x_sum(sources)))
        with jax.named_scope("columns_over_ctx"):
            for d in reversed(group):
                blocks[d] = exchange(blocks[d], "ctx", n_ctx, d) if d else blocks[d]
    with jax.named_scope("output"):
        return place_columns([blocks[d] for d in range(n_ctx)])


def solution(mesh):
    placed = (
        P(("groups", "ctx"), "head"),
        P(("groups", "ctx"), None),
        P(None, "head"),
        P("head", "ctx"),
        P("groups"),
        P("groups"),
    )
    return jax.shard_map(
        functools.partial(shards, mesh.shape["ctx"], mesh.shape["head"]),
        mesh=mesh,
        in_specs=placed,
        out_specs=P(("groups", "ctx", "head"), None),
        check_vma=False,
    )
```

```python
import functools
import math

import jax
import jax.numpy as jnp
from jax import lax
from jax.experimental import pallas as pl
from jax.experimental.pallas import tpu as pltpu
from jax.sharding import PartitionSpec as P

LAT = 512
NOPE = 128
ROPE = 64
VD = 128
HEAD = NOPE + ROPE
PROJ = NOPE + VD
SUB_ROWS = 256
LOAD_LIMIT = 44
MASKED = -1e30
RAISE_LATE = 20
RAISE_HANDED = 3
RAISE_X = 4
LOG2E = 1.4426950408889634
SCALE = LOG2E / math.sqrt(HEAD)


def cost(microseconds):
    return pl.CostEstimate(
        flops=int(1e9 * microseconds), bytes_accessed=int(3e6 * microseconds), transcendentals=0
    )


SHORT = pl.CostEstimate(flops=1024, bytes_accessed=1024, transcendentals=0)
IN_VMEM = pl.BlockSpec(memory_space=pltpu.VMEM)
IN_SMEM = pl.BlockSpec(memory_space=pltpu.SMEM)
IN_HBM = pl.BlockSpec(memory_space=pltpu.HBM)
ANYWHERE = pl.BlockSpec(memory_space=pl.ANY)


def chunk_rows(owned):
    return (owned // 2, owned // 2)


def params(mebibytes):
    return pltpu.CompilerParams(vmem_limit_bytes=mebibytes * 1024 * 1024)


def exchange(array, axis, size, bit):
    return lax.ppermute(array, axis, [(i, i ^ bit) for i in range(size)])


def tie_kernel(*refs):
    pass


def tie(array, after, lead=SHORT):
    return pl.pallas_call(
        tie_kernel,
        out_shape=jax.ShapeDtypeStruct(array.shape, array.dtype),
        in_specs=[ANYWHERE] * (1 + len(after)),
        out_specs=ANYWHERE,
        input_output_aliases={0: 0},
        compiler_params=params(1),
        cost_estimate=lead,
    )(array, *after)


def gather_pieces(own, size, after, lead):
    pieces = {0: own}
    bit = size // 2
    while bit:
        pieces[bit] = exchange(own, "ctx", size, bit)
        bit //= 2
    pieces[1] = tie(pieces[1], [], lead)
    bit = 1
    while bit < size:
        for offset in range(bit + 1, 2 * bit):
            if offset == bit + 1:
                pieces[bit] = tie(pieces[bit], after, lead)
            pieces[offset] = exchange(pieces[bit], "ctx", size, offset ^ bit)
        bit *= 2
    return [pieces[offset] for offset in range(size)]


def load_kernel(owners, pieces, cache_rows, order_ref, prefix_ref, q_hbm, up_hbm, own_hbm, *refs):
    count = len(pieces)
    q_exts, biases, refs = refs[:count], refs[count : 2 * count], refs[2 * count :]
    value_ref, own_ref, q_ref, key_ref, sems, key_sems, value_sems = refs
    rows = q_ref.shape[0]
    head_count = key_ref.shape[0]
    q_copy = pltpu.make_async_copy(q_hbm, q_ref, sems.at[0])
    own_copy = pltpu.make_async_copy(own_hbm, own_ref, sems.at[1])
    q_copy.start()
    key_copies, value_copies = [], []
    for head in range(head_count):
        source = up_hbm.at[:, pl.ds(head * PROJ, NOPE)]
        key_copies.append(pltpu.make_async_copy(source, key_ref.at[head], key_sems.at[head]))
        source = up_hbm.at[:, pl.ds(head * PROJ + NOPE, VD)]
        value_copies.append(pltpu.make_async_copy(source, value_ref.at[head], value_sems.at[head]))
    for copy in key_copies + [own_copy] + value_copies:
        copy.start()
    start = 0
    for piece, bias_ref in zip(pieces, biases):
        visible_bias(
            order_ref, prefix_ref, bias_ref, rows, owners, start, own_hbm.shape[1], cache_rows
        )
        start += piece
    q_copy.wait()
    for head in range(head_count):
        nope = q_ref[:, head * HEAD : head * HEAD + NOPE]
        rope = q_ref[:, head * HEAD + NOPE : (head + 1) * HEAD].astype(jnp.float32) * SCALE
        key_copies[head].wait()
        absorbed = lax.dot_general(
            nope, key_ref[head], (((1,), (1,)), ((), ())), preferred_element_type=jnp.float32
        )
        absorbed = (absorbed * SCALE).reshape(owners, rows // owners, LAT)
        rope = rope.reshape(owners, rows // owners, ROPE)
        start = 0
        for piece, q_ext in zip(pieces, q_exts):
            part = absorbed[:, start : start + piece].reshape(owners * piece, LAT)
            q_ext[head, :, :LAT] = part.astype(jnp.bfloat16)
            part = rope[:, start : start + piece].reshape(owners * piece, ROPE)
            q_ext[head, :, LAT:] = part.astype(jnp.bfloat16)
            start += piece
    for copy in [own_copy] + value_copies:
        copy.wait()


def load(queries, w_kv_up, own_keys, stretch_order, prefix_len, owners, pieces, cache_rows):
    head_count = w_kv_up.shape[1] // PROJ
    amount = stretch_order.shape[0] * own_keys.shape[1]
    out_shape = [
        jax.ShapeDtypeStruct((head_count, owners * piece, LAT + ROPE), jnp.bfloat16)
        for piece in pieces
    ]
    out_shape += [jax.ShapeDtypeStruct((owners * piece, amount), jnp.float32) for piece in pieces]
    out_shape += [
        jax.ShapeDtypeStruct((head_count, LAT, VD), jnp.bfloat16),
        jax.ShapeDtypeStruct(own_keys.shape, jnp.bfloat16),
    ]
    out = pl.pallas_call(
        functools.partial(load_kernel, owners, pieces, cache_rows),
        out_shape=out_shape,
        in_specs=[IN_SMEM, IN_SMEM] + [IN_HBM] * 3,
        out_specs=[IN_VMEM] * len(out_shape),
        scratch_shapes=[
            pltpu.VMEM(queries.shape, jnp.bfloat16),
            pltpu.VMEM((head_count, LAT, NOPE), jnp.bfloat16),
            pltpu.SemaphoreType.DMA((2,)),
            pltpu.SemaphoreType.DMA((head_count,)),
            pltpu.SemaphoreType.DMA((head_count,)),
        ],
        compiler_params=params(LOAD_LIMIT),
        cost_estimate=SHORT,
    )(stretch_order, prefix_len, queries, w_kv_up, own_keys)
    count = len(pieces)
    return out[:count], out[count : 2 * count], *out[2 * count :]


def visible_bias(order_ref, prefix_ref, bias_ref, query_rows, owners, start, row_span, cache_rows):
    n_ctx = order_ref.shape[0]
    half = row_span // 2
    rows = bias_ref.shape[0]
    piece = rows // owners
    own = lax.axis_index("ctx")
    core = lax.axis_index("head") % 2
    blocks = [(0, 0), (0, 1)]
    blocks += [(offset, core) for offset in range(1, n_ctx)]
    blocks += [(offset, 1 - core) for offset in range(1, n_ctx)]
    row = lax.broadcasted_iota(jnp.int32, (rows, half), 0)
    column = lax.broadcasted_iota(jnp.int32, (rows, half), 1)
    within_own = row // piece * (query_rows // owners) + start + row % piece
    query_pos = order_ref[own] * query_rows + within_own
    for index, (offset, second) in enumerate(blocks):
        source = own ^ offset
        within = second * half + column
        cache_pos = jnp.where(
            source * cache_rows + within < prefix_ref[0], -1, n_ctx * query_rows
        )
        key_pos = order_ref[source] * query_rows + within - cache_rows
        first_seen = jnp.where(within < cache_rows, cache_pos, key_pos)
        bias = jnp.where(first_seen <= query_pos, 0.0, MASKED).astype(jnp.float32)
        bias_ref[:, index * half : (index + 1) * half] = bias


def attention_kernel(count, q_ref, bias_ref, value_ref, *refs):
    heads, rows, depth = q_ref.shape
    if count:
        piece_refs, (out_ref, keys_ref, latent_ref) = refs[:count], refs[count:]
        start = 0
        for piece_ref in piece_refs:
            width = piece_ref.shape[1]
            keys_ref[:, start : start + width] = piece_ref[...]
            latent_ref[start : start + width, :] = piece_ref[:LAT, :].T
            start += width
    else:
        keys_ref, latent_ref, out_ref = refs
    amount = keys_ref.shape[1]
    group = max(1, min(heads, SUB_ROWS // rows))
    size = group * rows

    def score(first):
        queries = q_ref[first : first + group].reshape(size, depth)
        return jnp.dot(queries, keys_ref[...], preferred_element_type=jnp.float32)

    scores = score(0)
    for first in range(0, heads, group):
        later = score(first + group) if first + group < heads else None
        scores = scores.reshape(group, rows, amount) + bias_ref[...][None]
        top = jnp.max(scores, axis=2, keepdims=True)
        weights = jnp.exp2(scores - top)
        total = jnp.sum(weights, axis=2, keepdims=True).reshape(size, 1)
        mixed = jnp.dot(
            weights.reshape(size, amount).astype(jnp.bfloat16),
            latent_ref[...],
            preferred_element_type=jnp.float32,
        )
        mixed = (mixed / total).astype(jnp.bfloat16)
        for head in range(first, first + group):
            result = jnp.dot(
                mixed[(head - first) * rows : (head - first + 1) * rows],
                value_ref[head],
                preferred_element_type=jnp.float32,
            )
            out_ref[:, head * VD : (head + 1) * VD] = result.astype(jnp.bfloat16)
        scores = later


def attention(q_ext, bias, w_values, keys, gathered):
    head_count, rows, depth = q_ext.shape
    amount = bias.shape[1]
    out_shape = [jax.ShapeDtypeStruct((rows, head_count * VD), jnp.bfloat16)]
    if not gathered:
        out_shape.append(jax.ShapeDtypeStruct((depth, amount), jnp.bfloat16))
        out_shape.append(jax.ShapeDtypeStruct((amount, LAT), jnp.bfloat16))
    return pl.pallas_call(
        functools.partial(attention_kernel, 0 if gathered else len(keys)),
        out_shape=out_shape,
        in_specs=[IN_VMEM] * (3 + len(keys)),
        out_specs=[IN_VMEM] * len(out_shape),
        compiler_params=params(16 if amount <= 1024 else 40),
        cost_estimate=SHORT,
    )(q_ext, bias, w_values, *keys)


def product_kernel(count, n_x, after, weight_ref, *refs):
    piece_refs = refs[:count]
    sent_ref, kept_ref, rows_ref = refs[count + after :]
    rows = piece_refs[0].shape[0]
    columns = weight_ref.shape[1]
    for index, piece_ref in enumerate(piece_refs):
        rows_ref[index * rows : (index + 1) * rows, :] = piece_ref[...]
    is_first = lax.axis_index("head") % 2 == 0
    width = 256 if columns % 256 == 0 else columns
    for start in range(0, columns, width):
        span = slice(start, start + width)
        result = jnp.dot(rows_ref[...], weight_ref[:, span], preferred_element_type=jnp.float32)
        result = result.reshape(count, n_x, 2, rows // (2 * n_x), width)
        for x in range(n_x):
            first = result[:, x, 0].reshape(rows * count // (2 * n_x), width)
            second = result[:, x, 1].reshape(rows * count // (2 * n_x), width)
            sent_ref[x, :, span] = jnp.where(is_first, second, first).astype(jnp.bfloat16)
            kept_ref[x, :, span] = jnp.where(is_first, first, second)


def product(pieces, w_out, n_x, after):
    rows, depth = pieces[0].shape
    count = len(pieces)
    shape = (n_x, count * rows // (2 * n_x), w_out.shape[1])
    return pl.pallas_call(
        functools.partial(product_kernel, count, n_x, len(after)),
        out_shape=[jax.ShapeDtypeStruct(shape, jnp.bfloat16), jax.ShapeDtypeStruct(shape, jnp.float32)],
        in_specs=[IN_VMEM] * (1 + count) + [ANYWHERE] * len(after),
        out_specs=[IN_VMEM, IN_VMEM],
        scratch_shapes=[pltpu.VMEM((count * rows, depth), jnp.bfloat16)],
        compiler_params=params(16),
        cost_estimate=SHORT,
    )(w_out, *pieces, *after)


def core_sum_kernel(n_x, after, kept_ref, received_ref, *refs):
    total_ref, *sent_refs = refs[after:]
    x = lax.axis_index("head") // 2
    for offset in range(n_x):
        summed = kept_ref[x ^ offset] + received_ref[x ^ offset].astype(jnp.float32)
        if offset:
            sent_refs[offset - 1][...] = summed.astype(jnp.bfloat16)
        else:
            total_ref[...] = summed


def core_sum(kept, received, after):
    n_x, rows, columns = kept.shape
    own = jax.ShapeDtypeStruct((rows, columns), jnp.float32)
    sent = jax.ShapeDtypeStruct((rows, columns), jnp.bfloat16)
    out = pl.pallas_call(
        functools.partial(core_sum_kernel, n_x, len(after)),
        out_shape=[own] + [sent] * (n_x - 1),
        in_specs=[IN_VMEM, IN_VMEM] + [ANYWHERE] * len(after),
        out_specs=[IN_VMEM] * n_x,
        compiler_params=params(4),
        cost_estimate=SHORT,
    )(kept, received, *after)
    return out[0], out[1:]


def x_sum_kernel(counts, rows, places, *refs):
    sources, refs = [], list(refs)
    for count in counts:
        total = refs.pop(0)[...]
        for _ in range(count):
            total = total + refs.pop(0)[...].astype(jnp.float32)
        sources.append(total)
    for out_ref, parts in zip(refs, places):
        parts = [sources[unit][index * rows : (index + 1) * rows] for unit, index in parts]
        out_ref[...] = jnp.concatenate(parts, axis=0).astype(jnp.bfloat16)


def x_sum(sums, rows, places):
    columns = sums[0][0].shape[1]
    arrays = [array for total, received in sums for array in [total, *received]]
    counts = [len(received) for _, received in sums]
    blocks = [jax.ShapeDtypeStruct((rows * len(parts), columns), jnp.bfloat16) for parts in places]
    return pl.pallas_call(
        functools.partial(x_sum_kernel, counts, rows, places),
        out_shape=blocks,
        in_specs=[IN_VMEM] * len(arrays),
        out_specs=[IN_VMEM] * len(blocks),
        compiler_params=params(8),
        cost_estimate=SHORT,
    )(*arrays)


def place_kernel(*refs):
    blocks, out_ref = refs[:-1], refs[-1]
    ctx = lax.axis_index("ctx")
    width = blocks[0].shape[1]
    for offset, block in enumerate(blocks):
        column = pl.multiple_of((ctx ^ offset) * width, 128)
        out_ref[:, pl.ds(column, width)] = block[...]


def place_columns(blocks):
    n_ctx = len(blocks)
    rows, width = blocks[0].shape
    if width % 128:
        ctx = lax.axis_index("ctx")
        out = jnp.zeros((rows, n_ctx * width), jnp.bfloat16)
        for offset, block in enumerate(blocks):
            out = lax.dynamic_update_slice(out, block, (0, (ctx ^ offset) * width))
        return out
    return pl.pallas_call(
        place_kernel,
        grid=(1,),
        out_shape=jax.ShapeDtypeStruct((rows, n_ctx * width), jnp.bfloat16),
        in_specs=[IN_VMEM] * n_ctx,
        out_specs=pl.BlockSpec((rows, n_ctx * width), lambda i: (0, 0)),
        compiler_params=params(4),
        cost_estimate=SHORT,
    )(*blocks)


def shards(n_ctx, n_head, queries, kv_rows, w_kv_up, w_out, stretch_order, prefix_len):
    query_rows = queries.shape[0]
    row_span = kv_rows.shape[0]
    cache_rows = row_span - query_rows
    half = row_span // 2
    n_x = n_head // 2
    pieces = chunk_rows(query_rows // n_head)
    core = lax.axis_index("head") % 2

    with jax.named_scope("keys_over_ctx"):
        kv_t = kv_rows.T
        own_half = jnp.where(core == 0, kv_t[:, :half], kv_t[:, half:])
        halves = [exchange(own_half, "ctx", n_ctx, offset) for offset in range(1, n_ctx)]
    with jax.named_scope("load"):
        q_ext, bias, w_values, own_keys = load(
            queries, w_kv_up, kv_t, stretch_order, prefix_len, n_head, pieces, cache_rows
        )
    with jax.named_scope("keys_over_cores"):
        halves = [tie(array, [own_keys]) for array in halves]
        others = [exchange(array, "head", n_head, 1) for array in halves]
    with jax.named_scope("attention"):
        first, *keys = attention(q_ext[0], bias[0], w_values, [own_keys] + halves + others, False)
        attended = [first]
        for chunk in range(1, len(pieces)):
            attended += attention(q_ext[chunk], bias[chunk], w_values, keys, True)
    with jax.named_scope("attended_over_ctx"):
        early = gather_pieces(attended[0], n_ctx, attended[1:], SHORT)
        late = gather_pieces(attended[1], n_ctx, [], cost(RAISE_LATE))
    powers = [1 << bit for bit in range(n_ctx.bit_length() - 1)]
    handed = [offset for offset in range(1, n_ctx) if offset not in powers]
    for offset in handed:
        late[offset] = tie(late[offset], [late[n_ctx // 2]], cost(RAISE_HANDED))
    gathered = [early, late]
    units = [
        [(0, 0), (1, 0)],
        [(0, offset) for offset in range(1, n_ctx)],
        [(1, offset) for offset in powers],
        [(1, offset) for offset in handed],
    ]
    sums = []
    for unit, members in enumerate(units):
        with jax.named_scope("out_product"):
            sources = [gathered[chunk][offset] for chunk, offset in members]
            after = [*attended[1:], *sums[0][1]] if unit == 1 else []
            sent, kept = product(sources, w_out, n_x, after)
        with jax.named_scope("sum_over_cores"):
            if unit == 3:
                sent = tie(sent, [sums[2][0]])
            total, sent = core_sum(kept, exchange(sent, "head", n_head, 1), [])
        with jax.named_scope("sum_over_x"):
            if unit == 3:
                before = sums[1][1]
                sent = [tie(array, before, cost(RAISE_X)) for array in sent]
            crossed = [exchange(array, "head", n_head, 2 * d) for d, array in enumerate(sent, 1)]
        sums.append((total, crossed))
    blocks = {}
    for offsets, last in (([0], 0), (powers, 2), (handed, 3)):
        with jax.named_scope("sum_over_x"):
            sources = [sums[0]] if offsets == [0] else [sums[1], sums[last]]
            places = []
            for offset in offsets:
                parts = [(0, 0), (0, 1)]
                if offset:
                    parts = [(0, offset - 1), (1, units[last].index((1, offset)))]
                places.append(parts)
            found = x_sum(sources, pieces[0], places)
        with jax.named_scope("columns_over_ctx"):
            for offset, block in reversed(list(zip(offsets, found))):
                blocks[offset] = exchange(block, "ctx", n_ctx, offset) if offset else block
    with jax.named_scope("output"):
        return place_columns([blocks[d] for d in range(n_ctx)])


def solution(mesh):
    placed = (
        P(("groups", "ctx"), "head"),
        P(("groups", "ctx"), None),
        P(None, "head"),
        P("head", "ctx"),
        P("groups"),
        P("groups"),
    )
    return jax.shard_map(
        functools.partial(shards, mesh.shape["ctx"], mesh.shape["head"]),
        mesh=mesh,
        in_specs=placed,
        out_specs=P(("groups", "ctx", "head"), None),
        check_vma=False,
    )
```

```python
import functools
import math

import jax
import jax.numpy as jnp
from jax import lax
from jax.experimental import pallas as pl
from jax.experimental.pallas import tpu as pltpu
from jax.sharding import PartitionSpec as P

LAT = 512
NOPE = 128
ROPE = 64
VD = 128
HEAD = NOPE + ROPE
PROJ = NOPE + VD
SUB_ROWS = 256
LOAD_LIMIT = 44
MASKED = -1e30
LEAD_EARLY = 6
LEAD_NEAR = 2
LEAD_LATE = 3
LEAD_HANDED = 3
LEAD_X = 1
LOG2E = 1.4426950408889634
SCALE = LOG2E / math.sqrt(HEAD)


def cost(microseconds):
    return pl.CostEstimate(
        flops=int(1e9 * microseconds), bytes_accessed=int(3e6 * microseconds), transcendentals=0
    )


SHORT = pl.CostEstimate(flops=1024, bytes_accessed=1024, transcendentals=0)
IN_VMEM = pl.BlockSpec(memory_space=pltpu.VMEM)
IN_SMEM = pl.BlockSpec(memory_space=pltpu.SMEM)
IN_HBM = pl.BlockSpec(memory_space=pltpu.HBM)
ANYWHERE = pl.BlockSpec(memory_space=pl.ANY)


def chunk_rows(owned):
    return (owned // 2, owned // 2)


def params(mebibytes):
    return pltpu.CompilerParams(vmem_limit_bytes=mebibytes * 1024 * 1024)


def exchange(array, axis, size, bit):
    return lax.ppermute(array, axis, [(i, i ^ bit) for i in range(size)])


def tie_kernel(*refs):
    pass


def tie(array, after, lead=SHORT):
    return pl.pallas_call(
        tie_kernel,
        out_shape=jax.ShapeDtypeStruct(array.shape, array.dtype),
        in_specs=[ANYWHERE] * (1 + len(after)),
        out_specs=ANYWHERE,
        input_output_aliases={0: 0},
        compiler_params=params(1),
        cost_estimate=lead,
    )(array, *after)


def gather_pieces(own, near, size, after, lead, far_lead):
    pieces = {0: own, 1: tie(exchange(near, "ctx", size, 1), [], lead)}
    bit = size // 2
    while bit > 1:
        pieces[bit] = exchange(own, "ctx", size, bit)
        bit //= 2
    bit = 2
    while bit < size:
        for offset in range(bit + 1, 2 * bit):
            if offset == bit + 1:
                pieces[bit] = tie(pieces[bit], after, far_lead)
            pieces[offset] = exchange(pieces[bit], "ctx", size, offset ^ bit)
        bit *= 2
    return [pieces[offset] for offset in range(size)]


def load_kernel(owners, pieces, cache_rows, order_ref, prefix_ref, q_hbm, up_hbm, own_hbm, *refs):
    count = len(pieces)
    q_exts, biases, refs = refs[:count], refs[count : 2 * count], refs[2 * count :]
    value_ref, own_ref, q_ref, key_ref, sems, key_sems, value_sems = refs
    rows = q_ref.shape[0]
    head_count = key_ref.shape[0]
    q_copy = pltpu.make_async_copy(q_hbm, q_ref, sems.at[0])
    own_copy = pltpu.make_async_copy(own_hbm, own_ref, sems.at[1])
    q_copy.start()
    key_copies, value_copies = [], []
    for head in range(head_count):
        source = up_hbm.at[:, pl.ds(head * PROJ, NOPE)]
        key_copies.append(pltpu.make_async_copy(source, key_ref.at[head], key_sems.at[head]))
        source = up_hbm.at[:, pl.ds(head * PROJ + NOPE, VD)]
        value_copies.append(pltpu.make_async_copy(source, value_ref.at[head], value_sems.at[head]))
    for copy in key_copies + [own_copy] + value_copies:
        copy.start()
    start = 0
    for piece, bias_ref in zip(pieces, biases):
        visible_bias(
            order_ref, prefix_ref, bias_ref, rows, owners, start, own_hbm.shape[1], cache_rows
        )
        start += piece
    q_copy.wait()
    for head in range(head_count):
        nope = q_ref[:, head * HEAD : head * HEAD + NOPE]
        rope = q_ref[:, head * HEAD + NOPE : (head + 1) * HEAD].astype(jnp.float32) * SCALE
        key_copies[head].wait()
        absorbed = lax.dot_general(
            nope, key_ref[head], (((1,), (1,)), ((), ())), preferred_element_type=jnp.float32
        )
        absorbed = (absorbed * SCALE).reshape(owners, rows // owners, LAT)
        rope = rope.reshape(owners, rows // owners, ROPE)
        start = 0
        for piece, q_ext in zip(pieces, q_exts):
            part = absorbed[:, start : start + piece].reshape(owners * piece, LAT)
            q_ext[head, :, :LAT] = part.astype(jnp.bfloat16)
            part = rope[:, start : start + piece].reshape(owners * piece, ROPE)
            q_ext[head, :, LAT:] = part.astype(jnp.bfloat16)
            start += piece
    for copy in [own_copy] + value_copies:
        copy.wait()


def load(queries, w_kv_up, own_keys, stretch_order, prefix_len, owners, pieces, cache_rows):
    head_count = w_kv_up.shape[1] // PROJ
    amount = stretch_order.shape[0] * own_keys.shape[1]
    out_shape = [
        jax.ShapeDtypeStruct((head_count, owners * piece, LAT + ROPE), jnp.bfloat16)
        for piece in pieces
    ]
    out_shape += [jax.ShapeDtypeStruct((owners * piece, amount), jnp.float32) for piece in pieces]
    out_shape += [
        jax.ShapeDtypeStruct((head_count, LAT, VD), jnp.bfloat16),
        jax.ShapeDtypeStruct(own_keys.shape, jnp.bfloat16),
    ]
    out = pl.pallas_call(
        functools.partial(load_kernel, owners, pieces, cache_rows),
        out_shape=out_shape,
        in_specs=[IN_SMEM, IN_SMEM] + [IN_HBM] * 3,
        out_specs=[IN_VMEM] * len(out_shape),
        scratch_shapes=[
            pltpu.VMEM(queries.shape, jnp.bfloat16),
            pltpu.VMEM((head_count, LAT, NOPE), jnp.bfloat16),
            pltpu.SemaphoreType.DMA((2,)),
            pltpu.SemaphoreType.DMA((head_count,)),
            pltpu.SemaphoreType.DMA((head_count,)),
        ],
        compiler_params=params(LOAD_LIMIT),
        cost_estimate=SHORT,
    )(stretch_order, prefix_len, queries, w_kv_up, own_keys)
    count = len(pieces)
    return out[:count], out[count : 2 * count], *out[2 * count :]


def visible_bias(order_ref, prefix_ref, bias_ref, query_rows, owners, start, row_span, cache_rows):
    n_ctx = order_ref.shape[0]
    half = row_span // 2
    rows = bias_ref.shape[0]
    piece = rows // owners
    own = lax.axis_index("ctx")
    core = lax.axis_index("head") % 2
    blocks = [(0, 0), (0, 1)]
    blocks += [(offset, core) for offset in range(1, n_ctx)]
    blocks += [(offset, 1 - core) for offset in range(1, n_ctx)]
    row = lax.broadcasted_iota(jnp.int32, (rows, half), 0)
    column = lax.broadcasted_iota(jnp.int32, (rows, half), 1)
    within_own = row // piece * (query_rows // owners) + start + row % piece
    query_pos = order_ref[own] * query_rows + within_own
    for index, (offset, second) in enumerate(blocks):
        source = own ^ offset
        within = second * half + column
        cache_pos = jnp.where(
            source * cache_rows + within < prefix_ref[0], -1, n_ctx * query_rows
        )
        key_pos = order_ref[source] * query_rows + within - cache_rows
        first_seen = jnp.where(within < cache_rows, cache_pos, key_pos)
        bias = jnp.where(first_seen <= query_pos, 0.0, MASKED).astype(jnp.float32)
        bias_ref[:, index * half : (index + 1) * half] = bias


def attention_kernel(count, q_ref, bias_ref, value_ref, *refs):
    heads, rows, depth = q_ref.shape
    if count:
        piece_refs, (out_ref, keys_ref, latent_ref) = refs[:count], refs[count:]
        start = 0
        for piece_ref in piece_refs:
            width = piece_ref.shape[1]
            keys_ref[:, start : start + width] = piece_ref[...]
            latent_ref[start : start + width, :] = piece_ref[:LAT, :].T
            start += width
    else:
        keys_ref, latent_ref, out_ref, copy_ref = refs
    amount = keys_ref.shape[1]
    group = max(1, min(heads, SUB_ROWS // rows))
    size = group * rows

    def score(first):
        queries = q_ref[first : first + group].reshape(size, depth)
        return jnp.dot(queries, keys_ref[...], preferred_element_type=jnp.float32)

    scores = score(0)
    for first in range(0, heads, group):
        later = score(first + group) if first + group < heads else None
        scores = scores.reshape(group, rows, amount) + bias_ref[...][None]
        top = jnp.max(scores, axis=2, keepdims=True)
        weights = jnp.exp2(scores - top)
        total = jnp.sum(weights, axis=2, keepdims=True).reshape(size, 1)
        mixed = jnp.dot(
            weights.reshape(size, amount).astype(jnp.bfloat16),
            latent_ref[...],
            preferred_element_type=jnp.float32,
        )
        mixed = (mixed / total).astype(jnp.bfloat16)
        for head in range(first, first + group):
            result = jnp.dot(
                mixed[(head - first) * rows : (head - first + 1) * rows],
                value_ref[head],
                preferred_element_type=jnp.float32,
            )
            out_ref[:, head * VD : (head + 1) * VD] = result.astype(jnp.bfloat16)
            if not count:
                copy_ref[:, head * VD : (head + 1) * VD] = result.astype(jnp.bfloat16)
        scores = later


def attention(q_ext, bias, w_values, keys, gathered):
    head_count, rows, depth = q_ext.shape
    amount = bias.shape[1]
    out_shape = [jax.ShapeDtypeStruct((rows, head_count * VD), jnp.bfloat16)]
    if gathered:
        out_shape *= 2
    else:
        out_shape.append(jax.ShapeDtypeStruct((depth, amount), jnp.bfloat16))
        out_shape.append(jax.ShapeDtypeStruct((amount, LAT), jnp.bfloat16))
    return pl.pallas_call(
        functools.partial(attention_kernel, 0 if gathered else len(keys)),
        out_shape=out_shape,
        in_specs=[IN_VMEM] * (3 + len(keys)),
        out_specs=[IN_VMEM] * len(out_shape),
        compiler_params=params(16 if amount <= 1024 else 40),
        cost_estimate=SHORT,
    )(q_ext, bias, w_values, *keys)


def product_kernel(count, n_x, after, weight_ref, *refs):
    piece_refs = refs[:count]
    sent_ref, kept_ref, rows_ref = refs[count + after :]
    rows = piece_refs[0].shape[0]
    columns = weight_ref.shape[1]
    for index, piece_ref in enumerate(piece_refs):
        rows_ref[index * rows : (index + 1) * rows, :] = piece_ref[...]
    is_first = lax.axis_index("head") % 2 == 0
    width = 256 if columns % 256 == 0 else columns
    for start in range(0, columns, width):
        span = slice(start, start + width)
        result = jnp.dot(rows_ref[...], weight_ref[:, span], preferred_element_type=jnp.float32)
        result = result.reshape(count, n_x, 2, rows // (2 * n_x), width)
        for x in range(n_x):
            first = result[:, x, 0].reshape(rows * count // (2 * n_x), width)
            second = result[:, x, 1].reshape(rows * count // (2 * n_x), width)
            sent_ref[x, :, span] = jnp.where(is_first, second, first).astype(jnp.bfloat16)
            kept_ref[x, :, span] = jnp.where(is_first, first, second)


def product(pieces, w_out, n_x, after):
    rows, depth = pieces[0].shape
    count = len(pieces)
    shape = (n_x, count * rows // (2 * n_x), w_out.shape[1])
    return pl.pallas_call(
        functools.partial(product_kernel, count, n_x, len(after)),
        out_shape=[jax.ShapeDtypeStruct(shape, jnp.bfloat16), jax.ShapeDtypeStruct(shape, jnp.float32)],
        in_specs=[IN_VMEM] * (1 + count) + [ANYWHERE] * len(after),
        out_specs=[IN_VMEM, IN_VMEM],
        scratch_shapes=[pltpu.VMEM((count * rows, depth), jnp.bfloat16)],
        compiler_params=params(16),
        cost_estimate=SHORT,
    )(w_out, *pieces, *after)


def core_sum_kernel(n_x, after, kept_ref, received_ref, *refs):
    total_ref, *sent_refs = refs[after:]
    x = lax.axis_index("head") // 2
    for offset in range(n_x):
        summed = kept_ref[x ^ offset] + received_ref[x ^ offset].astype(jnp.float32)
        if offset:
            sent_refs[offset - 1][...] = summed.astype(jnp.bfloat16)
        else:
            total_ref[...] = summed


def core_sum(kept, received, after):
    n_x, rows, columns = kept.shape
    own = jax.ShapeDtypeStruct((rows, columns), jnp.float32)
    sent = jax.ShapeDtypeStruct((rows, columns), jnp.bfloat16)
    out = pl.pallas_call(
        functools.partial(core_sum_kernel, n_x, len(after)),
        out_shape=[own] + [sent] * (n_x - 1),
        in_specs=[IN_VMEM, IN_VMEM] + [ANYWHERE] * len(after),
        out_specs=[IN_VMEM] * n_x,
        compiler_params=params(4),
        cost_estimate=SHORT,
    )(kept, received, *after)
    return out[0], out[1:]


def x_sum_kernel(counts, rows, places, *refs):
    sources, refs = [], list(refs)
    for count in counts:
        total = refs.pop(0)[...]
        for _ in range(count):
            total = total + refs.pop(0)[...].astype(jnp.float32)
        sources.append(total)
    for out_ref, parts in zip(refs, places):
        parts = [sources[unit][index * rows : (index + 1) * rows] for unit, index in parts]
        out_ref[...] = jnp.concatenate(parts, axis=0).astype(jnp.bfloat16)


def x_sum(sums, rows, places):
    columns = sums[0][0].shape[1]
    arrays = [array for total, received in sums for array in [total, *received]]
    counts = [len(received) for _, received in sums]
    blocks = [jax.ShapeDtypeStruct((rows * len(parts), columns), jnp.bfloat16) for parts in places]
    return pl.pallas_call(
        functools.partial(x_sum_kernel, counts, rows, places),
        out_shape=blocks,
        in_specs=[IN_VMEM] * len(arrays),
        out_specs=[IN_VMEM] * len(blocks),
        compiler_params=params(8),
        cost_estimate=SHORT,
    )(*arrays)


def place_kernel(*refs):
    blocks, out_ref = refs[:-1], refs[-1]
    ctx = lax.axis_index("ctx")
    width = blocks[0].shape[1]
    for offset, block in enumerate(blocks):
        column = pl.multiple_of((ctx ^ offset) * width, 128)
        out_ref[:, pl.ds(column, width)] = block[...]


def place_columns(blocks):
    n_ctx = len(blocks)
    rows, width = blocks[0].shape
    if width % 128:
        ctx = lax.axis_index("ctx")
        out = jnp.zeros((rows, n_ctx * width), jnp.bfloat16)
        for offset, block in enumerate(blocks):
            out = lax.dynamic_update_slice(out, block, (0, (ctx ^ offset) * width))
        return out
    return pl.pallas_call(
        place_kernel,
        grid=(1,),
        out_shape=jax.ShapeDtypeStruct((rows, n_ctx * width), jnp.bfloat16),
        in_specs=[IN_VMEM] * n_ctx,
        out_specs=pl.BlockSpec((rows, n_ctx * width), lambda i: (0, 0)),
        compiler_params=params(4),
        cost_estimate=SHORT,
    )(*blocks)


def shards(n_ctx, n_head, queries, kv_rows, w_kv_up, w_out, stretch_order, prefix_len):
    query_rows = queries.shape[0]
    row_span = kv_rows.shape[0]
    cache_rows = row_span - query_rows
    half = row_span // 2
    n_x = n_head // 2
    pieces = chunk_rows(query_rows // n_head)
    core = lax.axis_index("head") % 2

    with jax.named_scope("keys_over_ctx"):
        kv_t = kv_rows.T
        own_half = jnp.where(core == 0, kv_t[:, :half], kv_t[:, half:])
        halves = [exchange(own_half, "ctx", n_ctx, offset) for offset in range(1, n_ctx)]
    with jax.named_scope("load"):
        q_ext, bias, w_values, own_keys = load(
            queries, w_kv_up, kv_t, stretch_order, prefix_len, n_head, pieces, cache_rows
        )
    with jax.named_scope("keys_over_cores"):
        halves = [tie(array, [own_keys]) for array in halves]
        others = [exchange(array, "head", n_head, 1) for array in halves]
    with jax.named_scope("attention"):
        first, *keys = attention(q_ext[0], bias[0], w_values, [own_keys] + halves + others, False)
        second, again = attention(q_ext[1], bias[1], w_values, keys, True)
    with jax.named_scope("attended_over_ctx"):
        early = gather_pieces(first, first, n_ctx, [second], cost(LEAD_EARLY), SHORT)
        again = tie(again, [early[n_ctx // 2]])
        late = gather_pieces(second, again, n_ctx, [early[n_ctx - 1]], cost(LEAD_NEAR), cost(LEAD_LATE))
    powers = [1 << bit for bit in range(n_ctx.bit_length() - 1)]
    handed = [offset for offset in range(1, n_ctx) if offset not in powers]
    gathered = [early, late]
    units = [
        [(0, 0), (1, 0)],
        [(0, offset) for offset in range(1, n_ctx)],
        [(1, offset) for offset in powers],
        [(1, offset) for offset in handed],
    ]
    sums = []
    for unit, members in enumerate(units):
        with jax.named_scope("out_product"):
            if unit == 3:
                for offset in handed:
                    late[offset] = tie(late[offset], sums[1][1], cost(LEAD_HANDED))
            sources = [gathered[chunk][offset] for chunk, offset in members]
            after = [second, *sums[0][1]] if unit == 1 else []
            sent, kept = product(sources, w_out, n_x, after)
        with jax.named_scope("sum_over_cores"):
            if unit == 3:
                sent = tie(sent, [sums[2][0]])
            total, sent = core_sum(kept, exchange(sent, "head", n_head, 1), [])
        with jax.named_scope("sum_over_x"):
            if unit == 3:
                before = sums[1][1]
                sent = [tie(array, before, cost(LEAD_X)) for array in sent]
            crossed = [exchange(array, "head", n_head, 2 * d) for d, array in enumerate(sent, 1)]
        sums.append((total, crossed))
    blocks = {}
    for offsets, last in (([0], 0), (powers, 2), (handed, 3)):
        with jax.named_scope("sum_over_x"):
            sources = [sums[0]] if offsets == [0] else [sums[1], sums[last]]
            places = []
            for offset in offsets:
                parts = [(0, 0), (0, 1)]
                if offset:
                    parts = [(0, offset - 1), (1, units[last].index((1, offset)))]
                places.append(parts)
            found = x_sum(sources, pieces[0], places)
        with jax.named_scope("columns_over_ctx"):
            for offset, block in reversed(list(zip(offsets, found))):
                blocks[offset] = exchange(block, "ctx", n_ctx, offset) if offset else block
    with jax.named_scope("output"):
        return place_columns([blocks[d] for d in range(n_ctx)])


def solution(mesh):
    placed = (
        P(("groups", "ctx"), "head"),
        P(("groups", "ctx"), None),
        P(None, "head"),
        P("head", "ctx"),
        P("groups"),
        P("groups"),
    )
    return jax.shard_map(
        functools.partial(shards, mesh.shape["ctx"], mesh.shape["head"]),
        mesh=mesh,
        in_specs=placed,
        out_specs=P(("groups", "ctx", "head"), None),
        check_vma=False,
    )
```

```python
import functools
import math

import jax
import jax.numpy as jnp
from jax import lax
from jax.experimental import pallas as pl
from jax.experimental.pallas import tpu as pltpu
from jax.sharding import PartitionSpec as P

LAT = 512
NOPE = 128
ROPE = 64
VD = 128
HEAD = NOPE + ROPE
PROJ = NOPE + VD
SUB_ROWS = 256
LOAD_LIMIT = 44
MASKED = -1e30
LEAD_EARLY = 6
LEAD_NEAR = 2
LEAD_LATE = 3
LEAD_HANDED = 3
LEAD_AHEAD = 3
LEAD_X = 1
LOG2E = 1.4426950408889634
SCALE = LOG2E / math.sqrt(HEAD)


def cost(microseconds):
    return pl.CostEstimate(
        flops=int(1e9 * microseconds), bytes_accessed=int(3e6 * microseconds), transcendentals=0
    )


SHORT = pl.CostEstimate(flops=1024, bytes_accessed=1024, transcendentals=0)
IN_VMEM = pl.BlockSpec(memory_space=pltpu.VMEM)
IN_SMEM = pl.BlockSpec(memory_space=pltpu.SMEM)
IN_HBM = pl.BlockSpec(memory_space=pltpu.HBM)
ANYWHERE = pl.BlockSpec(memory_space=pl.ANY)


def chunk_rows(owned):
    return (owned // 2, owned // 2)


def params(mebibytes):
    return pltpu.CompilerParams(vmem_limit_bytes=mebibytes * 1024 * 1024)


def exchange(array, axis, size, bit):
    return lax.ppermute(array, axis, [(i, i ^ bit) for i in range(size)])


def tie_kernel(*refs):
    pass


def tie(array, after, lead=SHORT):
    return pl.pallas_call(
        tie_kernel,
        out_shape=jax.ShapeDtypeStruct(array.shape, array.dtype),
        in_specs=[ANYWHERE] * (1 + len(after)),
        out_specs=ANYWHERE,
        input_output_aliases={0: 0},
        compiler_params=params(1),
        cost_estimate=lead,
    )(array, *after)


def gather_pieces(own, near, size, after, lead, far_lead):
    pieces = {0: own, 1: tie(exchange(near, "ctx", size, 1), [], lead)}
    bit = size // 2
    while bit > 1:
        pieces[bit] = exchange(own, "ctx", size, bit)
        bit //= 2
    bit = 2
    while bit < size:
        for offset in range(bit + 1, 2 * bit):
            if offset == bit + 1:
                pieces[bit] = tie(pieces[bit], after, far_lead)
            pieces[offset] = exchange(pieces[bit], "ctx", size, offset ^ bit)
        bit *= 2
    return [pieces[offset] for offset in range(size)]


def load_kernel(owners, pieces, cache_rows, order_ref, prefix_ref, q_hbm, up_hbm, own_hbm, *refs):
    count = len(pieces)
    q_exts, biases, refs = refs[:count], refs[count : 2 * count], refs[2 * count :]
    value_ref, own_ref, q_ref, key_ref, sems, key_sems, value_sems = refs
    rows = q_ref.shape[0]
    head_count = key_ref.shape[0]
    q_copy = pltpu.make_async_copy(q_hbm, q_ref, sems.at[0])
    own_copy = pltpu.make_async_copy(own_hbm, own_ref, sems.at[1])
    q_copy.start()
    key_copies, value_copies = [], []
    for head in range(head_count):
        source = up_hbm.at[:, pl.ds(head * PROJ, NOPE)]
        key_copies.append(pltpu.make_async_copy(source, key_ref.at[head], key_sems.at[head]))
        source = up_hbm.at[:, pl.ds(head * PROJ + NOPE, VD)]
        value_copies.append(pltpu.make_async_copy(source, value_ref.at[head], value_sems.at[head]))
    for copy in key_copies + [own_copy] + value_copies:
        copy.start()
    start = 0
    for piece, bias_ref in zip(pieces, biases):
        visible_bias(
            order_ref, prefix_ref, bias_ref, rows, owners, start, own_hbm.shape[1], cache_rows
        )
        start += piece
    q_copy.wait()
    for head in range(head_count):
        nope = q_ref[:, head * HEAD : head * HEAD + NOPE]
        rope = q_ref[:, head * HEAD + NOPE : (head + 1) * HEAD].astype(jnp.float32) * SCALE
        key_copies[head].wait()
        absorbed = lax.dot_general(
            nope, key_ref[head], (((1,), (1,)), ((), ())), preferred_element_type=jnp.float32
        )
        absorbed = (absorbed * SCALE).reshape(owners, rows // owners, LAT)
        rope = rope.reshape(owners, rows // owners, ROPE)
        start = 0
        for piece, q_ext in zip(pieces, q_exts):
            part = absorbed[:, start : start + piece].reshape(owners * piece, LAT)
            q_ext[head, :, :LAT] = part.astype(jnp.bfloat16)
            part = rope[:, start : start + piece].reshape(owners * piece, ROPE)
            q_ext[head, :, LAT:] = part.astype(jnp.bfloat16)
            start += piece
    for copy in [own_copy] + value_copies:
        copy.wait()


def load(queries, w_kv_up, own_keys, stretch_order, prefix_len, owners, pieces, cache_rows):
    head_count = w_kv_up.shape[1] // PROJ
    amount = stretch_order.shape[0] * own_keys.shape[1]
    out_shape = [
        jax.ShapeDtypeStruct((head_count, owners * piece, LAT + ROPE), jnp.bfloat16)
        for piece in pieces
    ]
    out_shape += [jax.ShapeDtypeStruct((owners * piece, amount), jnp.float32) for piece in pieces]
    out_shape += [
        jax.ShapeDtypeStruct((head_count, LAT, VD), jnp.bfloat16),
        jax.ShapeDtypeStruct(own_keys.shape, jnp.bfloat16),
    ]
    out = pl.pallas_call(
        functools.partial(load_kernel, owners, pieces, cache_rows),
        out_shape=out_shape,
        in_specs=[IN_SMEM, IN_SMEM] + [IN_HBM] * 3,
        out_specs=[IN_VMEM] * len(out_shape),
        scratch_shapes=[
            pltpu.VMEM(queries.shape, jnp.bfloat16),
            pltpu.VMEM((head_count, LAT, NOPE), jnp.bfloat16),
            pltpu.SemaphoreType.DMA((2,)),
            pltpu.SemaphoreType.DMA((head_count,)),
            pltpu.SemaphoreType.DMA((head_count,)),
        ],
        compiler_params=params(LOAD_LIMIT),
        cost_estimate=SHORT,
    )(stretch_order, prefix_len, queries, w_kv_up, own_keys)
    count = len(pieces)
    return out[:count], out[count : 2 * count], *out[2 * count :]


def visible_bias(order_ref, prefix_ref, bias_ref, query_rows, owners, start, row_span, cache_rows):
    n_ctx = order_ref.shape[0]
    half = row_span // 2
    rows = bias_ref.shape[0]
    piece = rows // owners
    own = lax.axis_index("ctx")
    core = lax.axis_index("head") % 2
    blocks = [(0, 0), (0, 1)]
    blocks += [(offset, core) for offset in range(1, n_ctx)]
    blocks += [(offset, 1 - core) for offset in range(1, n_ctx)]
    row = lax.broadcasted_iota(jnp.int32, (rows, half), 0)
    column = lax.broadcasted_iota(jnp.int32, (rows, half), 1)
    within_own = row // piece * (query_rows // owners) + start + row % piece
    query_pos = order_ref[own] * query_rows + within_own
    for index, (offset, second) in enumerate(blocks):
        source = own ^ offset
        within = second * half + column
        cache_pos = jnp.where(
            source * cache_rows + within < prefix_ref[0], -1, n_ctx * query_rows
        )
        key_pos = order_ref[source] * query_rows + within - cache_rows
        first_seen = jnp.where(within < cache_rows, cache_pos, key_pos)
        bias = jnp.where(first_seen <= query_pos, 0.0, MASKED).astype(jnp.float32)
        bias_ref[:, index * half : (index + 1) * half] = bias


def attention_kernel(count, q_ref, bias_ref, value_ref, *refs):
    heads, rows, depth = q_ref.shape
    if count:
        piece_refs, (out_ref, keys_ref, latent_ref) = refs[:count], refs[count:]
        start = 0
        for piece_ref in piece_refs:
            width = piece_ref.shape[1]
            keys_ref[:, start : start + width] = piece_ref[...]
            latent_ref[start : start + width, :] = piece_ref[:LAT, :].T
            start += width
    else:
        keys_ref, latent_ref, out_ref, copy_ref = refs
    amount = keys_ref.shape[1]
    group = max(1, min(heads, SUB_ROWS // rows))
    size = group * rows

    def score(first):
        queries = q_ref[first : first + group].reshape(size, depth)
        return jnp.dot(queries, keys_ref[...], preferred_element_type=jnp.float32)

    scores = score(0)
    for first in range(0, heads, group):
        later = score(first + group) if first + group < heads else None
        scores = scores.reshape(group, rows, amount) + bias_ref[...][None]
        top = jnp.max(scores, axis=2, keepdims=True)
        weights = jnp.exp2(scores - top)
        total = jnp.sum(weights, axis=2, keepdims=True).reshape(size, 1)
        mixed = jnp.dot(
            weights.reshape(size, amount).astype(jnp.bfloat16),
            latent_ref[...],
            preferred_element_type=jnp.float32,
        )
        mixed = (mixed / total).astype(jnp.bfloat16)
        for head in range(first, first + group):
            result = jnp.dot(
                mixed[(head - first) * rows : (head - first + 1) * rows],
                value_ref[head],
                preferred_element_type=jnp.float32,
            )
            out_ref[:, head * VD : (head + 1) * VD] = result.astype(jnp.bfloat16)
            if not count:
                copy_ref[:, head * VD : (head + 1) * VD] = result.astype(jnp.bfloat16)
        scores = later


def attention(q_ext, bias, w_values, keys, gathered):
    head_count, rows, depth = q_ext.shape
    amount = bias.shape[1]
    out_shape = [jax.ShapeDtypeStruct((rows, head_count * VD), jnp.bfloat16)]
    if gathered:
        out_shape *= 2
    else:
        out_shape.append(jax.ShapeDtypeStruct((depth, amount), jnp.bfloat16))
        out_shape.append(jax.ShapeDtypeStruct((amount, LAT), jnp.bfloat16))
    return pl.pallas_call(
        functools.partial(attention_kernel, 0 if gathered else len(keys)),
        out_shape=out_shape,
        in_specs=[IN_VMEM] * (3 + len(keys)),
        out_specs=[IN_VMEM] * len(out_shape),
        compiler_params=params(16 if amount <= 1024 else 40),
        cost_estimate=SHORT,
    )(q_ext, bias, w_values, *keys)


def product_kernel(count, n_x, after, weight_ref, *refs):
    piece_refs = refs[:count]
    sent_ref, kept_ref, rows_ref = refs[count + after :]
    rows = piece_refs[0].shape[0]
    columns = weight_ref.shape[1]
    for index, piece_ref in enumerate(piece_refs):
        rows_ref[index * rows : (index + 1) * rows, :] = piece_ref[...]
    is_first = lax.axis_index("head") % 2 == 0
    width = 256 if columns % 256 == 0 else columns
    for start in range(0, columns, width):
        span = slice(start, start + width)
        result = jnp.dot(rows_ref[...], weight_ref[:, span], preferred_element_type=jnp.float32)
        result = result.reshape(count, n_x, 2, rows // (2 * n_x), width)
        for x in range(n_x):
            first = result[:, x, 0].reshape(rows * count // (2 * n_x), width)
            second = result[:, x, 1].reshape(rows * count // (2 * n_x), width)
            sent_ref[x, :, span] = jnp.where(is_first, second, first).astype(jnp.bfloat16)
            kept_ref[x, :, span] = jnp.where(is_first, first, second)


def product(pieces, w_out, n_x, after):
    rows, depth = pieces[0].shape
    count = len(pieces)
    shape = (n_x, count * rows // (2 * n_x), w_out.shape[1])
    return pl.pallas_call(
        functools.partial(product_kernel, count, n_x, len(after)),
        out_shape=[jax.ShapeDtypeStruct(shape, jnp.bfloat16), jax.ShapeDtypeStruct(shape, jnp.float32)],
        in_specs=[IN_VMEM] * (1 + count) + [ANYWHERE] * len(after),
        out_specs=[IN_VMEM, IN_VMEM],
        scratch_shapes=[pltpu.VMEM((count * rows, depth), jnp.bfloat16)],
        compiler_params=params(16),
        cost_estimate=SHORT,
    )(w_out, *pieces, *after)


def core_sum_kernel(n_x, after, kept_ref, received_ref, *refs):
    total_ref, *sent_refs = refs[after:]
    x = lax.axis_index("head") // 2
    for offset in range(n_x):
        summed = kept_ref[x ^ offset] + received_ref[x ^ offset].astype(jnp.float32)
        if offset:
            sent_refs[offset - 1][...] = summed.astype(jnp.bfloat16)
        else:
            total_ref[...] = summed


def core_sum(kept, received, after):
    n_x, rows, columns = kept.shape
    own = jax.ShapeDtypeStruct((rows, columns), jnp.float32)
    sent = jax.ShapeDtypeStruct((rows, columns), jnp.bfloat16)
    out = pl.pallas_call(
        functools.partial(core_sum_kernel, n_x, len(after)),
        out_shape=[own] + [sent] * (n_x - 1),
        in_specs=[IN_VMEM, IN_VMEM] + [ANYWHERE] * len(after),
        out_specs=[IN_VMEM] * n_x,
        compiler_params=params(4),
        cost_estimate=SHORT,
    )(kept, received, *after)
    return out[0], out[1:]


def x_sum_kernel(counts, rows, places, *refs):
    sources, refs = [], list(refs)
    for count in counts:
        total = refs.pop(0)[...]
        for _ in range(count):
            total = total + refs.pop(0)[...].astype(jnp.float32)
        sources.append(total)
    for out_ref, parts in zip(refs, places):
        parts = [sources[unit][index * rows : (index + 1) * rows] for unit, index in parts]
        out_ref[...] = jnp.concatenate(parts, axis=0).astype(jnp.bfloat16)


def x_sum(sums, rows, places):
    columns = sums[0][0].shape[1]
    arrays = [array for total, received in sums for array in [total, *received]]
    counts = [len(received) for _, received in sums]
    blocks = [jax.ShapeDtypeStruct((rows * len(parts), columns), jnp.bfloat16) for parts in places]
    return pl.pallas_call(
        functools.partial(x_sum_kernel, counts, rows, places),
        out_shape=blocks,
        in_specs=[IN_VMEM] * len(arrays),
        out_specs=[IN_VMEM] * len(blocks),
        compiler_params=params(8),
        cost_estimate=SHORT,
    )(*arrays)


def place_kernel(counts, *refs):
    refs, out_ref = list(refs[:-1]), refs[-1]
    ctx = lax.axis_index("ctx")
    width = refs[0].shape[1]
    for offset, count in enumerate(counts):
        parts = [refs.pop(0)[...].astype(jnp.float32) for _ in range(count)]
        column = pl.multiple_of((ctx ^ offset) * width, 128)
        out_ref[:, pl.ds(column, width)] = jnp.concatenate(parts, axis=0).astype(jnp.bfloat16)


def place_columns(blocks):
    n_ctx = len(blocks)
    rows = sum(block.shape[0] for block in blocks[0])
    width = blocks[0][0].shape[1]
    if width % 128:
        ctx = lax.axis_index("ctx")
        out = jnp.zeros((rows, n_ctx * width), jnp.bfloat16)
        for offset, parts in enumerate(blocks):
            block = jnp.concatenate(parts, axis=0)
            out = lax.dynamic_update_slice(out, block, (0, (ctx ^ offset) * width))
        return out
    arrays = [block for parts in blocks for block in parts]
    return pl.pallas_call(
        functools.partial(place_kernel, [len(parts) for parts in blocks]),
        grid=(1,),
        out_shape=jax.ShapeDtypeStruct((rows, n_ctx * width), jnp.bfloat16),
        in_specs=[IN_VMEM] * len(arrays),
        out_specs=pl.BlockSpec((rows, n_ctx * width), lambda i: (0, 0)),
        compiler_params=params(4),
        cost_estimate=SHORT,
    )(*arrays)


def shards(n_ctx, n_head, queries, kv_rows, w_kv_up, w_out, stretch_order, prefix_len):
    query_rows = queries.shape[0]
    row_span = kv_rows.shape[0]
    cache_rows = row_span - query_rows
    half = row_span // 2
    n_x = n_head // 2
    pieces = chunk_rows(query_rows // n_head)
    core = lax.axis_index("head") % 2

    with jax.named_scope("keys_over_ctx"):
        kv_t = kv_rows.T
        own_half = jnp.where(core == 0, kv_t[:, :half], kv_t[:, half:])
        halves = [exchange(own_half, "ctx", n_ctx, offset) for offset in range(1, n_ctx)]
    with jax.named_scope("load"):
        q_ext, bias, w_values, own_keys = load(
            queries, w_kv_up, kv_t, stretch_order, prefix_len, n_head, pieces, cache_rows
        )
    with jax.named_scope("keys_over_cores"):
        halves = [tie(array, [own_keys]) for array in halves]
        others = [exchange(array, "head", n_head, 1) for array in halves]
    with jax.named_scope("attention"):
        first, *keys = attention(q_ext[0], bias[0], w_values, [own_keys] + halves + others, False)
        second, again = attention(q_ext[1], bias[1], w_values, keys, True)
    with jax.named_scope("attended_over_ctx"):
        early = gather_pieces(first, first, n_ctx, [second], cost(LEAD_EARLY), SHORT)
        again = tie(again, [early[n_ctx // 2]])
        late = gather_pieces(second, again, n_ctx, [early[n_ctx - 1]], cost(LEAD_NEAR), cost(LEAD_LATE))
    powers = [1 << bit for bit in range(n_ctx.bit_length() - 1)]
    handed = [offset for offset in range(1, n_ctx) if offset not in powers]
    gathered = [early, late]
    units = [
        [(0, 0), (1, 0)],
        [(0, offset) for offset in range(1, n_ctx)],
        [(1, offset) for offset in powers],
        [(1, offset) for offset in handed],
    ]
    sums = []
    for unit, members in enumerate(units):
        with jax.named_scope("out_product"):
            if unit == 3:
                for offset in handed:
                    late[offset] = tie(late[offset], sums[1][1], cost(LEAD_HANDED))
            sources = [gathered[chunk][offset] for chunk, offset in members]
            after = [second, *sums[0][1]] if unit == 1 else []
            if unit == 2:
                after = [sums[1][0]]
            sent, kept = product(sources, w_out, n_x, after)
        with jax.named_scope("sum_over_cores"):
            if unit == 3:
                sent = tie(sent, [sums[2][0]])
            total, sent = core_sum(kept, exchange(sent, "head", n_head, 1), [])
        with jax.named_scope("sum_over_x"):
            if unit == 3:
                before = sums[1][1]
                sent = [tie(array, before, cost(LEAD_X)) for array in sent]
            crossed = [exchange(array, "head", n_head, 2 * d) for d, array in enumerate(sent, 1)]
        sums.append((total, crossed))
    def added(units_in, offsets, parts_of):
        with jax.named_scope("sum_over_x"):
            places = [parts_of(offset) for offset in offsets]
            found = x_sum([sums[unit] for unit in units_in], pieces[0], places)
        with jax.named_scope("columns_over_ctx"):
            return [
                exchange(block, "ctx", n_ctx, offset) if offset else block
                for offset, block in zip(offsets, found)
            ]

    blocks = {0: added([0], [0], lambda offset: [(0, 0), (0, 1)])}
    ahead = added([1], handed, lambda offset: [(0, offset - 1)])
    ahead = [tie(block, [], cost(LEAD_AHEAD)) for block in ahead]
    both = added([1, 2], powers, lambda offset: [(0, offset - 1), (1, powers.index(offset))])
    behind = added([3], handed, lambda offset: [(0, handed.index(offset))])
    blocks.update({offset: [block] for offset, block in zip(powers, both)})
    for offset, first_rows, last_rows in zip(handed, ahead, behind):
        blocks[offset] = [first_rows, last_rows]
    with jax.named_scope("output"):
        return place_columns([blocks[d] for d in range(n_ctx)])


def solution(mesh):
    placed = (
        P(("groups", "ctx"), "head"),
        P(("groups", "ctx"), None),
        P(None, "head"),
        P("head", "ctx"),
        P("groups"),
        P("groups"),
    )
    return jax.shard_map(
        functools.partial(shards, mesh.shape["ctx"], mesh.shape["head"]),
        mesh=mesh,
        in_specs=placed,
        out_specs=P(("groups", "ctx", "head"), None),
        check_vma=False,
    )
```

```python
import functools
import math

import jax
import jax.numpy as jnp
from jax import lax
from jax.experimental import pallas as pl
from jax.experimental.pallas import tpu as pltpu
from jax.sharding import PartitionSpec as P

LAT = 512
NOPE = 128
ROPE = 64
VD = 128
HEAD = NOPE + ROPE
PROJ = NOPE + VD
SUB_ROWS = 512
LOAD_LIMIT = 44
MASKED = -1e30
LEAD_KEYS = 0.1
LEAD_EARLY = 6
LEAD_NEAR = 2
LEAD_LATE = 3
LEAD_HANDED = 3
LEAD_AHEAD = 3
LEAD_X = 1
LOG2E = 1.4426950408889634
SCALE = LOG2E / math.sqrt(HEAD)


def cost(microseconds):
    return pl.CostEstimate(
        flops=int(1e9 * microseconds), bytes_accessed=int(3e6 * microseconds), transcendentals=0
    )


SHORT = pl.CostEstimate(flops=1024, bytes_accessed=1024, transcendentals=0)
IN_VMEM = pl.BlockSpec(memory_space=pltpu.VMEM)
IN_SMEM = pl.BlockSpec(memory_space=pltpu.SMEM)
IN_HBM = pl.BlockSpec(memory_space=pltpu.HBM)
ANYWHERE = pl.BlockSpec(memory_space=pl.ANY)


def chunk_rows(owned):
    return (owned // 2, owned // 2)


def key_order(n_ctx):
    return [*range(2, n_ctx), 1]


def params(mebibytes):
    return pltpu.CompilerParams(vmem_limit_bytes=mebibytes * 1024 * 1024)


def exchange(array, axis, size, bit):
    return lax.ppermute(array, axis, [(i, i ^ bit) for i in range(size)])


def tie_kernel(*refs):
    pass


def tie(array, after, lead=SHORT):
    return pl.pallas_call(
        tie_kernel,
        out_shape=jax.ShapeDtypeStruct(array.shape, array.dtype),
        in_specs=[ANYWHERE] * (1 + len(after)),
        out_specs=ANYWHERE,
        input_output_aliases={0: 0},
        compiler_params=params(1),
        cost_estimate=lead,
    )(array, *after)


def gather_pieces(own, near, size, after, lead, far_lead):
    pieces = {0: own, 1: tie(exchange(near, "ctx", size, 1), [], lead)}
    bit = size // 2
    while bit > 1:
        pieces[bit] = exchange(own, "ctx", size, bit)
        bit //= 2
    bit = 2
    while bit < size:
        for offset in range(bit + 1, 2 * bit):
            if offset == bit + 1:
                pieces[bit] = tie(pieces[bit], after, far_lead)
            pieces[offset] = exchange(pieces[bit], "ctx", size, offset ^ bit)
        bit *= 2
    return [pieces[offset] for offset in range(size)]


def load_kernel(owners, pieces, cache_rows, order_ref, prefix_ref, q_hbm, up_hbm, own_hbm, *refs):
    count = len(pieces)
    q_exts, biases, refs = refs[:count], refs[count : 2 * count], refs[2 * count :]
    value_ref, own_ref, q_ref, key_ref, sems, key_sems, value_sems = refs
    rows = q_ref.shape[0]
    head_count = key_ref.shape[0]
    q_copy = pltpu.make_async_copy(q_hbm, q_ref, sems.at[0])
    own_copy = pltpu.make_async_copy(own_hbm, own_ref, sems.at[1])
    q_copy.start()
    key_copies, value_copies = [], []
    for head in range(head_count):
        source = up_hbm.at[:, pl.ds(head * PROJ, NOPE)]
        key_copies.append(pltpu.make_async_copy(source, key_ref.at[head], key_sems.at[head]))
        source = up_hbm.at[:, pl.ds(head * PROJ + NOPE, VD)]
        value_copies.append(pltpu.make_async_copy(source, value_ref.at[head], value_sems.at[head]))
    for copy in key_copies + [own_copy] + value_copies:
        copy.start()
    start = 0
    for piece, bias_ref in zip(pieces, biases):
        visible_bias(
            order_ref, prefix_ref, bias_ref, rows, owners, start, own_hbm.shape[1], cache_rows
        )
        start += piece
    q_copy.wait()
    for head in range(head_count):
        nope = q_ref[:, head * HEAD : head * HEAD + NOPE]
        rope = q_ref[:, head * HEAD + NOPE : (head + 1) * HEAD].astype(jnp.float32) * SCALE
        key_copies[head].wait()
        absorbed = lax.dot_general(
            nope, key_ref[head], (((1,), (1,)), ((), ())), preferred_element_type=jnp.float32
        )
        absorbed = (absorbed * SCALE).reshape(owners, rows // owners, LAT)
        rope = rope.reshape(owners, rows // owners, ROPE)
        start = 0
        for piece, q_ext in zip(pieces, q_exts):
            part = absorbed[:, start : start + piece].reshape(owners * piece, LAT)
            q_ext[head, :, :LAT] = part.astype(jnp.bfloat16)
            part = rope[:, start : start + piece].reshape(owners * piece, ROPE)
            q_ext[head, :, LAT:] = part.astype(jnp.bfloat16)
            start += piece
    for copy in [own_copy] + value_copies:
        copy.wait()


def load(queries, w_kv_up, own_keys, stretch_order, prefix_len, owners, pieces, cache_rows):
    head_count = w_kv_up.shape[1] // PROJ
    amount = stretch_order.shape[0] * own_keys.shape[1]
    out_shape = [
        jax.ShapeDtypeStruct((head_count, owners * piece, LAT + ROPE), jnp.bfloat16)
        for piece in pieces
    ]
    out_shape += [jax.ShapeDtypeStruct((owners * piece, amount), jnp.float32) for piece in pieces]
    out_shape += [
        jax.ShapeDtypeStruct((head_count, LAT, VD), jnp.bfloat16),
        jax.ShapeDtypeStruct(own_keys.shape, jnp.bfloat16),
    ]
    out = pl.pallas_call(
        functools.partial(load_kernel, owners, pieces, cache_rows),
        out_shape=out_shape,
        in_specs=[IN_SMEM, IN_SMEM] + [IN_HBM] * 3,
        out_specs=[IN_VMEM] * len(out_shape),
        scratch_shapes=[
            pltpu.VMEM(queries.shape, jnp.bfloat16),
            pltpu.VMEM((head_count, LAT, NOPE), jnp.bfloat16),
            pltpu.SemaphoreType.DMA((2,)),
            pltpu.SemaphoreType.DMA((head_count,)),
            pltpu.SemaphoreType.DMA((head_count,)),
        ],
        compiler_params=params(LOAD_LIMIT),
        cost_estimate=SHORT,
    )(stretch_order, prefix_len, queries, w_kv_up, own_keys)
    count = len(pieces)
    return out[:count], out[count : 2 * count], *out[2 * count :]


def visible_bias(order_ref, prefix_ref, bias_ref, query_rows, owners, start, row_span, cache_rows):
    n_ctx = order_ref.shape[0]
    half = row_span // 2
    rows = bias_ref.shape[0]
    piece = rows // owners
    own = lax.axis_index("ctx")
    core = lax.axis_index("head") % 2
    blocks = [(0, 0), (0, 1)]
    blocks += [(offset, core) for offset in key_order(n_ctx)]
    blocks += [(offset, 1 - core) for offset in key_order(n_ctx)]
    row = lax.broadcasted_iota(jnp.int32, (rows, half), 0)
    column = lax.broadcasted_iota(jnp.int32, (rows, half), 1)
    within_own = row // piece * (query_rows // owners) + start + row % piece
    query_pos = order_ref[own] * query_rows + within_own
    for index, (offset, second) in enumerate(blocks):
        source = own ^ offset
        within = second * half + column
        cache_pos = jnp.where(
            source * cache_rows + within < prefix_ref[0], -1, n_ctx * query_rows
        )
        key_pos = order_ref[source] * query_rows + within - cache_rows
        first_seen = jnp.where(within < cache_rows, cache_pos, key_pos)
        bias = jnp.where(first_seen <= query_pos, 0.0, MASKED).astype(jnp.float32)
        bias_ref[:, index * half : (index + 1) * half] = bias


def attention_kernel(count, q_ref, bias_ref, value_ref, *refs):
    heads, rows, depth = q_ref.shape
    if count:
        piece_refs, (out_ref, keys_ref, latent_ref) = refs[:count], refs[count:]
        start = 0
        for piece_ref in piece_refs:
            width = piece_ref.shape[1]
            keys_ref[:, start : start + width] = piece_ref[...]
            latent_ref[start : start + width, :] = piece_ref[:LAT, :].T
            start += width
    else:
        keys_ref, latent_ref, out_ref, copy_ref = refs
    amount = keys_ref.shape[1]
    group = max(1, min(heads, SUB_ROWS // rows))
    size = group * rows

    def score(first):
        queries = q_ref[first : first + group].reshape(size, depth)
        return jnp.dot(queries, keys_ref[...], preferred_element_type=jnp.float32)

    scores = score(0)
    for first in range(0, heads, group):
        later = score(first + group) if first + group < heads else None
        scores = scores.reshape(group, rows, amount) + bias_ref[...][None]
        top = jnp.max(scores, axis=2, keepdims=True)
        weights = jnp.exp2(scores - top)
        total = jnp.sum(weights, axis=2, keepdims=True).reshape(size, 1)
        mixed = jnp.dot(
            weights.reshape(size, amount).astype(jnp.bfloat16),
            latent_ref[...],
            preferred_element_type=jnp.float32,
        )
        mixed = (mixed / total).astype(jnp.bfloat16)
        for head in range(first, first + group):
            result = jnp.dot(
                mixed[(head - first) * rows : (head - first + 1) * rows],
                value_ref[head],
                preferred_element_type=jnp.float32,
            )
            out_ref[:, head * VD : (head + 1) * VD] = result.astype(jnp.bfloat16)
            if not count:
                copy_ref[:, head * VD : (head + 1) * VD] = result.astype(jnp.bfloat16)
        scores = later


def attention(q_ext, bias, w_values, keys, gathered):
    head_count, rows, depth = q_ext.shape
    amount = bias.shape[1]
    out_shape = [jax.ShapeDtypeStruct((rows, head_count * VD), jnp.bfloat16)]
    if gathered:
        out_shape *= 2
    else:
        out_shape.append(jax.ShapeDtypeStruct((depth, amount), jnp.bfloat16))
        out_shape.append(jax.ShapeDtypeStruct((amount, LAT), jnp.bfloat16))
    return pl.pallas_call(
        functools.partial(attention_kernel, 0 if gathered else len(keys)),
        out_shape=out_shape,
        in_specs=[IN_VMEM] * (3 + len(keys)),
        out_specs=[IN_VMEM] * len(out_shape),
        compiler_params=params(16 if amount <= 1024 else 40),
        cost_estimate=SHORT,
    )(q_ext, bias, w_values, *keys)


def product_kernel(count, n_x, after, weight_ref, *refs):
    piece_refs = refs[:count]
    sent_ref, kept_ref, rows_ref = refs[count + after :]
    rows = piece_refs[0].shape[0]
    columns = weight_ref.shape[1]
    for index, piece_ref in enumerate(piece_refs):
        rows_ref[index * rows : (index + 1) * rows, :] = piece_ref[...]
    is_first = lax.axis_index("head") % 2 == 0
    width = 256 if columns % 256 == 0 else columns
    for start in range(0, columns, width):
        span = slice(start, start + width)
        result = jnp.dot(rows_ref[...], weight_ref[:, span], preferred_element_type=jnp.float32)
        result = result.reshape(count, n_x, 2, rows // (2 * n_x), width)
        for x in range(n_x):
            first = result[:, x, 0].reshape(rows * count // (2 * n_x), width)
            second = result[:, x, 1].reshape(rows * count // (2 * n_x), width)
            sent_ref[x, :, span] = jnp.where(is_first, second, first).astype(jnp.bfloat16)
            kept_ref[x, :, span] = jnp.where(is_first, first, second)


def product(pieces, w_out, n_x, after):
    rows, depth = pieces[0].shape
    count = len(pieces)
    shape = (n_x, count * rows // (2 * n_x), w_out.shape[1])
    return pl.pallas_call(
        functools.partial(product_kernel, count, n_x, len(after)),
        out_shape=[jax.ShapeDtypeStruct(shape, jnp.bfloat16), jax.ShapeDtypeStruct(shape, jnp.float32)],
        in_specs=[IN_VMEM] * (1 + count) + [ANYWHERE] * len(after),
        out_specs=[IN_VMEM, IN_VMEM],
        scratch_shapes=[pltpu.VMEM((count * rows, depth), jnp.bfloat16)],
        compiler_params=params(16),
        cost_estimate=SHORT,
    )(w_out, *pieces, *after)


def core_sum_kernel(n_x, after, kept_ref, received_ref, *refs):
    total_ref, *sent_refs = refs[after:]
    x = lax.axis_index("head") // 2
    for offset in range(n_x):
        summed = kept_ref[x ^ offset] + received_ref[x ^ offset].astype(jnp.float32)
        if offset:
            sent_refs[offset - 1][...] = summed.astype(jnp.bfloat16)
        else:
            total_ref[...] = summed


def core_sum(kept, received, after):
    n_x, rows, columns = kept.shape
    own = jax.ShapeDtypeStruct((rows, columns), jnp.float32)
    sent = jax.ShapeDtypeStruct((rows, columns), jnp.bfloat16)
    out = pl.pallas_call(
        functools.partial(core_sum_kernel, n_x, len(after)),
        out_shape=[own] + [sent] * (n_x - 1),
        in_specs=[IN_VMEM, IN_VMEM] + [ANYWHERE] * len(after),
        out_specs=[IN_VMEM] * n_x,
        compiler_params=params(4),
        cost_estimate=SHORT,
    )(kept, received, *after)
    return out[0], out[1:]


def x_sum_kernel(counts, rows, places, *refs):
    sources, refs = [], list(refs)
    for count in counts:
        total = refs.pop(0)[...]
        for _ in range(count):
            total = total + refs.pop(0)[...].astype(jnp.float32)
        sources.append(total)
    for out_ref, parts in zip(refs, places):
        parts = [sources[unit][index * rows : (index + 1) * rows] for unit, index in parts]
        out_ref[...] = jnp.concatenate(parts, axis=0).astype(jnp.bfloat16)


def x_sum(sums, rows, places):
    columns = sums[0][0].shape[1]
    arrays = [array for total, received in sums for array in [total, *received]]
    counts = [len(received) for _, received in sums]
    blocks = [jax.ShapeDtypeStruct((rows * len(parts), columns), jnp.bfloat16) for parts in places]
    return pl.pallas_call(
        functools.partial(x_sum_kernel, counts, rows, places),
        out_shape=blocks,
        in_specs=[IN_VMEM] * len(arrays),
        out_specs=[IN_VMEM] * len(blocks),
        compiler_params=params(8),
        cost_estimate=SHORT,
    )(*arrays)


def place_kernel(counts, *refs):
    refs, out_ref = list(refs[:-1]), refs[-1]
    ctx = lax.axis_index("ctx")
    width = refs[0].shape[1]
    for offset, count in enumerate(counts):
        parts = [refs.pop(0)[...].astype(jnp.float32) for _ in range(count)]
        column = pl.multiple_of((ctx ^ offset) * width, 128)
        out_ref[:, pl.ds(column, width)] = jnp.concatenate(parts, axis=0).astype(jnp.bfloat16)


def place_columns(blocks):
    n_ctx = len(blocks)
    rows = sum(block.shape[0] for block in blocks[0])
    width = blocks[0][0].shape[1]
    if width % 128:
        ctx = lax.axis_index("ctx")
        out = jnp.zeros((rows, n_ctx * width), jnp.bfloat16)
        for offset, parts in enumerate(blocks):
            block = jnp.concatenate(parts, axis=0)
            out = lax.dynamic_update_slice(out, block, (0, (ctx ^ offset) * width))
        return out
    arrays = [block for parts in blocks for block in parts]
    return pl.pallas_call(
        functools.partial(place_kernel, [len(parts) for parts in blocks]),
        grid=(1,),
        out_shape=jax.ShapeDtypeStruct((rows, n_ctx * width), jnp.bfloat16),
        in_specs=[IN_VMEM] * len(arrays),
        out_specs=pl.BlockSpec((rows, n_ctx * width), lambda i: (0, 0)),
        compiler_params=params(4),
        cost_estimate=SHORT,
    )(*arrays)


def shards(n_ctx, n_head, queries, kv_rows, w_kv_up, w_out, stretch_order, prefix_len):
    query_rows = queries.shape[0]
    row_span = kv_rows.shape[0]
    cache_rows = row_span - query_rows
    half = row_span // 2
    n_x = n_head // 2
    pieces = chunk_rows(query_rows // n_head)
    core = lax.axis_index("head") % 2

    with jax.named_scope("keys_over_ctx"):
        kv_t = kv_rows.T
        own_half = jnp.where(core == 0, kv_t[:, :half], kv_t[:, half:])
        halves = [exchange(own_half, "ctx", n_ctx, offset) for offset in key_order(n_ctx)]
    with jax.named_scope("load"):
        q_ext, bias, w_values, own_keys = load(
            queries, w_kv_up, kv_t, stretch_order, prefix_len, n_head, pieces, cache_rows
        )
    with jax.named_scope("keys_over_cores"):
        leads = [cost(LEAD_KEYS)] * (n_ctx - 2) + [SHORT]
        halves = [tie(array, [own_keys], lead) for array, lead in zip(halves, leads)]
        others = [exchange(array, "head", n_head, 1) for array in halves]
    with jax.named_scope("attention"):
        first, *keys = attention(q_ext[0], bias[0], w_values, [own_keys] + halves + others, False)
        second, again = attention(q_ext[1], bias[1], w_values, keys, True)
    with jax.named_scope("attended_over_ctx"):
        early = gather_pieces(first, first, n_ctx, [second], cost(LEAD_EARLY), SHORT)
        again = tie(again, [early[n_ctx // 2]])
        late = gather_pieces(second, again, n_ctx, [early[n_ctx - 1]], cost(LEAD_NEAR), cost(LEAD_LATE))
    powers = [1 << bit for bit in range(n_ctx.bit_length() - 1)]
    handed = [offset for offset in range(1, n_ctx) if offset not in powers]
    gathered = [early, late]
    units = [
        [(0, 0), (1, 0)],
        [(0, offset) for offset in range(1, n_ctx)],
        [(1, offset) for offset in powers],
        [(1, offset) for offset in handed],
    ]
    sums = []
    for unit, members in enumerate(units):
        with jax.named_scope("out_product"):
            if unit == 3:
                for offset in handed:
                    late[offset] = tie(late[offset], sums[1][1], cost(LEAD_HANDED))
            sources = [gathered[chunk][offset] for chunk, offset in members]
            after = [second, *sums[0][1]] if unit == 1 else []
            if unit == 2:
                after = [sums[1][0]]
            sent, kept = product(sources, w_out, n_x, after)
        with jax.named_scope("sum_over_cores"):
            if unit == 3:
                sent = tie(sent, [sums[2][0]])
            total, sent = core_sum(kept, exchange(sent, "head", n_head, 1), [])
        with jax.named_scope("sum_over_x"):
            if unit == 3:
                before = sums[1][1]
                sent = [tie(array, before, cost(LEAD_X)) for array in sent]
            crossed = [exchange(array, "head", n_head, 2 * d) for d, array in enumerate(sent, 1)]
        sums.append((total, crossed))
    def added(units_in, offsets, parts_of):
        with jax.named_scope("sum_over_x"):
            places = [parts_of(offset) for offset in offsets]
            found = x_sum([sums[unit] for unit in units_in], pieces[0], places)
        with jax.named_scope("columns_over_ctx"):
            return [
                exchange(block, "ctx", n_ctx, offset) if offset else block
                for offset, block in zip(offsets, found)
            ]

    blocks = {0: added([0], [0], lambda offset: [(0, 0), (0, 1)])}
    ahead = added([1], handed, lambda offset: [(0, offset - 1)])
    ahead = [tie(block, [], cost(LEAD_AHEAD)) for block in ahead]
    both = added([1, 2], powers, lambda offset: [(0, offset - 1), (1, powers.index(offset))])
    behind = added([3], handed, lambda offset: [(0, handed.index(offset))])
    blocks.update({offset: [block] for offset, block in zip(powers, both)})
    for offset, first_rows, last_rows in zip(handed, ahead, behind):
        blocks[offset] = [first_rows, last_rows]
    with jax.named_scope("output"):
        return place_columns([blocks[d] for d in range(n_ctx)])


def solution(mesh):
    placed = (
        P(("groups", "ctx"), "head"),
        P(("groups", "ctx"), None),
        P(None, "head"),
        P("head", "ctx"),
        P("groups"),
        P("groups"),
    )
    return jax.shard_map(
        functools.partial(shards, mesh.shape["ctx"], mesh.shape["head"]),
        mesh=mesh,
        in_specs=placed,
        out_specs=P(("groups", "ctx", "head"), None),
        check_vma=False,
    )
```

```python
import functools
import math

import jax
import jax.numpy as jnp
from jax import lax
from jax.experimental import pallas as pl
from jax.experimental.pallas import tpu as pltpu
from jax.sharding import PartitionSpec as P

LAT = 512
NOPE = 128
ROPE = 64
VD = 128
HEAD = NOPE + ROPE
PROJ = NOPE + VD
SUB_ROWS = 512
ABSORB_LIMIT = 56
LOAD_LIMIT = 44
MASKED = -1e30
LEAD_EARLY = 6
LEAD_NEAR = 2
LEAD_LATE = 3
LEAD_HANDED = 3
LEAD_AHEAD = 3
LEAD_X = 1
LOG2E = 1.4426950408889634
SCALE = LOG2E / math.sqrt(HEAD)


def cost(microseconds):
    return pl.CostEstimate(
        flops=int(1e9 * microseconds), bytes_accessed=int(3e6 * microseconds), transcendentals=0
    )


SHORT = pl.CostEstimate(flops=1024, bytes_accessed=1024, transcendentals=0)
IN_VMEM = pl.BlockSpec(memory_space=pltpu.VMEM)
IN_SMEM = pl.BlockSpec(memory_space=pltpu.SMEM)
IN_HBM = pl.BlockSpec(memory_space=pltpu.HBM)
ANYWHERE = pl.BlockSpec(memory_space=pl.ANY)


def chunk_rows(owned):
    return (owned // 2, owned // 2)


def params(mebibytes):
    return pltpu.CompilerParams(vmem_limit_bytes=mebibytes * 1024 * 1024)


def exchange(array, axis, size, bit):
    return lax.ppermute(array, axis, [(i, i ^ bit) for i in range(size)])


def tie_kernel(*refs):
    pass


def tie(array, after, lead=SHORT):
    return pl.pallas_call(
        tie_kernel,
        out_shape=jax.ShapeDtypeStruct(array.shape, array.dtype),
        in_specs=[ANYWHERE] * (1 + len(after)),
        out_specs=ANYWHERE,
        input_output_aliases={0: 0},
        compiler_params=params(1),
        cost_estimate=lead,
    )(array, *after)


def gather_pieces(own, near, size, after, lead, far_lead):
    pieces = {0: own, 1: tie(exchange(near, "ctx", size, 1), [], lead)}
    bit = size // 2
    while bit > 1:
        pieces[bit] = exchange(own, "ctx", size, bit)
        bit //= 2
    bit = 2
    while bit < size:
        for offset in range(bit + 1, 2 * bit):
            if offset == bit + 1:
                pieces[bit] = tie(pieces[bit], after, far_lead)
            pieces[offset] = exchange(pieces[bit], "ctx", size, offset ^ bit)
        bit *= 2
    return [pieces[offset] for offset in range(size)]


def absorb_kernel(owners, pieces, first, q_hbm, up_hbm, *refs):
    count = len(pieces)
    q_exts, (q_ref, key_ref, q_sem, key_sems) = refs[:count], refs[count:]
    rows = q_ref.shape[0]
    head_count = key_ref.shape[0]
    window = pl.ds(first * HEAD, head_count * HEAD)
    q_copy = pltpu.make_async_copy(q_hbm.at[:, window], q_ref, q_sem)
    q_copy.start()
    key_copies = []
    for head in range(head_count):
        source = up_hbm.at[:, pl.ds((first + head) * PROJ, NOPE)]
        key_copies.append(pltpu.make_async_copy(source, key_ref.at[head], key_sems.at[head]))
        key_copies[-1].start()
    q_copy.wait()
    for head in range(head_count):
        nope = q_ref[:, head * HEAD : head * HEAD + NOPE]
        rope = q_ref[:, head * HEAD + NOPE : (head + 1) * HEAD].astype(jnp.float32) * SCALE
        key_copies[head].wait()
        absorbed = lax.dot_general(
            nope, key_ref[head], (((1,), (1,)), ((), ())), preferred_element_type=jnp.float32
        )
        absorbed = (absorbed * SCALE).reshape(owners, rows // owners, LAT)
        rope = rope.reshape(owners, rows // owners, ROPE)
        start = 0
        for piece, q_ext in zip(pieces, q_exts):
            part = absorbed[:, start : start + piece].reshape(owners * piece, LAT)
            q_ext[head, :, :LAT] = part.astype(jnp.bfloat16)
            part = rope[:, start : start + piece].reshape(owners * piece, ROPE)
            q_ext[head, :, LAT:] = part.astype(jnp.bfloat16)
            start += piece


def load_kernel(owners, pieces, cache_rows, first, order_ref, prefix_ref, q_hbm, up_hbm, own_hbm, *refs):
    count = len(pieces)
    q_exts, biases, refs = refs[:count], refs[count : 2 * count], refs[2 * count :]
    value_ref, own_ref, q_ref, key_ref, q_sem, key_sems, own_sem, value_sems = refs
    copies = [pltpu.make_async_copy(own_hbm, own_ref, own_sem)]
    for head in range(value_ref.shape[0]):
        source = up_hbm.at[:, pl.ds(head * PROJ + NOPE, VD)]
        copies.append(pltpu.make_async_copy(source, value_ref.at[head], value_sems.at[head]))
    for copy in copies:
        copy.start()
    start = 0
    for piece, bias_ref in zip(pieces, biases):
        visible_bias(
            order_ref, prefix_ref, bias_ref, q_ref.shape[0], owners, start, own_hbm.shape[1], cache_rows
        )
        start += piece
    absorb_kernel(owners, pieces, first, q_hbm, up_hbm, *q_exts, q_ref, key_ref, q_sem, key_sems)
    for copy in copies:
        copy.wait()


def absorb_shapes(queries, head_count, owners, pieces):
    results = [
        jax.ShapeDtypeStruct((head_count, owners * piece, LAT + ROPE), jnp.bfloat16)
        for piece in pieces
    ]
    scratch = [
        pltpu.VMEM((queries.shape[0], head_count * HEAD), jnp.bfloat16),
        pltpu.VMEM((head_count, LAT, NOPE), jnp.bfloat16),
        pltpu.SemaphoreType.DMA,
        pltpu.SemaphoreType.DMA((head_count,)),
    ]
    return results, scratch


def absorb(queries, w_kv_up, owners, pieces):
    half = w_kv_up.shape[1] // PROJ // 2
    results, scratch = absorb_shapes(queries, half, owners, pieces)
    return pl.pallas_call(
        functools.partial(absorb_kernel, owners, pieces, 0),
        out_shape=results,
        in_specs=[IN_HBM] * 2,
        out_specs=[IN_VMEM] * len(results),
        scratch_shapes=scratch,
        compiler_params=params(ABSORB_LIMIT),
        cost_estimate=SHORT,
    )(queries, w_kv_up)


def load(queries, w_kv_up, own_keys, stretch_order, prefix_len, owners, pieces, cache_rows):
    head_count = w_kv_up.shape[1] // PROJ
    half = head_count // 2
    amount = stretch_order.shape[0] * own_keys.shape[1]
    results, scratch = absorb_shapes(queries, half, owners, pieces)
    results += [jax.ShapeDtypeStruct((owners * piece, amount), jnp.float32) for piece in pieces]
    results += [
        jax.ShapeDtypeStruct((head_count, LAT, VD), jnp.bfloat16),
        jax.ShapeDtypeStruct(own_keys.shape, jnp.bfloat16),
    ]
    scratch += [pltpu.SemaphoreType.DMA, pltpu.SemaphoreType.DMA((head_count,))]
    out = pl.pallas_call(
        functools.partial(load_kernel, owners, pieces, cache_rows, half),
        out_shape=results,
        in_specs=[IN_SMEM, IN_SMEM] + [IN_HBM] * 3,
        out_specs=[IN_VMEM] * len(results),
        scratch_shapes=scratch,
        compiler_params=params(LOAD_LIMIT),
        cost_estimate=SHORT,
    )(stretch_order, prefix_len, queries, w_kv_up, own_keys)
    count = len(pieces)
    return out[:count], out[count : 2 * count], *out[2 * count :]


def visible_bias(order_ref, prefix_ref, bias_ref, query_rows, owners, start, row_span, cache_rows):
    n_ctx = order_ref.shape[0]
    half = row_span // 2
    rows = bias_ref.shape[0]
    piece = rows // owners
    own = lax.axis_index("ctx")
    core = lax.axis_index("head") % 2
    blocks = [(0, 0), (0, 1)]
    blocks += [(offset, core) for offset in range(1, n_ctx)]
    blocks += [(offset, 1 - core) for offset in range(1, n_ctx)]
    row = lax.broadcasted_iota(jnp.int32, (rows, half), 0)
    column = lax.broadcasted_iota(jnp.int32, (rows, half), 1)
    within_own = row // piece * (query_rows // owners) + start + row % piece
    query_pos = order_ref[own] * query_rows + within_own
    for index, (offset, second) in enumerate(blocks):
        source = own ^ offset
        within = second * half + column
        cache_pos = jnp.where(
            source * cache_rows + within < prefix_ref[0], -1, n_ctx * query_rows
        )
        key_pos = order_ref[source] * query_rows + within - cache_rows
        first_seen = jnp.where(within < cache_rows, cache_pos, key_pos)
        bias = jnp.where(first_seen <= query_pos, 0.0, MASKED).astype(jnp.float32)
        bias_ref[:, index * half : (index + 1) * half] = bias


def attention_kernel(count, low_ref, high_ref, bias_ref, value_ref, *refs):
    part, rows, depth = low_ref.shape
    heads = 2 * part
    if count:
        piece_refs, (out_ref, keys_ref, latent_ref) = refs[:count], refs[count:]
        start = 0
        for piece_ref in piece_refs:
            width = piece_ref.shape[1]
            keys_ref[:, start : start + width] = piece_ref[...]
            latent_ref[start : start + width, :] = piece_ref[:LAT, :].T
            start += width
    else:
        keys_ref, latent_ref, out_ref, copy_ref = refs
    amount = keys_ref.shape[1]
    group = max(1, min(part, SUB_ROWS // rows))
    size = group * rows

    def score(first):
        q_ref = low_ref if first < part else high_ref
        queries = q_ref[first % part : first % part + group].reshape(size, depth)
        return jnp.dot(queries, keys_ref[...], preferred_element_type=jnp.float32)

    scores = score(0)
    for first in range(0, heads, group):
        later = score(first + group) if first + group < heads else None
        scores = scores.reshape(group, rows, amount) + bias_ref[...][None]
        top = jnp.max(scores, axis=2, keepdims=True)
        weights = jnp.exp2(scores - top)
        total = jnp.sum(weights, axis=2, keepdims=True).reshape(size, 1)
        mixed = jnp.dot(
            weights.reshape(size, amount).astype(jnp.bfloat16),
            latent_ref[...],
            preferred_element_type=jnp.float32,
        )
        mixed = (mixed / total).astype(jnp.bfloat16)
        for head in range(first, first + group):
            result = jnp.dot(
                mixed[(head - first) * rows : (head - first + 1) * rows],
                value_ref[head],
                preferred_element_type=jnp.float32,
            )
            out_ref[:, head * VD : (head + 1) * VD] = result.astype(jnp.bfloat16)
            if not count:
                copy_ref[:, head * VD : (head + 1) * VD] = result.astype(jnp.bfloat16)
        scores = later


def attention(q_ext, bias, w_values, keys, gathered):
    part, rows, depth = q_ext[0].shape
    head_count = 2 * part
    amount = bias.shape[1]
    out_shape = [jax.ShapeDtypeStruct((rows, head_count * VD), jnp.bfloat16)]
    if gathered:
        out_shape *= 2
    else:
        out_shape.append(jax.ShapeDtypeStruct((depth, amount), jnp.bfloat16))
        out_shape.append(jax.ShapeDtypeStruct((amount, LAT), jnp.bfloat16))
    return pl.pallas_call(
        functools.partial(attention_kernel, 0 if gathered else len(keys)),
        out_shape=out_shape,
        in_specs=[IN_VMEM] * (4 + len(keys)),
        out_specs=[IN_VMEM] * len(out_shape),
        compiler_params=params(16 if amount <= 1024 else 40),
        cost_estimate=SHORT,
    )(*q_ext, bias, w_values, *keys)


def product_kernel(count, n_x, after, weight_ref, *refs):
    piece_refs = refs[:count]
    sent_ref, kept_ref, rows_ref = refs[count + after :]
    rows = piece_refs[0].shape[0]
    columns = weight_ref.shape[1]
    for index, piece_ref in enumerate(piece_refs):
        rows_ref[index * rows : (index + 1) * rows, :] = piece_ref[...]
    is_first = lax.axis_index("head") % 2 == 0
    width = 256 if columns % 256 == 0 else columns
    for start in range(0, columns, width):
        span = slice(start, start + width)
        result = jnp.dot(rows_ref[...], weight_ref[:, span], preferred_element_type=jnp.float32)
        result = result.reshape(count, n_x, 2, rows // (2 * n_x), width)
        for x in range(n_x):
            first = result[:, x, 0].reshape(rows * count // (2 * n_x), width)
            second = result[:, x, 1].reshape(rows * count // (2 * n_x), width)
            sent_ref[x, :, span] = jnp.where(is_first, second, first).astype(jnp.bfloat16)
            kept_ref[x, :, span] = jnp.where(is_first, first, second)


def product(pieces, w_out, n_x, after):
    rows, depth = pieces[0].shape
    count = len(pieces)
    shape = (n_x, count * rows // (2 * n_x), w_out.shape[1])
    return pl.pallas_call(
        functools.partial(product_kernel, count, n_x, len(after)),
        out_shape=[jax.ShapeDtypeStruct(shape, jnp.bfloat16), jax.ShapeDtypeStruct(shape, jnp.float32)],
        in_specs=[IN_VMEM] * (1 + count) + [ANYWHERE] * len(after),
        out_specs=[IN_VMEM, IN_VMEM],
        scratch_shapes=[pltpu.VMEM((count * rows, depth), jnp.bfloat16)],
        compiler_params=params(16),
        cost_estimate=SHORT,
    )(w_out, *pieces, *after)


def core_sum_kernel(n_x, after, kept_ref, received_ref, *refs):
    total_ref, *sent_refs = refs[after:]
    x = lax.axis_index("head") // 2
    for offset in range(n_x):
        summed = kept_ref[x ^ offset] + received_ref[x ^ offset].astype(jnp.float32)
        if offset:
            sent_refs[offset - 1][...] = summed.astype(jnp.bfloat16)
        else:
            total_ref[...] = summed


def core_sum(kept, received, after):
    n_x, rows, columns = kept.shape
    own = jax.ShapeDtypeStruct((rows, columns), jnp.float32)
    sent = jax.ShapeDtypeStruct((rows, columns), jnp.bfloat16)
    out = pl.pallas_call(
        functools.partial(core_sum_kernel, n_x, len(after)),
        out_shape=[own] + [sent] * (n_x - 1),
        in_specs=[IN_VMEM, IN_VMEM] + [ANYWHERE] * len(after),
        out_specs=[IN_VMEM] * n_x,
        compiler_params=params(4),
        cost_estimate=SHORT,
    )(kept, received, *after)
    return out[0], out[1:]


def x_sum_kernel(counts, rows, places, *refs):
    sources, refs = [], list(refs)
    for count in counts:
        total = refs.pop(0)[...]
        for _ in range(count):
            total = total + refs.pop(0)[...].astype(jnp.float32)
        sources.append(total)
    for out_ref, parts in zip(refs, places):
        parts = [sources[unit][index * rows : (index + 1) * rows] for unit, index in parts]
        out_ref[...] = jnp.concatenate(parts, axis=0).astype(jnp.bfloat16)


def x_sum(sums, rows, places):
    columns = sums[0][0].shape[1]
    arrays = [array for total, received in sums for array in [total, *received]]
    counts = [len(received) for _, received in sums]
    blocks = [jax.ShapeDtypeStruct((rows * len(parts), columns), jnp.bfloat16) for parts in places]
    return pl.pallas_call(
        functools.partial(x_sum_kernel, counts, rows, places),
        out_shape=blocks,
        in_specs=[IN_VMEM] * len(arrays),
        out_specs=[IN_VMEM] * len(blocks),
        compiler_params=params(8),
        cost_estimate=SHORT,
    )(*arrays)


def place_kernel(counts, *refs):
    refs, out_ref = list(refs[:-1]), refs[-1]
    ctx = lax.axis_index("ctx")
    width = refs[0].shape[1]
    for offset, count in enumerate(counts):
        parts = [refs.pop(0)[...].astype(jnp.float32) for _ in range(count)]
        column = pl.multiple_of((ctx ^ offset) * width, 128)
        out_ref[:, pl.ds(column, width)] = jnp.concatenate(parts, axis=0).astype(jnp.bfloat16)


def place_columns(blocks):
    n_ctx = len(blocks)
    rows = sum(block.shape[0] for block in blocks[0])
    width = blocks[0][0].shape[1]
    if width % 128:
        ctx = lax.axis_index("ctx")
        out = jnp.zeros((rows, n_ctx * width), jnp.bfloat16)
        for offset, parts in enumerate(blocks):
            block = jnp.concatenate(parts, axis=0)
            out = lax.dynamic_update_slice(out, block, (0, (ctx ^ offset) * width))
        return out
    arrays = [block for parts in blocks for block in parts]
    return pl.pallas_call(
        functools.partial(place_kernel, [len(parts) for parts in blocks]),
        grid=(1,),
        out_shape=jax.ShapeDtypeStruct((rows, n_ctx * width), jnp.bfloat16),
        in_specs=[IN_VMEM] * len(arrays),
        out_specs=pl.BlockSpec((rows, n_ctx * width), lambda i: (0, 0)),
        compiler_params=params(4),
        cost_estimate=SHORT,
    )(*arrays)


def shards(n_ctx, n_head, queries, kv_rows, w_kv_up, w_out, stretch_order, prefix_len):
    query_rows = queries.shape[0]
    row_span = kv_rows.shape[0]
    cache_rows = row_span - query_rows
    half = row_span // 2
    n_x = n_head // 2
    pieces = chunk_rows(query_rows // n_head)
    core = lax.axis_index("head") % 2

    with jax.named_scope("keys_over_ctx"):
        kv_t = kv_rows.T
        own_half = jnp.where(core == 0, kv_t[:, :half], kv_t[:, half:])
        halves = {}
        for bit in reversed(range(n_ctx.bit_length() - 1)):
            halves[1 << bit] = exchange(own_half, "ctx", n_ctx, 1 << bit)
    with jax.named_scope("load"):
        low = absorb(queries, w_kv_up, n_head, pieces)
    with jax.named_scope("keys_over_ctx"):
        direct = list(halves)
        for offset in direct:
            halves[offset] = tie(halves[offset], low[:1])
        for offset in range(3, n_ctx):
            near = 1 << (offset.bit_length() - 1)
            if offset != near:
                halves[offset] = exchange(halves[near], "ctx", n_ctx, offset ^ near)
    with jax.named_scope("load"):
        high, bias, w_values, own_keys = load(
            queries, w_kv_up, kv_t, stretch_order, prefix_len, n_head, pieces, cache_rows
        )
        q_ext = list(zip(low, high))
    with jax.named_scope("keys_over_cores"):
        for offset in range(3, n_ctx):
            if offset not in direct:
                halves[offset] = tie(halves[offset], [own_keys])
        halves = [halves[offset] for offset in range(1, n_ctx)]
        others = [exchange(array, "head", n_head, 1) for array in halves]
    with jax.named_scope("attention"):
        first, *keys = attention(q_ext[0], bias[0], w_values, [own_keys] + halves + others, False)
        second, again = attention(q_ext[1], bias[1], w_values, keys, True)
    with jax.named_scope("attended_over_ctx"):
        early = gather_pieces(first, first, n_ctx, [second], cost(LEAD_EARLY), SHORT)
        again = tie(again, [early[n_ctx // 2]])
        late = gather_pieces(second, again, n_ctx, [early[n_ctx - 1]], cost(LEAD_NEAR), cost(LEAD_LATE))
    powers = [1 << bit for bit in range(n_ctx.bit_length() - 1)]
    handed = [offset for offset in range(1, n_ctx) if offset not in powers]
    gathered = [early, late]
    units = [
        [(0, 0), (1, 0)],
        [(0, offset) for offset in range(1, n_ctx)],
        [(1, offset) for offset in powers],
        [(1, offset) for offset in handed],
    ]
    sums = []
    for unit, members in enumerate(units):
        with jax.named_scope("out_product"):
            if unit == 3:
                for offset in handed:
                    late[offset] = tie(late[offset], sums[1][1], cost(LEAD_HANDED))
            sources = [gathered[chunk][offset] for chunk, offset in members]
            after = [second, *sums[0][1]] if unit == 1 else []
            if unit == 2:
                after = [sums[1][0]]
            sent, kept = product(sources, w_out, n_x, after)
        with jax.named_scope("sum_over_cores"):
            if unit == 3:
                sent = tie(sent, [sums[2][0]])
            total, sent = core_sum(kept, exchange(sent, "head", n_head, 1), [])
        with jax.named_scope("sum_over_x"):
            if unit == 3:
                before = sums[1][1]
                sent = [tie(array, before, cost(LEAD_X)) for array in sent]
            crossed = [exchange(array, "head", n_head, 2 * d) for d, array in enumerate(sent, 1)]
        sums.append((total, crossed))
    def added(units_in, offsets, parts_of):
        with jax.named_scope("sum_over_x"):
            places = [parts_of(offset) for offset in offsets]
            found = x_sum([sums[unit] for unit in units_in], pieces[0], places)
        with jax.named_scope("columns_over_ctx"):
            return [
                exchange(block, "ctx", n_ctx, offset) if offset else block
                for offset, block in zip(offsets, found)
            ]

    blocks = {0: added([0], [0], lambda offset: [(0, 0), (0, 1)])}
    ahead = added([1], handed, lambda offset: [(0, offset - 1)])
    ahead = [tie(block, [], cost(LEAD_AHEAD)) for block in ahead]
    both = added([1, 2], powers, lambda offset: [(0, offset - 1), (1, powers.index(offset))])
    behind = added([3], handed, lambda offset: [(0, handed.index(offset))])
    blocks.update({offset: [block] for offset, block in zip(powers, both)})
    for offset, first_rows, last_rows in zip(handed, ahead, behind):
        blocks[offset] = [first_rows, last_rows]
    with jax.named_scope("output"):
        return place_columns([blocks[d] for d in range(n_ctx)])


def solution(mesh):
    placed = (
        P(("groups", "ctx"), "head"),
        P(("groups", "ctx"), None),
        P(None, "head"),
        P("head", "ctx"),
        P("groups"),
        P("groups"),
    )
    return jax.shard_map(
        functools.partial(shards, mesh.shape["ctx"], mesh.shape["head"]),
        mesh=mesh,
        in_specs=placed,
        out_specs=P(("groups", "ctx", "head"), None),
        check_vma=False,
    )
```

```python
import functools
import math

import jax
import jax.numpy as jnp
from jax import lax
from jax.experimental import pallas as pl
from jax.experimental.pallas import tpu as pltpu
from jax.sharding import PartitionSpec as P

LAT = 512
NOPE = 128
ROPE = 64
VD = 128
HEAD = NOPE + ROPE
PROJ = NOPE + VD
SUB_ROWS = 512
LOAD_LIMIT = 44
MASKED = -1e30
LEAD_EARLY = 6
LEAD_NEAR = 2
LEAD_LATE = 3
LEAD_HANDED = 3
LEAD_AHEAD = 1
LEAD_X = 1
LOG2E = 1.4426950408889634
SCALE = LOG2E / math.sqrt(HEAD)


def cost(microseconds):
    return pl.CostEstimate(
        flops=int(1e9 * microseconds), bytes_accessed=int(3e6 * microseconds), transcendentals=0
    )


SHORT = pl.CostEstimate(flops=1024, bytes_accessed=1024, transcendentals=0)
IN_VMEM = pl.BlockSpec(memory_space=pltpu.VMEM)
IN_SMEM = pl.BlockSpec(memory_space=pltpu.SMEM)
IN_HBM = pl.BlockSpec(memory_space=pltpu.HBM)
ANYWHERE = pl.BlockSpec(memory_space=pl.ANY)


def chunk_rows(owned):
    return (owned // 2, owned // 2)


def params(mebibytes):
    return pltpu.CompilerParams(vmem_limit_bytes=mebibytes * 1024 * 1024)


def exchange(array, axis, size, bit):
    return lax.ppermute(array, axis, [(i, i ^ bit) for i in range(size)])


def tie_kernel(*refs):
    pass


def tie(array, after, lead=SHORT):
    return pl.pallas_call(
        tie_kernel,
        out_shape=jax.ShapeDtypeStruct(array.shape, array.dtype),
        in_specs=[ANYWHERE] * (1 + len(after)),
        out_specs=ANYWHERE,
        input_output_aliases={0: 0},
        compiler_params=params(1),
        cost_estimate=lead,
    )(array, *after)


def gather_pieces(own, near, size, after, lead, far_lead):
    pieces = {0: own, 1: tie(exchange(near, "ctx", size, 1), [], lead)}
    bit = size // 2
    while bit > 1:
        pieces[bit] = exchange(own, "ctx", size, bit)
        bit //= 2
    bit = 2
    while bit < size:
        for offset in range(bit + 1, 2 * bit):
            if offset == bit + 1:
                pieces[bit] = tie(pieces[bit], after, far_lead)
            pieces[offset] = exchange(pieces[bit], "ctx", size, offset ^ bit)
        bit *= 2
    return [pieces[offset] for offset in range(size)]


def load_kernel(owners, pieces, cache_rows, order_ref, prefix_ref, q_hbm, up_hbm, own_hbm, *refs):
    count = len(pieces)
    q_exts, biases, refs = refs[:count], refs[count : 2 * count], refs[2 * count :]
    value_ref, own_ref, q_ref, key_ref, sems, key_sems, value_sems = refs
    rows = q_ref.shape[0]
    head_count = key_ref.shape[0]
    q_copy = pltpu.make_async_copy(q_hbm, q_ref, sems.at[0])
    own_copy = pltpu.make_async_copy(own_hbm, own_ref, sems.at[1])
    q_copy.start()
    key_copies, value_copies = [], []
    for head in range(head_count):
        source = up_hbm.at[:, pl.ds(head * PROJ, NOPE)]
        key_copies.append(pltpu.make_async_copy(source, key_ref.at[head], key_sems.at[head]))
        source = up_hbm.at[:, pl.ds(head * PROJ + NOPE, VD)]
        value_copies.append(pltpu.make_async_copy(source, value_ref.at[head], value_sems.at[head]))
    for copy in key_copies + [own_copy] + value_copies:
        copy.start()
    start = 0
    for piece, bias_ref in zip(pieces, biases):
        visible_bias(
            order_ref, prefix_ref, bias_ref, rows, owners, start, own_hbm.shape[1], cache_rows
        )
        start += piece
    q_copy.wait()
    for head in range(head_count):
        nope = q_ref[:, head * HEAD : head * HEAD + NOPE]
        rope = q_ref[:, head * HEAD + NOPE : (head + 1) * HEAD].astype(jnp.float32) * SCALE
        key_copies[head].wait()
        absorbed = lax.dot_general(
            nope, key_ref[head], (((1,), (1,)), ((), ())), preferred_element_type=jnp.float32
        )
        absorbed = (absorbed * SCALE).reshape(owners, rows // owners, LAT)
        rope = rope.reshape(owners, rows // owners, ROPE)
        start = 0
        for piece, q_ext in zip(pieces, q_exts):
            part = absorbed[:, start : start + piece].reshape(owners * piece, LAT)
            q_ext[head, :, :LAT] = part.astype(jnp.bfloat16)
            part = rope[:, start : start + piece].reshape(owners * piece, ROPE)
            q_ext[head, :, LAT:] = part.astype(jnp.bfloat16)
            start += piece
    for copy in [own_copy] + value_copies:
        copy.wait()


def load(queries, w_kv_up, own_keys, stretch_order, prefix_len, owners, pieces, cache_rows):
    head_count = w_kv_up.shape[1] // PROJ
    amount = stretch_order.shape[0] * own_keys.shape[1]
    out_shape = [
        jax.ShapeDtypeStruct((head_count, owners * piece, LAT + ROPE), jnp.bfloat16)
        for piece in pieces
    ]
    out_shape += [jax.ShapeDtypeStruct((owners * piece, amount), jnp.float32) for piece in pieces]
    out_shape += [
        jax.ShapeDtypeStruct((head_count, LAT, VD), jnp.bfloat16),
        jax.ShapeDtypeStruct(own_keys.shape, jnp.bfloat16),
    ]
    out = pl.pallas_call(
        functools.partial(load_kernel, owners, pieces, cache_rows),
        out_shape=out_shape,
        in_specs=[IN_SMEM, IN_SMEM] + [IN_HBM] * 3,
        out_specs=[IN_VMEM] * len(out_shape),
        scratch_shapes=[
            pltpu.VMEM(queries.shape, jnp.bfloat16),
            pltpu.VMEM((head_count, LAT, NOPE), jnp.bfloat16),
            pltpu.SemaphoreType.DMA((2,)),
            pltpu.SemaphoreType.DMA((head_count,)),
            pltpu.SemaphoreType.DMA((head_count,)),
        ],
        compiler_params=params(LOAD_LIMIT),
        cost_estimate=SHORT,
    )(stretch_order, prefix_len, queries, w_kv_up, own_keys)
    count = len(pieces)
    return out[:count], out[count : 2 * count], *out[2 * count :]


def visible_bias(order_ref, prefix_ref, bias_ref, query_rows, owners, start, row_span, cache_rows):
    n_ctx = order_ref.shape[0]
    half = row_span // 2
    rows = bias_ref.shape[0]
    piece = rows // owners
    own = lax.axis_index("ctx")
    core = lax.axis_index("head") % 2
    blocks = [(0, 0), (0, 1)]
    blocks += [(offset, core) for offset in range(1, n_ctx)]
    blocks += [(offset, 1 - core) for offset in range(1, n_ctx)]
    row = lax.broadcasted_iota(jnp.int32, (rows, half), 0)
    column = lax.broadcasted_iota(jnp.int32, (rows, half), 1)
    within_own = row // piece * (query_rows // owners) + start + row % piece
    query_pos = order_ref[own] * query_rows + within_own
    for index, (offset, second) in enumerate(blocks):
        source = own ^ offset
        within = second * half + column
        cache_pos = jnp.where(
            source * cache_rows + within < prefix_ref[0], -1, n_ctx * query_rows
        )
        key_pos = order_ref[source] * query_rows + within - cache_rows
        first_seen = jnp.where(within < cache_rows, cache_pos, key_pos)
        bias = jnp.where(first_seen <= query_pos, 0.0, MASKED).astype(jnp.float32)
        bias_ref[:, index * half : (index + 1) * half] = bias


def attention_kernel(count, q_ref, bias_ref, value_ref, *refs):
    heads, rows, depth = q_ref.shape
    if count:
        piece_refs, (out_ref, keys_ref, latent_ref) = refs[:count], refs[count:]
        start = 0
        for piece_ref in piece_refs:
            width = piece_ref.shape[1]
            keys_ref[:, start : start + width] = piece_ref[...]
            latent_ref[start : start + width, :] = piece_ref[:LAT, :].T
            start += width
    else:
        keys_ref, latent_ref, out_ref, copy_ref = refs
    amount = keys_ref.shape[1]
    group = max(1, min(heads, SUB_ROWS // rows))
    size = group * rows

    def score(first):
        queries = q_ref[first : first + group].reshape(size, depth)
        return jnp.dot(queries, keys_ref[...], preferred_element_type=jnp.float32)

    scores = score(0)
    for first in range(0, heads, group):
        later = score(first + group) if first + group < heads else None
        scores = scores.reshape(group, rows, amount) + bias_ref[...][None]
        top = jnp.max(scores, axis=2, keepdims=True)
        weights = jnp.exp2(scores - top)
        total = jnp.sum(weights, axis=2, keepdims=True).reshape(size, 1)
        mixed = jnp.dot(
            weights.reshape(size, amount).astype(jnp.bfloat16),
            latent_ref[...],
            preferred_element_type=jnp.float32,
        )
        mixed = (mixed / total).astype(jnp.bfloat16)
        for head in range(first, first + group):
            result = jnp.dot(
                mixed[(head - first) * rows : (head - first + 1) * rows],
                value_ref[head],
                preferred_element_type=jnp.float32,
            )
            out_ref[:, head * VD : (head + 1) * VD] = result.astype(jnp.bfloat16)
            if not count:
                copy_ref[:, head * VD : (head + 1) * VD] = result.astype(jnp.bfloat16)
        scores = later


def attention(q_ext, bias, w_values, keys, gathered):
    head_count, rows, depth = q_ext.shape
    amount = bias.shape[1]
    out_shape = [jax.ShapeDtypeStruct((rows, head_count * VD), jnp.bfloat16)]
    if gathered:
        out_shape *= 2
    else:
        out_shape.append(jax.ShapeDtypeStruct((depth, amount), jnp.bfloat16))
        out_shape.append(jax.ShapeDtypeStruct((amount, LAT), jnp.bfloat16))
    return pl.pallas_call(
        functools.partial(attention_kernel, 0 if gathered else len(keys)),
        out_shape=out_shape,
        in_specs=[IN_VMEM] * (3 + len(keys)),
        out_specs=[IN_VMEM] * len(out_shape),
        compiler_params=params(16 if amount <= 1024 else 40),
        cost_estimate=SHORT,
    )(q_ext, bias, w_values, *keys)


def product_kernel(count, n_x, after, weight_ref, *refs):
    piece_refs = refs[:count]
    sent_ref, kept_ref, rows_ref = refs[count + after :]
    rows = piece_refs[0].shape[0]
    columns = weight_ref.shape[1]
    for index, piece_ref in enumerate(piece_refs):
        rows_ref[index * rows : (index + 1) * rows, :] = piece_ref[...]
    is_first = lax.axis_index("head") % 2 == 0
    width = 256 if columns % 256 == 0 else columns
    for start in range(0, columns, width):
        span = slice(start, start + width)
        result = jnp.dot(rows_ref[...], weight_ref[:, span], preferred_element_type=jnp.float32)
        result = result.reshape(count, n_x, 2, rows // (2 * n_x), width)
        for x in range(n_x):
            first = result[:, x, 0].reshape(rows * count // (2 * n_x), width)
            second = result[:, x, 1].reshape(rows * count // (2 * n_x), width)
            sent_ref[x, :, span] = jnp.where(is_first, second, first).astype(jnp.bfloat16)
            kept_ref[x, :, span] = jnp.where(is_first, first, second)


def product(pieces, w_out, n_x, after):
    rows, depth = pieces[0].shape
    count = len(pieces)
    shape = (n_x, count * rows // (2 * n_x), w_out.shape[1])
    return pl.pallas_call(
        functools.partial(product_kernel, count, n_x, len(after)),
        out_shape=[jax.ShapeDtypeStruct(shape, jnp.bfloat16), jax.ShapeDtypeStruct(shape, jnp.float32)],
        in_specs=[IN_VMEM] * (1 + count) + [ANYWHERE] * len(after),
        out_specs=[IN_VMEM, IN_VMEM],
        scratch_shapes=[pltpu.VMEM((count * rows, depth), jnp.bfloat16)],
        compiler_params=params(16),
        cost_estimate=SHORT,
    )(w_out, *pieces, *after)


def core_sum_kernel(n_x, after, kept_ref, received_ref, *refs):
    total_ref, *sent_refs = refs[after:]
    x = lax.axis_index("head") // 2
    for offset in range(n_x):
        summed = kept_ref[x ^ offset] + received_ref[x ^ offset].astype(jnp.float32)
        if offset:
            sent_refs[offset - 1][...] = summed.astype(jnp.bfloat16)
        else:
            total_ref[...] = summed


def core_sum(kept, received, after):
    n_x, rows, columns = kept.shape
    own = jax.ShapeDtypeStruct((rows, columns), jnp.float32)
    sent = jax.ShapeDtypeStruct((rows, columns), jnp.bfloat16)
    out = pl.pallas_call(
        functools.partial(core_sum_kernel, n_x, len(after)),
        out_shape=[own] + [sent] * (n_x - 1),
        in_specs=[IN_VMEM, IN_VMEM] + [ANYWHERE] * len(after),
        out_specs=[IN_VMEM] * n_x,
        compiler_params=params(4),
        cost_estimate=SHORT,
    )(kept, received, *after)
    return out[0], out[1:]


def x_sum_kernel(counts, rows, places, *refs):
    sources, refs = [], list(refs)
    for count in counts:
        total = refs.pop(0)[...]
        for _ in range(count):
            total = total + refs.pop(0)[...].astype(jnp.float32)
        sources.append(total)
    for out_ref, parts in zip(refs, places):
        parts = [sources[unit][index * rows : (index + 1) * rows] for unit, index in parts]
        out_ref[...] = jnp.concatenate(parts, axis=0).astype(jnp.bfloat16)


def x_sum(sums, rows, places):
    columns = sums[0][0].shape[1]
    arrays = [array for total, received in sums for array in [total, *received]]
    counts = [len(received) for _, received in sums]
    blocks = [jax.ShapeDtypeStruct((rows * len(parts), columns), jnp.bfloat16) for parts in places]
    return pl.pallas_call(
        functools.partial(x_sum_kernel, counts, rows, places),
        out_shape=blocks,
        in_specs=[IN_VMEM] * len(arrays),
        out_specs=[IN_VMEM] * len(blocks),
        compiler_params=params(8),
        cost_estimate=SHORT,
    )(*arrays)


def place_kernel(counts, *refs):
    refs, out_ref = list(refs[:-1]), refs[-1]
    ctx = lax.axis_index("ctx")
    width = refs[0].shape[1]
    for offset, count in enumerate(counts):
        parts = [refs.pop(0)[...].astype(jnp.float32) for _ in range(count)]
        column = pl.multiple_of((ctx ^ offset) * width, 128)
        out_ref[:, pl.ds(column, width)] = jnp.concatenate(parts, axis=0).astype(jnp.bfloat16)


def place_columns(blocks):
    n_ctx = len(blocks)
    rows = sum(block.shape[0] for block in blocks[0])
    width = blocks[0][0].shape[1]
    if width % 128:
        ctx = lax.axis_index("ctx")
        out = jnp.zeros((rows, n_ctx * width), jnp.bfloat16)
        for offset, parts in enumerate(blocks):
            block = jnp.concatenate(parts, axis=0)
            out = lax.dynamic_update_slice(out, block, (0, (ctx ^ offset) * width))
        return out
    arrays = [block for parts in blocks for block in parts]
    return pl.pallas_call(
        functools.partial(place_kernel, [len(parts) for parts in blocks]),
        grid=(1,),
        out_shape=jax.ShapeDtypeStruct((rows, n_ctx * width), jnp.bfloat16),
        in_specs=[IN_VMEM] * len(arrays),
        out_specs=pl.BlockSpec((rows, n_ctx * width), lambda i: (0, 0)),
        compiler_params=params(4),
        cost_estimate=SHORT,
    )(*arrays)


def shards(n_ctx, n_head, queries, kv_rows, w_kv_up, w_out, stretch_order, prefix_len):
    query_rows = queries.shape[0]
    row_span = kv_rows.shape[0]
    cache_rows = row_span - query_rows
    half = row_span // 2
    n_x = n_head // 2
    pieces = chunk_rows(query_rows // n_head)
    core = lax.axis_index("head") % 2

    with jax.named_scope("keys_over_ctx"):
        kv_t = kv_rows.T
        own_half = jnp.where(core == 0, kv_t[:, :half], kv_t[:, half:])
        halves = [exchange(own_half, "ctx", n_ctx, offset) for offset in range(1, n_ctx)]
    with jax.named_scope("load"):
        q_ext, bias, w_values, own_keys = load(
            queries, w_kv_up, kv_t, stretch_order, prefix_len, n_head, pieces, cache_rows
        )
    with jax.named_scope("keys_over_cores"):
        halves = [tie(array, [own_keys]) for array in halves]
        others = [exchange(array, "head", n_head, 1) for array in halves]
    with jax.named_scope("attention"):
        first, *keys = attention(q_ext[0], bias[0], w_values, [own_keys] + halves + others, False)
        second, again = attention(q_ext[1], bias[1], w_values, keys, True)
    with jax.named_scope("attended_over_ctx"):
        early = gather_pieces(first, first, n_ctx, [second], cost(LEAD_EARLY), SHORT)
        again = tie(again, [early[n_ctx // 2]])
        late = gather_pieces(second, again, n_ctx, [early[n_ctx - 1]], cost(LEAD_NEAR), cost(LEAD_LATE))
    powers = [1 << bit for bit in range(n_ctx.bit_length() - 1)]
    handed = [offset for offset in range(1, n_ctx) if offset not in powers]
    gathered = [early, late]
    units = [
        [(0, 0), (1, 0)],
        [(0, offset) for offset in range(1, n_ctx)],
        [(1, offset) for offset in powers],
        [(1, offset) for offset in handed],
    ]
    sums = []
    for unit, members in enumerate(units):
        with jax.named_scope("out_product"):
            if unit == 3:
                for offset in handed:
                    late[offset] = tie(late[offset], sums[1][1], cost(LEAD_HANDED))
            sources = [gathered[chunk][offset] for chunk, offset in members]
            after = [second, *sums[0][1]] if unit == 1 else []
            if unit == 2:
                after = [sums[1][0]]
            sent, kept = product(sources, w_out, n_x, after)
        with jax.named_scope("sum_over_cores"):
            if unit == 3:
                sent = tie(sent, [sums[2][0]])
            total, sent = core_sum(kept, exchange(sent, "head", n_head, 1), [])
        with jax.named_scope("sum_over_x"):
            if unit == 3:
                before = sums[1][1]
                sent = [tie(array, before, cost(LEAD_X)) for array in sent]
            crossed = [exchange(array, "head", n_head, 2 * d) for d, array in enumerate(sent, 1)]
        sums.append((total, crossed))
    def added(units_in, offsets, parts_of):
        with jax.named_scope("sum_over_x"):
            places = [parts_of(offset) for offset in offsets]
            found = x_sum([sums[unit] for unit in units_in], pieces[0], places)
        with jax.named_scope("columns_over_ctx"):
            return [
                exchange(block, "ctx", n_ctx, offset) if offset else block
                for offset, block in zip(offsets, found)
            ]

    blocks = {0: added([0], [0], lambda offset: [(0, 0), (0, 1)])}
    crossing = [offset for offset in range(1, n_ctx) if offset >= n_ctx // 2]
    ahead = added([1], crossing, lambda offset: [(0, offset - 1)])
    ahead = [tie(block, [], cost(LEAD_AHEAD)) for block in ahead]
    blocks.update({offset: [block] for offset, block in zip(crossing, ahead)})

    def rest(unit, offsets):
        def parts_of(offset):
            last_rows = (1, offsets.index(offset))
            return [last_rows] if offset in crossing else [(0, offset - 1), last_rows]

        for offset, block in zip(offsets, added([1, unit], offsets, parts_of)):
            blocks[offset] = [*blocks.get(offset, []), block]

    rest(2, powers)
    rest(3, handed)
    with jax.named_scope("output"):
        return place_columns([blocks[d] for d in range(n_ctx)])


def solution(mesh):
    placed = (
        P(("groups", "ctx"), "head"),
        P(("groups", "ctx"), None),
        P(None, "head"),
        P("head", "ctx"),
        P("groups"),
        P("groups"),
    )
    return jax.shard_map(
        functools.partial(shards, mesh.shape["ctx"], mesh.shape["head"]),
        mesh=mesh,
        in_specs=placed,
        out_specs=P(("groups", "ctx", "head"), None),
        check_vma=False,
    )
```

```python
import functools
import math

import jax
import jax.numpy as jnp
from jax import lax
from jax.experimental import pallas as pl
from jax.experimental.pallas import tpu as pltpu
from jax.sharding import PartitionSpec as P

LAT = 512
NOPE = 128
ROPE = 64
VD = 128
HEAD = NOPE + ROPE
PROJ = NOPE + VD
SUB_ROWS = 512
LOAD_LIMIT = 44
MASKED = -1e30
LEAD_EARLY = 6
LEAD_NEAR = 2
LEAD_LATE = 3
LEAD_HANDED = 3
LEAD_AHEAD = 2
LEAD_X = 1
LOG2E = 1.4426950408889634
SCALE = LOG2E / math.sqrt(HEAD)


def cost(microseconds):
    return pl.CostEstimate(
        flops=int(1e9 * microseconds), bytes_accessed=int(3e6 * microseconds), transcendentals=0
    )


SHORT = pl.CostEstimate(flops=1024, bytes_accessed=1024, transcendentals=0)
IN_VMEM = pl.BlockSpec(memory_space=pltpu.VMEM)
IN_SMEM = pl.BlockSpec(memory_space=pltpu.SMEM)
IN_HBM = pl.BlockSpec(memory_space=pltpu.HBM)
ANYWHERE = pl.BlockSpec(memory_space=pl.ANY)


def chunk_rows(owned):
    return (owned // 2, owned // 2)


def params(mebibytes):
    return pltpu.CompilerParams(vmem_limit_bytes=mebibytes * 1024 * 1024)


def exchange(array, axis, size, bit):
    return lax.ppermute(array, axis, [(i, i ^ bit) for i in range(size)])


def tie_kernel(*refs):
    pass


def tie(array, after, lead=SHORT):
    return pl.pallas_call(
        tie_kernel,
        out_shape=jax.ShapeDtypeStruct(array.shape, array.dtype),
        in_specs=[ANYWHERE] * (1 + len(after)),
        out_specs=ANYWHERE,
        input_output_aliases={0: 0},
        compiler_params=params(1),
        cost_estimate=lead,
    )(array, *after)


def gather_pieces(own, near, size, after, lead, far_lead):
    pieces = {0: own, 1: tie(exchange(near, "ctx", size, 1), [], lead)}
    bit = size // 2
    while bit > 1:
        pieces[bit] = exchange(own, "ctx", size, bit)
        bit //= 2
    bit = 2
    while bit < size:
        for offset in range(bit + 1, 2 * bit):
            if offset == bit + 1:
                pieces[bit] = tie(pieces[bit], after, far_lead)
            pieces[offset] = exchange(pieces[bit], "ctx", size, offset ^ bit)
        bit *= 2
    return [pieces[offset] for offset in range(size)]


def load_kernel(owners, pieces, cache_rows, order_ref, prefix_ref, q_hbm, up_hbm, own_hbm, *refs):
    count = len(pieces)
    q_exts, biases, refs = refs[:count], refs[count : 2 * count], refs[2 * count :]
    value_ref, own_ref, q_ref, key_ref, sems, key_sems, value_sems = refs
    rows = q_ref.shape[0]
    head_count = key_ref.shape[0]
    q_copy = pltpu.make_async_copy(q_hbm, q_ref, sems.at[0])
    own_copy = pltpu.make_async_copy(own_hbm, own_ref, sems.at[1])
    q_copy.start()
    key_copies, value_copies = [], []
    for head in range(head_count):
        source = up_hbm.at[:, pl.ds(head * PROJ, NOPE)]
        key_copies.append(pltpu.make_async_copy(source, key_ref.at[head], key_sems.at[head]))
        source = up_hbm.at[:, pl.ds(head * PROJ + NOPE, VD)]
        value_copies.append(pltpu.make_async_copy(source, value_ref.at[head], value_sems.at[head]))
    for copy in key_copies + [own_copy] + value_copies:
        copy.start()
    start = 0
    for piece, bias_ref in zip(pieces, biases):
        visible_bias(
            order_ref, prefix_ref, bias_ref, rows, owners, start, own_hbm.shape[1], cache_rows
        )
        start += piece
    q_copy.wait()
    for head in range(head_count):
        nope = q_ref[:, head * HEAD : head * HEAD + NOPE]
        rope = q_ref[:, head * HEAD + NOPE : (head + 1) * HEAD].astype(jnp.float32) * SCALE
        key_copies[head].wait()
        absorbed = lax.dot_general(
            nope, key_ref[head], (((1,), (1,)), ((), ())), preferred_element_type=jnp.float32
        )
        absorbed = (absorbed * SCALE).reshape(owners, rows // owners, LAT)
        rope = rope.reshape(owners, rows // owners, ROPE)
        start = 0
        for piece, q_ext in zip(pieces, q_exts):
            part = absorbed[:, start : start + piece].reshape(owners * piece, LAT)
            q_ext[head, :, :LAT] = part.astype(jnp.bfloat16)
            part = rope[:, start : start + piece].reshape(owners * piece, ROPE)
            q_ext[head, :, LAT:] = part.astype(jnp.bfloat16)
            start += piece
    for copy in [own_copy] + value_copies:
        copy.wait()


def load(queries, w_kv_up, own_keys, stretch_order, prefix_len, owners, pieces, cache_rows):
    head_count = w_kv_up.shape[1] // PROJ
    amount = stretch_order.shape[0] * own_keys.shape[1]
    out_shape = [
        jax.ShapeDtypeStruct((head_count, owners * piece, LAT + ROPE), jnp.bfloat16)
        for piece in pieces
    ]
    out_shape += [jax.ShapeDtypeStruct((owners * piece, amount), jnp.float32) for piece in pieces]
    out_shape += [
        jax.ShapeDtypeStruct((head_count, LAT, VD), jnp.bfloat16),
        jax.ShapeDtypeStruct(own_keys.shape, jnp.bfloat16),
    ]
    out = pl.pallas_call(
        functools.partial(load_kernel, owners, pieces, cache_rows),
        out_shape=out_shape,
        in_specs=[IN_SMEM, IN_SMEM] + [IN_HBM] * 3,
        out_specs=[IN_VMEM] * len(out_shape),
        scratch_shapes=[
            pltpu.VMEM(queries.shape, jnp.bfloat16),
            pltpu.VMEM((head_count, LAT, NOPE), jnp.bfloat16),
            pltpu.SemaphoreType.DMA((2,)),
            pltpu.SemaphoreType.DMA((head_count,)),
            pltpu.SemaphoreType.DMA((head_count,)),
        ],
        compiler_params=params(LOAD_LIMIT),
        cost_estimate=SHORT,
    )(stretch_order, prefix_len, queries, w_kv_up, own_keys)
    count = len(pieces)
    return out[:count], out[count : 2 * count], *out[2 * count :]


def visible_bias(order_ref, prefix_ref, bias_ref, query_rows, owners, start, row_span, cache_rows):
    n_ctx = order_ref.shape[0]
    half = row_span // 2
    rows = bias_ref.shape[0]
    piece = rows // owners
    own = lax.axis_index("ctx")
    core = lax.axis_index("head") % 2
    blocks = [(0, 0), (0, 1)]
    blocks += [(offset, core) for offset in range(1, n_ctx)]
    blocks += [(offset, 1 - core) for offset in range(1, n_ctx)]
    row = lax.broadcasted_iota(jnp.int32, (rows, half), 0)
    column = lax.broadcasted_iota(jnp.int32, (rows, half), 1)
    within_own = row // piece * (query_rows // owners) + start + row % piece
    query_pos = order_ref[own] * query_rows + within_own
    for index, (offset, second) in enumerate(blocks):
        source = own ^ offset
        within = second * half + column
        cache_pos = jnp.where(
            source * cache_rows + within < prefix_ref[0], -1, n_ctx * query_rows
        )
        key_pos = order_ref[source] * query_rows + within - cache_rows
        first_seen = jnp.where(within < cache_rows, cache_pos, key_pos)
        bias = jnp.where(first_seen <= query_pos, 0.0, MASKED).astype(jnp.float32)
        bias_ref[:, index * half : (index + 1) * half] = bias


def attention_kernel(count, q_ref, bias_ref, value_ref, *refs):
    heads, rows, depth = q_ref.shape
    if count:
        piece_refs, (out_ref, keys_ref, latent_ref) = refs[:count], refs[count:]
        start = 0
        for piece_ref in piece_refs:
            width = piece_ref.shape[1]
            keys_ref[:, start : start + width] = piece_ref[...]
            latent_ref[start : start + width, :] = piece_ref[:LAT, :].T
            start += width
    else:
        keys_ref, latent_ref, out_ref, copy_ref = refs
    amount = keys_ref.shape[1]
    group = max(1, min(heads, SUB_ROWS // rows))
    size = group * rows

    def score(first):
        queries = q_ref[first : first + group].reshape(size, depth)
        return jnp.dot(queries, keys_ref[...], preferred_element_type=jnp.float32)

    scores = score(0)
    for first in range(0, heads, group):
        later = score(first + group) if first + group < heads else None
        scores = scores.reshape(group, rows, amount) + bias_ref[...][None]
        top = jnp.max(scores, axis=2, keepdims=True)
        weights = jnp.exp2(scores - top)
        total = jnp.sum(weights, axis=2, keepdims=True).reshape(size, 1)
        mixed = jnp.dot(
            weights.reshape(size, amount).astype(jnp.bfloat16),
            latent_ref[...],
            preferred_element_type=jnp.float32,
        )
        mixed = (mixed / total).astype(jnp.bfloat16)
        for head in range(first, first + group):
            result = jnp.dot(
                mixed[(head - first) * rows : (head - first + 1) * rows],
                value_ref[head],
                preferred_element_type=jnp.float32,
            )
            out_ref[:, head * VD : (head + 1) * VD] = result.astype(jnp.bfloat16)
            if not count:
                copy_ref[:, head * VD : (head + 1) * VD] = result.astype(jnp.bfloat16)
        scores = later


def attention(q_ext, bias, w_values, keys, gathered):
    head_count, rows, depth = q_ext.shape
    amount = bias.shape[1]
    out_shape = [jax.ShapeDtypeStruct((rows, head_count * VD), jnp.bfloat16)]
    if gathered:
        out_shape *= 2
    else:
        out_shape.append(jax.ShapeDtypeStruct((depth, amount), jnp.bfloat16))
        out_shape.append(jax.ShapeDtypeStruct((amount, LAT), jnp.bfloat16))
    return pl.pallas_call(
        functools.partial(attention_kernel, 0 if gathered else len(keys)),
        out_shape=out_shape,
        in_specs=[IN_VMEM] * (3 + len(keys)),
        out_specs=[IN_VMEM] * len(out_shape),
        compiler_params=params(16 if amount <= 1024 else 40),
        cost_estimate=SHORT,
    )(q_ext, bias, w_values, *keys)


def product_kernel(count, n_x, after, weight_ref, *refs):
    piece_refs = refs[:count]
    sent_ref, kept_ref, rows_ref = refs[count + after :]
    rows = piece_refs[0].shape[0]
    columns = weight_ref.shape[1]
    for index, piece_ref in enumerate(piece_refs):
        rows_ref[index * rows : (index + 1) * rows, :] = piece_ref[...]
    is_first = lax.axis_index("head") % 2 == 0
    width = 256 if columns % 256 == 0 else columns
    for start in range(0, columns, width):
        span = slice(start, start + width)
        result = jnp.dot(rows_ref[...], weight_ref[:, span], preferred_element_type=jnp.float32)
        result = result.reshape(count, n_x, 2, rows // (2 * n_x), width)
        for x in range(n_x):
            first = result[:, x, 0].reshape(rows * count // (2 * n_x), width)
            second = result[:, x, 1].reshape(rows * count // (2 * n_x), width)
            sent_ref[x, :, span] = jnp.where(is_first, second, first).astype(jnp.bfloat16)
            kept_ref[x, :, span] = jnp.where(is_first, first, second)


def product(pieces, w_out, n_x, after):
    rows, depth = pieces[0].shape
    count = len(pieces)
    shape = (n_x, count * rows // (2 * n_x), w_out.shape[1])
    return pl.pallas_call(
        functools.partial(product_kernel, count, n_x, len(after)),
        out_shape=[jax.ShapeDtypeStruct(shape, jnp.bfloat16), jax.ShapeDtypeStruct(shape, jnp.float32)],
        in_specs=[IN_VMEM] * (1 + count) + [ANYWHERE] * len(after),
        out_specs=[IN_VMEM, IN_VMEM],
        scratch_shapes=[pltpu.VMEM((count * rows, depth), jnp.bfloat16)],
        compiler_params=params(16),
        cost_estimate=SHORT,
    )(w_out, *pieces, *after)


def core_sum_kernel(n_x, after, kept_ref, received_ref, *refs):
    total_ref, *sent_refs = refs[after:]
    x = lax.axis_index("head") // 2
    for offset in range(n_x):
        summed = kept_ref[x ^ offset] + received_ref[x ^ offset].astype(jnp.float32)
        if offset:
            sent_refs[offset - 1][...] = summed.astype(jnp.bfloat16)
        else:
            total_ref[...] = summed


def core_sum(kept, received, after):
    n_x, rows, columns = kept.shape
    own = jax.ShapeDtypeStruct((rows, columns), jnp.float32)
    sent = jax.ShapeDtypeStruct((rows, columns), jnp.bfloat16)
    out = pl.pallas_call(
        functools.partial(core_sum_kernel, n_x, len(after)),
        out_shape=[own] + [sent] * (n_x - 1),
        in_specs=[IN_VMEM, IN_VMEM] + [ANYWHERE] * len(after),
        out_specs=[IN_VMEM] * n_x,
        compiler_params=params(4),
        cost_estimate=SHORT,
    )(kept, received, *after)
    return out[0], out[1:]


def x_sum_kernel(counts, rows, places, *refs):
    sources, refs = [], list(refs)
    for count in counts:
        total = refs.pop(0)[...]
        for _ in range(count):
            total = total + refs.pop(0)[...].astype(jnp.float32)
        sources.append(total)
    for out_ref, parts in zip(refs, places):
        parts = [sources[unit][index * rows : (index + 1) * rows] for unit, index in parts]
        out_ref[...] = jnp.concatenate(parts, axis=0).astype(jnp.bfloat16)


def x_sum(sums, rows, places):
    columns = sums[0][0].shape[1]
    arrays = [array for total, received in sums for array in [total, *received]]
    counts = [len(received) for _, received in sums]
    blocks = [jax.ShapeDtypeStruct((rows * len(parts), columns), jnp.bfloat16) for parts in places]
    return pl.pallas_call(
        functools.partial(x_sum_kernel, counts, rows, places),
        out_shape=blocks,
        in_specs=[IN_VMEM] * len(arrays),
        out_specs=[IN_VMEM] * len(blocks),
        compiler_params=params(8),
        cost_estimate=SHORT,
    )(*arrays)


def place_kernel(counts, *refs):
    refs, out_ref = list(refs[:-1]), refs[-1]
    ctx = lax.axis_index("ctx")
    width = refs[0].shape[1]
    for offset, count in enumerate(counts):
        parts = [refs.pop(0)[...].astype(jnp.float32) for _ in range(count)]
        column = pl.multiple_of((ctx ^ offset) * width, 128)
        out_ref[:, pl.ds(column, width)] = jnp.concatenate(parts, axis=0).astype(jnp.bfloat16)


def place_columns(blocks):
    n_ctx = len(blocks)
    rows = sum(block.shape[0] for block in blocks[0])
    width = blocks[0][0].shape[1]
    if width % 128:
        ctx = lax.axis_index("ctx")
        out = jnp.zeros((rows, n_ctx * width), jnp.bfloat16)
        for offset, parts in enumerate(blocks):
            block = jnp.concatenate(parts, axis=0)
            out = lax.dynamic_update_slice(out, block, (0, (ctx ^ offset) * width))
        return out
    arrays = [block for parts in blocks for block in parts]
    return pl.pallas_call(
        functools.partial(place_kernel, [len(parts) for parts in blocks]),
        grid=(1,),
        out_shape=jax.ShapeDtypeStruct((rows, n_ctx * width), jnp.bfloat16),
        in_specs=[IN_VMEM] * len(arrays),
        out_specs=pl.BlockSpec((rows, n_ctx * width), lambda i: (0, 0)),
        compiler_params=params(4),
        cost_estimate=SHORT,
    )(*arrays)


def shards(n_ctx, n_head, queries, kv_rows, w_kv_up, w_out, stretch_order, prefix_len):
    query_rows = queries.shape[0]
    row_span = kv_rows.shape[0]
    cache_rows = row_span - query_rows
    half = row_span // 2
    n_x = n_head // 2
    pieces = chunk_rows(query_rows // n_head)
    core = lax.axis_index("head") % 2

    with jax.named_scope("keys_over_ctx"):
        kv_t = kv_rows.T
        own_half = jnp.where(core == 0, kv_t[:, :half], kv_t[:, half:])
        halves = [exchange(own_half, "ctx", n_ctx, offset) for offset in range(1, n_ctx)]
    with jax.named_scope("load"):
        q_ext, bias, w_values, own_keys = load(
            queries, w_kv_up, kv_t, stretch_order, prefix_len, n_head, pieces, cache_rows
        )
    with jax.named_scope("keys_over_cores"):
        halves = [tie(array, [own_keys]) for array in halves]
        others = [exchange(array, "head", n_head, 1) for array in halves]
    with jax.named_scope("attention"):
        first, *keys = attention(q_ext[0], bias[0], w_values, [own_keys] + halves + others, False)
        second, again = attention(q_ext[1], bias[1], w_values, keys, True)
    with jax.named_scope("attended_over_ctx"):
        early = gather_pieces(first, first, n_ctx, [second], cost(LEAD_EARLY), SHORT)
        again = tie(again, [early[n_ctx // 2]])
        late = gather_pieces(second, again, n_ctx, [early[n_ctx - 1]], cost(LEAD_NEAR), cost(LEAD_LATE))
    powers = [1 << bit for bit in range(n_ctx.bit_length() - 1)]
    handed = [offset for offset in range(1, n_ctx) if offset not in powers]
    gathered = [early, late]
    units = [
        [(0, 0), (1, 0)],
        [(0, offset) for offset in range(1, n_ctx)],
        [(1, offset) for offset in powers],
        [(1, offset) for offset in handed],
    ]
    sums = []
    for unit, members in enumerate(units):
        with jax.named_scope("out_product"):
            if unit == 3:
                for offset in handed:
                    late[offset] = tie(late[offset], sums[1][1], cost(LEAD_HANDED))
            sources = [gathered[chunk][offset] for chunk, offset in members]
            after = [second, *sums[0][1]] if unit == 1 else []
            if unit == 2:
                after = [sums[1][0]]
            sent, kept = product(sources, w_out, n_x, after)
        with jax.named_scope("sum_over_cores"):
            if unit == 3:
                sent = tie(sent, [sums[2][0]])
            total, sent = core_sum(kept, exchange(sent, "head", n_head, 1), [])
        with jax.named_scope("sum_over_x"):
            if unit == 3:
                before = sums[1][1]
                sent = [tie(array, before, cost(LEAD_X)) for array in sent]
            crossed = [exchange(array, "head", n_head, 2 * d) for d, array in enumerate(sent, 1)]
        sums.append((total, crossed))
    def added(units_in, offsets, parts_of):
        with jax.named_scope("sum_over_x"):
            places = [parts_of(offset) for offset in offsets]
            found = x_sum([sums[unit] for unit in units_in], pieces[0], places)
        with jax.named_scope("columns_over_ctx"):
            return [
                exchange(block, "ctx", n_ctx, offset) if offset else block
                for offset, block in zip(offsets, found)
            ]

    blocks = {0: added([0], [0], lambda offset: [(0, 0), (0, 1)])}
    crossing = [offset for offset in range(1, n_ctx) if offset >= n_ctx // 2]
    ahead = added([1], crossing, lambda offset: [(0, offset - 1)])
    ahead[0] = tie(ahead[0], ahead[1:], cost(LEAD_AHEAD))
    blocks.update({offset: [block] for offset, block in zip(crossing, ahead)})

    def rest(unit, offsets):
        def parts_of(offset):
            last_rows = (1, offsets.index(offset))
            return [last_rows] if offset in crossing else [(0, offset - 1), last_rows]

        for offset, block in zip(offsets, added([1, unit], offsets, parts_of)):
            blocks[offset] = [*blocks.get(offset, []), block]

    rest(2, powers)
    rest(3, handed)
    with jax.named_scope("output"):
        return place_columns([blocks[d] for d in range(n_ctx)])


def solution(mesh):
    placed = (
        P(("groups", "ctx"), "head"),
        P(("groups", "ctx"), None),
        P(None, "head"),
        P("head", "ctx"),
        P("groups"),
        P("groups"),
    )
    return jax.shard_map(
        functools.partial(shards, mesh.shape["ctx"], mesh.shape["head"]),
        mesh=mesh,
        in_specs=placed,
        out_specs=P(("groups", "ctx", "head"), None),
        check_vma=False,
    )
```

```python
import functools
import math

import jax
import jax.numpy as jnp
from jax import lax
from jax.experimental import pallas as pl
from jax.experimental.pallas import tpu as pltpu
from jax.sharding import PartitionSpec as P

LAT = 512
NOPE = 128
ROPE = 64
VD = 128
HEAD = NOPE + ROPE
PROJ = NOPE + VD
SUB_ROWS = 512
LOAD_LIMIT = 44
MASKED = -1e30
LEAD_EARLY = 6
LEAD_NEAR = 2
LEAD_LATE = 3
LEAD_HANDED = 3
LEAD_AHEAD = 1
LEAD_X = 1
LOG2E = 1.4426950408889634
SCALE = LOG2E / math.sqrt(HEAD)


def cost(microseconds):
    return pl.CostEstimate(
        flops=int(1e9 * microseconds), bytes_accessed=int(3e6 * microseconds), transcendentals=0
    )


SHORT = pl.CostEstimate(flops=1024, bytes_accessed=1024, transcendentals=0)
IN_VMEM = pl.BlockSpec(memory_space=pltpu.VMEM)
IN_SMEM = pl.BlockSpec(memory_space=pltpu.SMEM)
IN_HBM = pl.BlockSpec(memory_space=pltpu.HBM)
ANYWHERE = pl.BlockSpec(memory_space=pl.ANY)


def chunk_rows(owned):
    return (owned // 2, owned // 2)


def params(mebibytes):
    return pltpu.CompilerParams(vmem_limit_bytes=mebibytes * 1024 * 1024)


def exchange(array, axis, size, bit):
    return lax.ppermute(array, axis, [(i, i ^ bit) for i in range(size)])


def tie_kernel(*refs):
    pass


def tie(array, after, lead=SHORT):
    return pl.pallas_call(
        tie_kernel,
        out_shape=jax.ShapeDtypeStruct(array.shape, array.dtype),
        in_specs=[ANYWHERE] * (1 + len(after)),
        out_specs=ANYWHERE,
        input_output_aliases={0: 0},
        compiler_params=params(1),
        cost_estimate=lead,
    )(array, *after)


def gather_pieces(own, near, size, after, lead, far_lead):
    pieces = {0: own, 1: tie(exchange(near, "ctx", size, 1), [], lead)}
    bit = size // 2
    while bit > 1:
        pieces[bit] = exchange(own, "ctx", size, bit)
        bit //= 2
    bit = 2
    while bit < size:
        for offset in range(bit + 1, 2 * bit):
            if offset == bit + 1:
                pieces[bit] = tie(pieces[bit], after, far_lead)
            pieces[offset] = exchange(pieces[bit], "ctx", size, offset ^ bit)
        bit *= 2
    return [pieces[offset] for offset in range(size)]


def load_kernel(owners, pieces, cache_rows, order_ref, prefix_ref, q_hbm, up_hbm, own_hbm, *refs):
    count = len(pieces)
    q_exts, biases, refs = refs[:count], refs[count : 2 * count], refs[2 * count :]
    value_ref, own_ref, q_ref, key_ref, sems, key_sems, value_sems = refs
    rows = q_ref.shape[0]
    head_count = key_ref.shape[0]
    q_copy = pltpu.make_async_copy(q_hbm, q_ref, sems.at[0])
    own_copy = pltpu.make_async_copy(own_hbm, own_ref, sems.at[1])
    q_copy.start()
    key_copies, value_copies = [], []
    for head in range(head_count):
        source = up_hbm.at[:, pl.ds(head * PROJ, NOPE)]
        key_copies.append(pltpu.make_async_copy(source, key_ref.at[head], key_sems.at[head]))
        source = up_hbm.at[:, pl.ds(head * PROJ + NOPE, VD)]
        value_copies.append(pltpu.make_async_copy(source, value_ref.at[head], value_sems.at[head]))
    for copy in key_copies + [own_copy] + value_copies:
        copy.start()
    start = 0
    for piece, bias_ref in zip(pieces, biases):
        visible_bias(
            order_ref, prefix_ref, bias_ref, rows, owners, start, own_hbm.shape[1], cache_rows
        )
        start += piece
    q_copy.wait()
    for head in range(head_count):
        nope = q_ref[:, head * HEAD : head * HEAD + NOPE]
        rope = q_ref[:, head * HEAD + NOPE : (head + 1) * HEAD].astype(jnp.float32) * SCALE
        key_copies[head].wait()
        absorbed = lax.dot_general(
            nope, key_ref[head], (((1,), (1,)), ((), ())), preferred_element_type=jnp.float32
        )
        absorbed = (absorbed * SCALE).reshape(owners, rows // owners, LAT)
        rope = rope.reshape(owners, rows // owners, ROPE)
        start = 0
        for piece, q_ext in zip(pieces, q_exts):
            part = absorbed[:, start : start + piece].reshape(owners * piece, LAT)
            q_ext[head, :, :LAT] = part.astype(jnp.bfloat16)
            part = rope[:, start : start + piece].reshape(owners * piece, ROPE)
            q_ext[head, :, LAT:] = part.astype(jnp.bfloat16)
            start += piece
    for copy in [own_copy] + value_copies:
        copy.wait()


def load(queries, w_kv_up, own_keys, stretch_order, prefix_len, owners, pieces, cache_rows):
    head_count = w_kv_up.shape[1] // PROJ
    amount = stretch_order.shape[0] * own_keys.shape[1]
    out_shape = [
        jax.ShapeDtypeStruct((head_count, owners * piece, LAT + ROPE), jnp.bfloat16)
        for piece in pieces
    ]
    out_shape += [jax.ShapeDtypeStruct((owners * piece, amount), jnp.float32) for piece in pieces]
    out_shape += [
        jax.ShapeDtypeStruct((head_count, LAT, VD), jnp.bfloat16),
        jax.ShapeDtypeStruct(own_keys.shape, jnp.bfloat16),
    ]
    out = pl.pallas_call(
        functools.partial(load_kernel, owners, pieces, cache_rows),
        out_shape=out_shape,
        in_specs=[IN_SMEM, IN_SMEM] + [IN_HBM] * 3,
        out_specs=[IN_VMEM] * len(out_shape),
        scratch_shapes=[
            pltpu.VMEM(queries.shape, jnp.bfloat16),
            pltpu.VMEM((head_count, LAT, NOPE), jnp.bfloat16),
            pltpu.SemaphoreType.DMA((2,)),
            pltpu.SemaphoreType.DMA((head_count,)),
            pltpu.SemaphoreType.DMA((head_count,)),
        ],
        compiler_params=params(LOAD_LIMIT),
        cost_estimate=SHORT,
    )(stretch_order, prefix_len, queries, w_kv_up, own_keys)
    count = len(pieces)
    return out[:count], out[count : 2 * count], *out[2 * count :]


def visible_bias(order_ref, prefix_ref, bias_ref, query_rows, owners, start, row_span, cache_rows):
    n_ctx = order_ref.shape[0]
    half = row_span // 2
    rows = bias_ref.shape[0]
    piece = rows // owners
    own = lax.axis_index("ctx")
    core = lax.axis_index("head") % 2
    blocks = [(0, 0), (0, 1)]
    blocks += [(offset, core) for offset in range(1, n_ctx)]
    blocks += [(offset, 1 - core) for offset in range(1, n_ctx)]
    row = lax.broadcasted_iota(jnp.int32, (rows, half), 0)
    column = lax.broadcasted_iota(jnp.int32, (rows, half), 1)
    within_own = row // piece * (query_rows // owners) + start + row % piece
    query_pos = order_ref[own] * query_rows + within_own
    for index, (offset, second) in enumerate(blocks):
        source = own ^ offset
        within = second * half + column
        cache_pos = jnp.where(
            source * cache_rows + within < prefix_ref[0], -1, n_ctx * query_rows
        )
        key_pos = order_ref[source] * query_rows + within - cache_rows
        first_seen = jnp.where(within < cache_rows, cache_pos, key_pos)
        bias = jnp.where(first_seen <= query_pos, 0.0, MASKED).astype(jnp.float32)
        bias_ref[:, index * half : (index + 1) * half] = bias


def attention_kernel(count, q_ref, bias_ref, value_ref, *refs):
    heads, rows, depth = q_ref.shape
    if count:
        piece_refs, (out_ref, keys_ref, latent_ref) = refs[:count], refs[count:]
        start = 0
        for piece_ref in piece_refs:
            width = piece_ref.shape[1]
            keys_ref[:, start : start + width] = piece_ref[...]
            latent_ref[start : start + width, :] = piece_ref[:LAT, :].T
            start += width
    else:
        keys_ref, latent_ref, out_ref, copy_ref = refs
    amount = keys_ref.shape[1]
    group = max(1, min(heads, SUB_ROWS // rows))
    size = group * rows

    def score(first):
        queries = q_ref[first : first + group].reshape(size, depth)
        return jnp.dot(queries, keys_ref[...], preferred_element_type=jnp.float32)

    scores = score(0)
    for first in range(0, heads, group):
        later = score(first + group) if first + group < heads else None
        scores = scores.reshape(group, rows, amount) + bias_ref[...][None]
        top = jnp.max(scores, axis=2, keepdims=True)
        weights = jnp.exp2(scores - top)
        total = jnp.sum(weights, axis=2, keepdims=True).reshape(size, 1)
        mixed = jnp.dot(
            weights.reshape(size, amount).astype(jnp.bfloat16),
            latent_ref[...],
            preferred_element_type=jnp.float32,
        )
        mixed = (mixed / total).astype(jnp.bfloat16)
        for head in range(first, first + group):
            result = jnp.dot(
                mixed[(head - first) * rows : (head - first + 1) * rows],
                value_ref[head],
                preferred_element_type=jnp.float32,
            )
            out_ref[:, head * VD : (head + 1) * VD] = result.astype(jnp.bfloat16)
            if not count:
                copy_ref[:, head * VD : (head + 1) * VD] = result.astype(jnp.bfloat16)
        scores = later


def attention(q_ext, bias, w_values, keys, gathered):
    head_count, rows, depth = q_ext.shape
    amount = bias.shape[1]
    out_shape = [jax.ShapeDtypeStruct((rows, head_count * VD), jnp.bfloat16)]
    if gathered:
        out_shape *= 2
    else:
        out_shape.append(jax.ShapeDtypeStruct((depth, amount), jnp.bfloat16))
        out_shape.append(jax.ShapeDtypeStruct((amount, LAT), jnp.bfloat16))
    return pl.pallas_call(
        functools.partial(attention_kernel, 0 if gathered else len(keys)),
        out_shape=out_shape,
        in_specs=[IN_VMEM] * (3 + len(keys)),
        out_specs=[IN_VMEM] * len(out_shape),
        compiler_params=params(16 if amount <= 1024 else 40),
        cost_estimate=SHORT,
    )(q_ext, bias, w_values, *keys)


def product_kernel(count, n_x, after, weight_ref, *refs):
    piece_refs = refs[:count]
    sent_ref, kept_ref, rows_ref = refs[count + after :]
    rows = piece_refs[0].shape[0]
    columns = weight_ref.shape[1]
    for index, piece_ref in enumerate(piece_refs):
        rows_ref[index * rows : (index + 1) * rows, :] = piece_ref[...]
    is_first = lax.axis_index("head") % 2 == 0
    result = jnp.dot(rows_ref[...], weight_ref[...], preferred_element_type=jnp.float32)
    result = result.reshape(count, n_x, 2, rows // (2 * n_x), columns)
    for x in range(n_x):
        first = result[:, x, 0].reshape(rows * count // (2 * n_x), columns)
        second = result[:, x, 1].reshape(rows * count // (2 * n_x), columns)
        sent_ref[x] = jnp.where(is_first, second, first).astype(jnp.bfloat16)
        kept_ref[x] = jnp.where(is_first, first, second)


def product(pieces, w_out, n_x, after):
    rows, depth = pieces[0].shape
    count = len(pieces)
    shape = (n_x, count * rows // (2 * n_x), w_out.shape[1])
    return pl.pallas_call(
        functools.partial(product_kernel, count, n_x, len(after)),
        out_shape=[jax.ShapeDtypeStruct(shape, jnp.bfloat16), jax.ShapeDtypeStruct(shape, jnp.float32)],
        in_specs=[IN_VMEM] * (1 + count) + [ANYWHERE] * len(after),
        out_specs=[IN_VMEM, IN_VMEM],
        scratch_shapes=[pltpu.VMEM((count * rows, depth), jnp.bfloat16)],
        compiler_params=params(16),
        cost_estimate=SHORT,
    )(w_out, *pieces, *after)


def core_sum_kernel(n_x, after, kept_ref, received_ref, *refs):
    total_ref, *sent_refs = refs[after:]
    x = lax.axis_index("head") // 2
    for offset in range(n_x):
        summed = kept_ref[x ^ offset] + received_ref[x ^ offset].astype(jnp.float32)
        if offset:
            sent_refs[offset - 1][...] = summed.astype(jnp.bfloat16)
        else:
            total_ref[...] = summed


def core_sum(kept, received, after):
    n_x, rows, columns = kept.shape
    own = jax.ShapeDtypeStruct((rows, columns), jnp.float32)
    sent = jax.ShapeDtypeStruct((rows, columns), jnp.bfloat16)
    out = pl.pallas_call(
        functools.partial(core_sum_kernel, n_x, len(after)),
        out_shape=[own] + [sent] * (n_x - 1),
        in_specs=[IN_VMEM, IN_VMEM] + [ANYWHERE] * len(after),
        out_specs=[IN_VMEM] * n_x,
        compiler_params=params(4),
        cost_estimate=SHORT,
    )(kept, received, *after)
    return out[0], out[1:]


def x_sum_kernel(counts, rows, places, *refs):
    sources, refs = [], list(refs)
    for count in counts:
        total = refs.pop(0)[...]
        for _ in range(count):
            total = total + refs.pop(0)[...].astype(jnp.float32)
        sources.append(total)
    for out_ref, parts in zip(refs, places):
        parts = [sources[unit][index * rows : (index + 1) * rows] for unit, index in parts]
        out_ref[...] = jnp.concatenate(parts, axis=0).astype(jnp.bfloat16)


def x_sum(sums, rows, places):
    columns = sums[0][0].shape[1]
    arrays = [array for total, received in sums for array in [total, *received]]
    counts = [len(received) for _, received in sums]
    blocks = [jax.ShapeDtypeStruct((rows * len(parts), columns), jnp.bfloat16) for parts in places]
    return pl.pallas_call(
        functools.partial(x_sum_kernel, counts, rows, places),
        out_shape=blocks,
        in_specs=[IN_VMEM] * len(arrays),
        out_specs=[IN_VMEM] * len(blocks),
        compiler_params=params(8),
        cost_estimate=SHORT,
    )(*arrays)


def place_kernel(counts, *refs):
    refs, out_ref = list(refs[:-1]), refs[-1]
    ctx = lax.axis_index("ctx")
    width = refs[0].shape[1]
    for offset, count in enumerate(counts):
        parts = [refs.pop(0)[...].astype(jnp.float32) for _ in range(count)]
        column = pl.multiple_of((ctx ^ offset) * width, 128)
        out_ref[:, pl.ds(column, width)] = jnp.concatenate(parts, axis=0).astype(jnp.bfloat16)


def place_columns(blocks):
    n_ctx = len(blocks)
    rows = sum(block.shape[0] for block in blocks[0])
    width = blocks[0][0].shape[1]
    if width % 128:
        ctx = lax.axis_index("ctx")
        out = jnp.zeros((rows, n_ctx * width), jnp.bfloat16)
        for offset, parts in enumerate(blocks):
            block = jnp.concatenate(parts, axis=0)
            out = lax.dynamic_update_slice(out, block, (0, (ctx ^ offset) * width))
        return out
    arrays = [block for parts in blocks for block in parts]
    return pl.pallas_call(
        functools.partial(place_kernel, [len(parts) for parts in blocks]),
        grid=(1,),
        out_shape=jax.ShapeDtypeStruct((rows, n_ctx * width), jnp.bfloat16),
        in_specs=[IN_VMEM] * len(arrays),
        out_specs=pl.BlockSpec((rows, n_ctx * width), lambda i: (0, 0)),
        compiler_params=params(4),
        cost_estimate=SHORT,
    )(*arrays)


def shards(n_ctx, n_head, queries, kv_rows, w_kv_up, w_out, stretch_order, prefix_len):
    query_rows = queries.shape[0]
    row_span = kv_rows.shape[0]
    cache_rows = row_span - query_rows
    half = row_span // 2
    n_x = n_head // 2
    pieces = chunk_rows(query_rows // n_head)
    core = lax.axis_index("head") % 2

    with jax.named_scope("keys_over_ctx"):
        kv_t = kv_rows.T
        own_half = jnp.where(core == 0, kv_t[:, :half], kv_t[:, half:])
        halves = [exchange(own_half, "ctx", n_ctx, offset) for offset in range(1, n_ctx)]
    with jax.named_scope("load"):
        q_ext, bias, w_values, own_keys = load(
            queries, w_kv_up, kv_t, stretch_order, prefix_len, n_head, pieces, cache_rows
        )
    with jax.named_scope("keys_over_cores"):
        halves = [tie(array, [own_keys]) for array in halves]
        others = [exchange(array, "head", n_head, 1) for array in halves]
    with jax.named_scope("attention"):
        first, *keys = attention(q_ext[0], bias[0], w_values, [own_keys] + halves + others, False)
        second, again = attention(q_ext[1], bias[1], w_values, keys, True)
    with jax.named_scope("attended_over_ctx"):
        early = gather_pieces(first, first, n_ctx, [second], cost(LEAD_EARLY), SHORT)
        again = tie(again, [early[n_ctx // 2]])
        late = gather_pieces(second, again, n_ctx, [early[n_ctx - 1]], cost(LEAD_NEAR), cost(LEAD_LATE))
    powers = [1 << bit for bit in range(n_ctx.bit_length() - 1)]
    handed = [offset for offset in range(1, n_ctx) if offset not in powers]
    gathered = [early, late]
    units = [
        [(0, 0), (1, 0)],
        [(0, offset) for offset in range(1, n_ctx)],
        [(1, offset) for offset in powers],
        [(1, offset) for offset in handed],
    ]
    sums = []
    for unit, members in enumerate(units):
        with jax.named_scope("out_product"):
            if unit == 3:
                for offset in handed:
                    late[offset] = tie(late[offset], sums[1][1], cost(LEAD_HANDED))
            sources = [gathered[chunk][offset] for chunk, offset in members]
            after = [second, *sums[0][1]] if unit == 1 else []
            if unit == 2:
                after = [sums[1][0]]
            sent, kept = product(sources, w_out, n_x, after)
        with jax.named_scope("sum_over_cores"):
            if unit == 3:
                sent = tie(sent, [sums[2][0]])
            total, sent = core_sum(kept, exchange(sent, "head", n_head, 1), [])
        with jax.named_scope("sum_over_x"):
            if unit == 3:
                before = sums[1][1]
                sent = [tie(array, before, cost(LEAD_X)) for array in sent]
            crossed = [exchange(array, "head", n_head, 2 * d) for d, array in enumerate(sent, 1)]
        sums.append((total, crossed))
    def added(units_in, offsets, parts_of):
        with jax.named_scope("sum_over_x"):
            places = [parts_of(offset) for offset in offsets]
            found = x_sum([sums[unit] for unit in units_in], pieces[0], places)
        with jax.named_scope("columns_over_ctx"):
            return [
                exchange(block, "ctx", n_ctx, offset) if offset else block
                for offset, block in zip(offsets, found)
            ]

    blocks = {0: added([0], [0], lambda offset: [(0, 0), (0, 1)])}
    crossing = [offset for offset in range(1, n_ctx) if offset >= n_ctx // 2]
    ahead = added([1], crossing, lambda offset: [(0, offset - 1)])
    ahead = [tie(block, [], cost(LEAD_AHEAD)) for block in ahead]
    blocks.update({offset: [block] for offset, block in zip(crossing, ahead)})

    def rest(unit, offsets):
        def parts_of(offset):
            last_rows = (1, offsets.index(offset))
            return [last_rows] if offset in crossing else [(0, offset - 1), last_rows]

        for offset, block in zip(offsets, added([1, unit], offsets, parts_of)):
            blocks[offset] = [*blocks.get(offset, []), block]

    rest(2, powers)
    rest(3, handed)
    with jax.named_scope("output"):
        return place_columns([blocks[d] for d in range(n_ctx)])


def solution(mesh):
    placed = (
        P(("groups", "ctx"), "head"),
        P(("groups", "ctx"), None),
        P(None, "head"),
        P("head", "ctx"),
        P("groups"),
        P("groups"),
    )
    return jax.shard_map(
        functools.partial(shards, mesh.shape["ctx"], mesh.shape["head"]),
        mesh=mesh,
        in_specs=placed,
        out_specs=P(("groups", "ctx", "head"), None),
        check_vma=False,
    )
```
